512 devices in a mesh: shot: 64 (over y_lo, z, core), rec: 8 (over y_hi, x).
Axes of the slice: x: 4, y: 8 (y_hi: 2, y_lo: 4; y = y_hi * 4 + y_lo), z: 8, core: 2. Of those that a mesh axis runs over, the one named last changes fastest.
Arguments:
- noisy: bfloat16 [1, 256, 32, 8, 512], P(None, 'shot', 'rec'), may hold values from -12 to 12
- misfit: bfloat16 [1, 256, 32, 8, 512], P(None, 'shot', 'rec'), may hold values from -48 to 48
- timestep: int32 [1], replicated, may hold values from 0 to 999
- segment_ids: int32 [256], replicated, may hold values from 0 to 41, never falling along the last dimension, each value on 1 to 12 neighbouring positions
- w_qkv: bfloat16 [2, 512, 1536], replicated, may hold values from -32 to 32
- w_out: bfloat16 [2, 512, 512], replicated, may hold values from -0.25 to 0.25
Outputs:
- denoised: bfloat16 [1, 256, 32, 8, 512], P(None, 'shot', 'rec')
- guidance: bfloat16 [1, 256, 32, 8, 512], P(None, 'shot', 'rec')
The draws below stay inside these ranges and needn't reach their ends.
Inputs may be any that keep to these rules, and one draw needn't show every extreme that they name: `segment_ids`: the shot group of each shot token; never falls from one shot token to the next; each group covers 1 to 12 shot tokens.
All inputs are finite; a program needn't handle non-finite values.
Results may differ from the reference program's by a relative error of at most 0.03.
The reference program's roundings to bfloat16 on the way count: a program that leaves them out, or rounds other values in their place, can miss the bound.
Values may be sent and summed in bfloat16 or wider, within the bound.
A program may use at most 128 MiB of HBM per device.

```python
import math
import jax
import jax.numpy as jnp
import numpy as np
from jax import lax

BATCH = 1
HEADS = 16
HS = 32
D = 512
WIN = 8
TT = 8
STEPS = 1000
ST = 256
RT = 32


def draw_noisy(key, part):
    key = jax.random.fold_in(key, 11)
    base_key = jax.random.fold_in(key, 0)
    shape = (BATCH, ST, RT, TT, D)
    values = jax.random.normal(base_key, shape, jnp.float32)
    return jnp.clip(values, -12.0, 12.0).astype(jnp.bfloat16)


def draw_misfit(key, part):
    key = jax.random.fold_in(key, 23)
    base_key, shot_key = jax.random.split(key, 2)
    shape = (BATCH, ST, RT, TT, D)
    shot_frac = jnp.arange(ST, dtype=jnp.float32) / (ST - 1)
    jitter = jnp.exp(jax.random.uniform(shot_key, (ST,), jnp.float32, -0.35, 0.35))
    shot_ramp = jnp.exp(shot_frac * math.log(3.0)) * jitter
    values = jax.random.normal(base_key, shape, jnp.float32) * shot_ramp[None, :, None, None, None]
    return jnp.clip(values, -48.0, 48.0).astype(jnp.bfloat16)


def draw_w_qkv(key, part):
    key = jax.random.fold_in(key, 37)
    base_key = jax.random.fold_in(key, 0)
    samples = jax.random.normal(base_key, (2, D, 3 * D), jnp.float32) * D ** (-0.5)
    return jnp.clip(samples, -32.0, 32.0).astype(jnp.bfloat16)


def profile(amount, total, most, slope):
    loads = [(1 << 20) // math.isqrt(rank ** slope) + 1 for rank in range(2, amount + 1)]
    spare, counts = total - most - (amount - 1), [1] * (amount - 1)
    while spare > 0:
        movable = [i for i in range(amount - 1) if counts[i] < most]
        whole, left = sum([loads[i] for i in movable]), spare
        for i in movable:
            extra = min(most - counts[i], max(1, left * loads[i] // whole), spare)
            counts[i] = counts[i] + extra
            spare = spare - extra
    return np.array([most] + counts)


def ragged(rng, amount, total, most, skew):
    if amount == 2:
        one = jax.random.randint(rng, (), max(1, total - most), min(most, total - 1) + 1)
        return jnp.stack([one, total - one])
    sizes = jnp.asarray(profile(amount, total, most, skew), jnp.int32)
    twos = (amount - 1) // 2
    donor, taker = sizes[1:1 + 2 * twos:2], sizes[2:2 + 2 * twos:2]
    room = jnp.minimum(donor - 1, most - taker)
    moved = jax.random.randint(jax.random.fold_in(rng, 1), (twos,), 0, 1 << 20) % (room + 1)
    sizes = sizes.at[1:1 + 2 * twos:2].set(donor - moved).at[2:2 + 2 * twos:2].set(taker + moved)
    return sizes[jax.random.permutation(jax.random.fold_in(rng, 2), amount)]


def bell_draw(stream_key, dims, width, limit, held_as=jnp.bfloat16):
    entries = width * jax.random.normal(stream_key, dims, jnp.float32)
    return jnp.clip(entries, min=-limit, max=limit).astype(held_as)


def setup_inputs(seed: int = 0) -> dict:
    streams_of = jax.random.split(jax.random.key(seed), 7)
    return {
        "noisy": draw_noisy(jax.random.fold_in(streams_of[6], 71), 0),
        "misfit": draw_misfit(jax.random.fold_in(streams_of[6], 71), 0),
        "timestep": jax.random.randint(streams_of[2], (1,), 0, STEPS).astype(jnp.int32),
        "segment_ids": jnp.searchsorted(jnp.cumsum(ragged(streams_of[3], ST // 6, ST, 12, 0)), jnp.arange(ST), side="right").astype(jnp.int32),
        "w_qkv": draw_w_qkv(jax.random.fold_in(streams_of[6], 71), 0),
        "w_out": bell_draw(streams_of[5], (2, D, D), D ** -0.5, 0.25),
    }


sigma_low = 0.5
sigma_high = 8.0
sigma_data = 0.5
norm_eps = 1e-06

def precondition(timestep):
    fraction = timestep[0].astype(jnp.float32) / (STEPS - 1)
    noise_level = sigma_low * jnp.exp(fraction * math.log(sigma_high / sigma_low))
    spread = noise_level * noise_level + sigma_data * sigma_data
    c_skip = sigma_data * sigma_data / spread
    c_out = noise_level * sigma_data * lax.rsqrt(spread)
    c_in = lax.rsqrt(spread)
    return (c_skip, c_out, c_in)

def rounded(values):
    return lax.optimization_barrier(values.astype(jnp.bfloat16)).astype(jnp.float32)

def split_heads(field):
    return field.astype(jnp.float32).reshape(-1, HEADS, HS)

def to_windows(field):
    last_dim = field.shape[-1]
    tiles = field.reshape(BATCH, ST // WIN, WIN, RT // WIN, WIN, TT, last_dim)
    tiles = tiles.transpose(0, 1, 3, 2, 4, 5, 6)
    return tiles.reshape(-1, WIN * WIN * TT, last_dim)

def from_windows(tiles):
    last_dim = tiles.shape[-1]
    field = tiles.reshape(BATCH, ST // WIN, RT // WIN, WIN, WIN, TT, last_dim)
    return field.transpose(0, 1, 3, 2, 4, 5, 6).reshape(BATCH, ST, RT, TT, last_dim)

def window_scores(tile, line):
    query_heads = split_heads(tile[:, :D])
    key_heads = split_heads(tile[:, D:2 * D])
    value_heads = split_heads(tile[:, 2 * D:])
    allowed = (line[:, None] == line[None, :])[:, None, :]
    scores = jnp.einsum('qhd,khd->qhk', query_heads, key_heads, precision=lax.Precision.HIGHEST) * HS ** (-0.5)
    return (query_heads, key_heads, value_heads, allowed, scores)

def window_ahead(packed):
    tile, line = packed
    query_heads, key_heads, value_heads, allowed, scores = window_scores(tile, line)
    row_max = lax.optimization_barrier(jnp.max(jnp.where(allowed, scores, -jnp.inf), axis=-1))
    shifted_exp = jnp.where(allowed, jnp.exp(scores - row_max[..., None]), 0.0)
    log_total = row_max + jnp.log(lax.optimization_barrier(jnp.sum(shifted_exp, axis=-1)))
    attention = jnp.where(allowed, jnp.exp(scores - log_total[..., None]), 0.0)
    attended = jnp.einsum('qhk,khd->qhd', rounded(attention), value_heads, precision=lax.Precision.HIGHEST)
    return (attended.reshape(-1, D).astype(jnp.bfloat16), log_total)

def window_back(packed):
    tile, line, grad_tile, log_total = packed
    query_heads, key_heads, value_heads, allowed, scores = window_scores(tile, line)
    attention = jnp.where(allowed, jnp.exp(scores - log_total[..., None]), 0.0)
    grad_heads = split_heads(grad_tile)
    grad_prob = jnp.einsum('qhd,khd->qhk', grad_heads, value_heads, precision=lax.Precision.HIGHEST)
    row_dot = lax.optimization_barrier(jnp.sum(attention * grad_prob, axis=-1))
    grad_score = rounded(attention * (grad_prob - row_dot[..., None]))
    grad_query = jnp.einsum('qhk,khd->qhd', grad_score, key_heads, precision=lax.Precision.HIGHEST) * HS ** (-0.5)
    grad_key = jnp.einsum('qhk,qhd->khd', grad_score, query_heads, precision=lax.Precision.HIGHEST) * HS ** (-0.5)
    grad_value = jnp.einsum('qhk,qhd->khd', rounded(attention), grad_heads, precision=lax.Precision.HIGHEST)
    parts = [grad_query.reshape(-1, D), grad_key.reshape(-1, D), grad_value.reshape(-1, D)]
    return jnp.concatenate(parts, axis=-1).astype(jnp.bfloat16)

def roll_grid(field, offset):
    return jnp.roll(field, (offset, offset), axis=(1, 2))

def region_ids(segment_ids, shifted):
    shot_part = segment_ids * 4
    if shifted:
        shot_part = shot_part + 2 * (jnp.arange(ST) < WIN // 2).astype(jnp.int32)
        rec_part = (jnp.arange(RT) < WIN // 2).astype(jnp.int32)
    else:
        rec_part = jnp.zeros((RT,), jnp.int32)
    ids = shot_part[:, None] + rec_part[None, :]
    return jnp.broadcast_to(ids[None, :, :, None, None], (BATCH, ST, RT, TT, 1)).astype(jnp.int32)

def block_ahead(stream, w_layer, w_proj, segment_ids, shifted):
    inverse = lax.rsqrt(lax.optimization_barrier(jnp.mean(stream * stream, axis=-1, keepdims=True)) + norm_eps)
    normed = (stream * inverse).astype(jnp.bfloat16)
    packed = jnp.dot(normed.reshape(-1, D), w_layer, preferred_element_type=jnp.float32)
    packed = packed.reshape(BATCH, ST, RT, TT, 3 * D)
    line = region_ids(segment_ids, shifted)
    if shifted:
        packed = roll_grid(packed, -(WIN // 2))
        line = roll_grid(line, -(WIN // 2))
    tiles = to_windows(packed)
    line_tiles = to_windows(line)[..., 0]
    attended, log_total = lax.map(window_ahead, (tiles, line_tiles))
    attended = from_windows(attended)
    if shifted:
        attended = roll_grid(attended, WIN // 2)
    branch = jnp.dot(attended.reshape(-1, D), w_proj, preferred_element_type=jnp.float32).reshape(stream.shape)
    return (stream + branch, (stream, inverse, tiles, line_tiles, log_total))

def block_back(grad_next, saved, w_layer, w_proj, shifted):
    stream, inverse, tiles, line_tiles, log_total = saved
    grad_attended = jnp.dot(grad_next.reshape(-1, D).astype(jnp.bfloat16), w_proj.T, preferred_element_type=jnp.float32)
    grad_attended = grad_attended.astype(jnp.bfloat16).reshape(BATCH, ST, RT, TT, D)
    if shifted:
        grad_attended = roll_grid(grad_attended, -(WIN // 2))
    grad_packed = lax.map(window_back, (tiles, line_tiles, to_windows(grad_attended), log_total))
    grad_packed = from_windows(grad_packed)
    if shifted:
        grad_packed = roll_grid(grad_packed, WIN // 2)
    grad_normed = jnp.dot(grad_packed.reshape(-1, 3 * D), w_layer.T, preferred_element_type=jnp.float32)
    grad_normed = grad_normed.reshape(stream.shape)
    normed_f = stream * inverse
    centred = grad_normed - normed_f * lax.optimization_barrier(jnp.mean(grad_normed * normed_f, axis=-1, keepdims=True))
    return grad_next + inverse * centred

def reference(noisy, misfit, timestep, segment_ids, w_qkv, w_out):
    c_skip, c_out, c_in = precondition(timestep)
    noisy_f = noisy.astype(jnp.float32)
    start = c_in * noisy_f
    middle, first_saved = block_ahead(start, w_qkv[0], w_out[0], segment_ids, False)
    final, second_saved = block_ahead(middle, w_qkv[1], w_out[1], segment_ids, True)
    denoised = (c_skip * noisy_f + c_out * final).astype(jnp.bfloat16)
    misfit_f = misfit.astype(jnp.float32)
    misfit_scale = lax.rsqrt(jnp.sum(misfit_f * misfit_f) / misfit.size + norm_eps)
    weight = misfit_f * misfit_scale
    grad_middle = block_back(c_out * weight, second_saved, w_qkv[1], w_out[1], True)
    grad_start = block_back(grad_middle, first_saved, w_qkv[0], w_out[0], False)
    guidance = (c_skip * weight + c_in * grad_start).astype(jnp.bfloat16)
    return (denoised, guidance)
```

```python
import functools
import math

import jax
import jax.numpy as jnp
from jax import lax
from jax.experimental import pallas as pl
from jax.experimental.pallas import tpu as pltpu
from jax.sharding import PartitionSpec as P

HEADS = 16
HS = 32
STEPS = 1000
D = 512
TOK = 128
HALF = 4
OWN = 4
CHUNKS = 4

sigma_low = 0.5
sigma_high = 8.0
sigma_data = 0.5
norm_eps = 1e-06
SCALE = HS ** (-0.5)
LOG2E = math.log2(math.e)
MASKED = -1e30

f32 = jnp.float32
bf16 = jnp.bfloat16
MESH = pl.DeviceIdType.MESH


def reduction_stages(n_shot, n_rec):
    digits = []
    for axis, size in ((0, n_shot), (1, n_rec)):
        stride = 2
        while stride < size:
            digits.append((axis, stride, 2))
            stride *= 2
    return [digits[i : i + 2] for i in range(0, len(digits), 2)]


def stage_peers(stage, shot, rec):
    place = [shot, rec]
    now, size = 0, 1
    for axis, stride, radix in stage:
        now = now + size * ((place[axis] // stride) % radix)
        size *= radix
    peers = []
    for k in range(1, size):
        later = (now + k) % size
        at = list(place)
        for axis, stride, radix in stage:
            digit = (place[axis] // stride) % radix
            at[axis] = at[axis] + stride * (later % radix - digit)
            later = later // radix
        peers.append((at[0], at[1]))
    return peers


def window_places(shot, rec, n_shot, n_rec):
    places = []
    near, far = shot % 2, rec % 2
    step_n, step_f = 1 - 2 * near, 1 - 2 * far
    places.append(
        (
            near,
            far,
            [(shot + step_n, rec), (shot, rec + step_f), (shot + step_n, rec + step_f)],
            [(shot - near + i % 2, 0) for i in range(4)],
        )
    )
    end = 1 - (rec % (n_rec - 1) + n_rec - 2) // (n_rec - 1)
    near = (shot + 1) % 2
    far = (1 - end) * ((rec + 1) % 2) + end * (((shot + 3) % 4) // 2)
    step_n, step_f = 1 - 2 * near, 1 - 2 * far
    move_s, move_r = 2 * end * step_f, (1 - end) * step_f
    near_shot = (shot + step_n + n_shot) % n_shot
    far_shot = (shot + move_s + n_shot) % n_shot
    diag_shot = (shot + step_n + move_s + n_shot) % n_shot
    first = shot - near - 2 * end * far + n_shot
    parts = []
    for i in range(4):
        at = (first + i % 2 + 2 * end * (i // 2)) % n_shot
        wrapped = 1 - (at + n_shot - 1) // n_shot
        parts.append((at, 2 * wrapped + end * (i // 2)))
    places.append(
        (near, far, [(near_shot, rec), (far_shot, rec + move_r), (diag_shot, rec + move_r)], parts)
    )
    return places


def split3(x):
    high = x.astype(bf16)
    rest = x - high.astype(f32)
    mid = rest.astype(bf16)
    low = (rest - mid.astype(f32)).astype(bf16)
    return high, mid, low


def dot(a, b):
    return lax.dot_general(a, b, (((1,), (0,)), ((), ())), preferred_element_type=f32)


def dot_nt(a, b):
    return lax.dot_general(a, b, (((1,), (1,)), ((), ())), preferred_element_type=f32)


def fold3(x):
    return x[:HS] + x[HS : 2 * HS] + x[2 * HS :]


def kernel(
    n_shot,
    n_rec,
    stages,
    noisy,
    misfit,
    timestep,
    segs,
    w_qkv,
    w_out,
    den,
    gui,
    noisy_v,
    misfit_v,
    noisy_t,
    misfit_t,
    stream1,
    inverse,
    wfull,
    wofull,
    wcol,
    wt,
    wot,
    nbuf,
    q3,
    k3,
    v3,
    k8t,
    v4t,
    bias,
    prob,
    pbuf,
    dbuf,
    ost,
    obuf,
    gst,
    gbuf,
    gpst,
    gpbuf,
    part,
    out_v,
    in_sem,
    w_sem,
    out_sem,
    near_s,
    near_r,
    far_s,
    far_r,
    rel_s,
    rel_r,
    o_s,
    o_r,
    g_s,
    g_r,
    gp_s,
    gp_r,
    red_s,
    red_r,
):
    shot, rec = lax.axis_index("shot"), lax.axis_index("rec")
    places = window_places(shot, rec, n_shot, n_rec)
    own, blocks, peers = [], [], []
    for near, far, partners, _ in places:
        here = 2 * far + near
        own.append(here)
        blocks.append([2 * far + 1 - near, 2 - 2 * far + near, 3 - 2 * far - near])
        peers.append(partners)
    red_peers = [peers[0]] + [stage_peers(stage, shot, rec) for stage in stages]

    noisy_in = pltpu.make_async_copy(noisy, noisy_v, in_sem.at[0])
    misfit_in = pltpu.make_async_copy(misfit, misfit_v, in_sem.at[1])
    noisy_in.start()
    misfit_in.start()
    col_in = [
        [
            pltpu.make_async_copy(
                w_qkv.at[b, :, pl.ds(pl.multiple_of(third * D + own[b] * TOK, TOK), TOK)],
                wcol.at[b, third],
                w_sem.at[3 * b + third],
            )
            for third in range(3)
        ]
        for b in range(2)
    ]
    out_in = [pltpu.make_async_copy(w_out.at[b], wofull.at[b], w_sem.at[6 + b]) for b in range(2)]
    full_in = [pltpu.make_async_copy(w_qkv.at[b], wfull.at[b], w_sem.at[8 + b]) for b in range(2)]
    for copy in col_in[0] + [out_in[0], out_in[1]] + col_in[1] + [full_in[1], full_in[0]]:
        copy.start()

    barrier = pltpu.get_barrier_semaphore()
    greeted = peers[0] + peers[1] + [peer for some in red_peers[1:] for peer in some]
    for peer in greeted:
        pl.semaphore_signal(barrier, inc=1, device_id=peer, device_id_type=MESH)

    def remote(src, dst, send, recv, peer):
        return pltpu.make_async_remote_copy(
            src_ref=src, dst_ref=dst, send_sem=send, recv_sem=recv, device_id=peer, device_id_type=MESH
        )

    rows = D // CHUNKS

    def near_copy(b):
        block = nbuf.at[b, own[b]]
        return remote(block, block, near_s.at[b], near_r.at[b], peers[b][0])

    def far_copy(b, k):
        block = nbuf.at[b, own[b], pl.ds(k * rows, rows)]
        return remote(block, block, far_s.at[b, k], far_r.at[b, k], peers[b][1])

    def relay_copy(b, k):
        block = nbuf.at[b, blocks[b][1], pl.ds(k * rows, rows)]
        return remote(block, block, rel_s.at[b, k], rel_r.at[b, k], peers[b][0])

    def o_copy(b, m):
        return remote(
            ost.at[b, blocks[b][m]], obuf.at[b, own[b]], o_s.at[b, m], o_r.at[b, m], peers[b][m]
        )

    def g_copy(b, m):
        return remote(
            gst.at[b, blocks[b][m]], gbuf.at[b, own[b]], g_s.at[b, m], g_r.at[b, m], peers[b][m]
        )

    def gp_copy(b, m, h):
        return remote(
            gpst.at[b, h, blocks[b][m]],
            gpbuf.at[b, own[b], h],
            gp_s.at[b, m, h],
            gp_r.at[b, m, h],
            peers[b][m],
        )

    def red_copy(stage, k):
        return remote(
            part.at[stage, 0],
            part.at[stage, k + 1],
            red_s.at[stage, k],
            red_r.at[stage, k],
            red_peers[stage][k],
        )

    def red_send(stage, value):
        part[stage, 0] = value
        for k in range(len(red_peers[stage])):
            red_copy(stage, k).start()

    def red_take(stage):
        total = part[stage, 0]
        for k in range(len(red_peers[stage])):
            red_copy(stage, k).wait_recv()
            total = total + part[stage, k + 1]
        return total

    fraction = jnp.full((1, TOK), timestep[0].astype(f32), f32) / (STEPS - 1)
    noise_level = sigma_low * jnp.exp(fraction * math.log(sigma_high / sigma_low))
    spread = noise_level * noise_level + sigma_data * sigma_data
    c_skip = sigma_data * sigma_data / spread
    c_out = noise_level * sigma_data * lax.rsqrt(spread)
    c_in = lax.rsqrt(spread)

    def normalise(b, stream):
        inv = lax.rsqrt(jnp.sum(stream * stream, axis=0, keepdims=True) * (1.0 / D) + norm_eps)
        inverse[b] = inv
        nbuf[b, own[b]] = (stream * inv).astype(bf16)

    noisy_in.wait()
    noisy_t[...] = noisy_v[...].astype(f32).T
    normalise(0, c_in * noisy_t[...])
    pl.semaphore_wait(barrier, len(greeted))

    def gather_start(b):
        for k in range(CHUNKS):
            far_copy(b, k).start()
        near_copy(b).start()

    def prepare_weights(b):
        for third in range(3):
            col_in[b][third].wait()
            wt[b, third * TOK : (third + 1) * TOK, :] = wcol[b, third].T

    def project(b, block):
        packed = dot(wt[b], nbuf[b, block])
        q = split3(packed[:TOK] * (SCALE * LOG2E))
        k = split3(packed[TOK : 2 * TOK])
        v = split3(packed[2 * TOK :])
        zero = jnp.zeros((HS, TOK), bf16)
        for h in range(OWN):
            at = slice(h * HS, (h + 1) * HS)
            kh, km, kl = [x[at] for x in k]
            vh, vm, vl = [x[at] for x in v]
            q3[b, h, block] = jnp.concatenate([x[at] for x in q], axis=0)
            k3[b, h, block] = jnp.concatenate([kh, km, kl], axis=0)
            v3[b, h, block] = jnp.concatenate([vh, vm, vl], axis=0)
            k8t[b, h, block] = jnp.concatenate([kh, kh, kh, km, km, kl, km, kl], axis=0).T
            v4t[b, h, block] = jnp.concatenate([vh, vm, vl, zero], axis=0).T

    def make_bias(b):
        parts = places[b][3]
        ids = []
        for at, mark in parts:
            ids.append([segs[HALF * at + s] * 4 + mark for s in range(HALF)])
        lane = lax.broadcasted_iota(jnp.int32, (HS, TOK), 1)
        for j in range(4):
            line = jnp.where(
                lane < 64,
                jnp.where(lane < 32, ids[j][0], ids[j][1]),
                jnp.where(lane < 96, ids[j][2], ids[j][3]),
            )
            for i in range(4):
                for s in range(HALF):
                    at = i * TOK + s * HS
                    bias[b, j, at : at + HS, :] = jnp.where(line == ids[i][s], 0.0, MASKED)

    def gather_rest(b):
        project(b, own[b])
        make_bias(b)
        near_copy(b).wait_recv()
        project(b, blocks[b][0])
        for k in range(CHUNKS):
            far_copy(b, k).wait_recv()
            relay_copy(b, k).start()
        project(b, blocks[b][1])

    def gather_last(b):
        for k in range(CHUNKS):
            relay_copy(b, k).wait_recv()
        project(b, blocks[b][2])

    def attention(b, h, j):
        q = q3[b, h, j]
        qh, qm, ql = q[:HS], q[HS : 2 * HS], q[2 * HS :]
        q8 = jnp.concatenate([qh, qm, ql, qh, qm, qh, ql, qm], axis=0)
        scores = dot(k8t[b, h].reshape(4 * TOK, 8 * HS), q8) + bias[b, j]
        shifted = jnp.exp2(scores - jnp.max(scores, axis=0, keepdims=True))
        return shifted * (1.0 / jnp.sum(shifted, axis=0, keepdims=True))

    def wide(ref, b, h):
        return jnp.concatenate([ref[b, h, i] for i in range(4)], axis=1)

    def wide_pairs(ref):
        return jnp.concatenate([ref[i] for i in range(4)], axis=1)

    def score_grad(b, h, j, p):
        g = gbuf[b, j, pl.ds(pl.multiple_of(h * HS, HS), HS), :]
        g4 = jnp.concatenate([g, g, g, g], axis=0)
        grad_prob = dot(v4t[b, h].reshape(4 * TOK, 4 * HS), g4)
        row_dot = jnp.sum(p * grad_prob, axis=0, keepdims=True)
        return (p * (grad_prob - row_dot)).astype(bf16)

    def head_back(b, h):
        pw, dw = wide_pairs(pbuf), wide_pairs(dbuf)
        g = jnp.concatenate(
            [gbuf[b, i, pl.ds(pl.multiple_of(h * HS, HS), HS), :] for i in range(4)], axis=1
        )
        grad_q = (fold3(dot(wide(k3, b, h), dw)) * SCALE).astype(bf16)
        grad_k = (fold3(dot_nt(wide(q3, b, h), dw)) * (1.0 / LOG2E)).astype(bf16)
        grad_v = dot_nt(g, pw).astype(bf16)
        for j in range(4):
            at = slice(j * TOK, (j + 1) * TOK)
            gpst[b, h, j] = jnp.concatenate([grad_q[:, at], grad_k[:, at], grad_v[:, at]], axis=0)
        for m in (2, 1, 0):
            gp_copy(b, m, h).start()
        gpbuf[b, own[b], h] = gpst[b, h, own[b]]

    def packed_back(b, stream, grad_next):
        def arrive(h, carry):
            for m in range(3):
                gp_copy(b, m, h).wait_recv()
            return carry

        lax.fori_loop(0, OWN, arrive, 0)
        pieces = []
        for third in range(3):
            for i in range(4):
                for h in range(OWN):
                    pieces.append(gpbuf[b, i, h, third * HS : (third + 1) * HS, :])
        grad_normed = dot(wfull[b], jnp.concatenate(pieces, axis=0))
        inv = inverse[b]
        normed = stream * inv
        mean = jnp.sum(grad_normed * normed, axis=0, keepdims=True) * (1.0 / D)
        return grad_next + inv * (grad_normed - normed * mean)

    def send_grads(b, grad_next):
        grads = dot(wofull[b], grad_next.astype(bf16)).astype(bf16)
        gst[b] = grads.reshape(4, TOK, TOK)
        for m in (2, 1, 0):
            g_copy(b, m).start()
        gbuf[b, own[b]] = gst[b, own[b]]

    def branch(b):
        return dot(wot[b], obuf[b].reshape(D, TOK))

    gather_start(0)
    misfit_in.wait()
    misfit_f = misfit_v[...].astype(f32)
    squares = jnp.sum(misfit_f * misfit_f, axis=0, keepdims=True)
    squares = squares[:, :128] + squares[:, 128:256] + squares[:, 256:384] + squares[:, 384:]
    red_send(0, jnp.broadcast_to(squares, (8, 128)))
    prepare_weights(0)
    gather_rest(0)
    misfit_t[...] = misfit_f.T
    stage = 0
    red_send(1, red_take(0))
    stage = 1
    gather_last(0)
    for m in (2, 1, 0, None):
        block = own[0] if m is None else blocks[0][m]
        for h in range(OWN):
            p = attention(0, h, block)
            prob[h, block] = p
            o = fold3(dot(wide(v3, 0, h), p.astype(bf16)))
            ost[0, block, h * HS : (h + 1) * HS, :] = o.astype(bf16)
        if m is None:
            obuf[0, own[0]] = ost[0, own[0]]
        else:
            o_copy(0, m).start()
        if stage < len(stages):
            red_send(stage + 1, red_take(stage))
            stage += 1
    while stage < len(stages):
        red_send(stage + 1, red_take(stage))
        stage += 1
    prepare_weights(1)
    for b in range(2):
        out_in[b].wait()
    wot[0] = wofull[0].T
    square_sum = jnp.sum(red_take(stage)[:1], axis=1, keepdims=True)
    entries = float(n_shot * n_rec * TOK * D)
    misfit_scale = lax.rsqrt(square_sum / entries + norm_eps)
    send_grads(1, c_out * (misfit_t[...] * misfit_scale))
    for m in range(3):
        o_copy(0, m).wait_recv()
    stream1[...] = c_in * noisy_t[...] + branch(0)
    normalise(1, stream1[...])

    gather_start(1)
    gather_rest(1)
    wot[1] = wofull[1].T
    for m in range(3):
        g_copy(1, m).wait_recv()
    gather_last(1)

    def second(h, carry):
        for j in range(4):
            p = attention(1, h, j)
            pbuf[j] = p.astype(bf16)
            dbuf[j] = score_grad(1, h, j, p)
        head_back(1, h)
        o = fold3(dot(wide(v3, 1, h), wide_pairs(pbuf))).astype(bf16)
        for j in range(4):
            ost[1, j, pl.ds(pl.multiple_of(h * HS, HS), HS), :] = o[:, j * TOK : (j + 1) * TOK]
        return carry

    lax.fori_loop(0, OWN, second, 0)
    for m in (2, 1, 0):
        o_copy(1, m).start()
    obuf[1, own[1]] = ost[1, own[1]]
    for b in (1, 0):
        full_in[b].wait()
    weight = misfit_t[...] * misfit_scale
    grad1 = packed_back(1, stream1[...], c_out * weight)
    send_grads(0, grad1)
    for m in range(3):
        o_copy(1, m).wait_recv()
    final = stream1[...] + branch(1)
    out_v[0] = (c_skip * noisy_t[...] + c_out * final).T.astype(bf16)
    den_out = pltpu.make_async_copy(out_v.at[0], den, out_sem.at[0])
    den_out.start()
    stream1[...] = grad1
    for m in range(3):
        g_copy(0, m).wait_recv()

    def first(h, carry):
        for j in range(4):
            p = prob[h, j]
            pbuf[j] = p.astype(bf16)
            dbuf[j] = score_grad(0, h, j, p)
        head_back(0, h)
        return carry

    lax.fori_loop(0, OWN, first, 0)
    grad0 = packed_back(0, c_in * noisy_t[...], stream1[...])
    weight = misfit_t[...] * misfit_scale
    out_v[1] = (c_skip * weight + c_in * grad0).T.astype(bf16)
    gui_out = pltpu.make_async_copy(out_v.at[1], gui, out_sem.at[1])
    gui_out.start()

    for b in range(2):
        near_copy(b).wait_send()
        for k in range(CHUNKS):
            far_copy(b, k).wait_send()
            relay_copy(b, k).wait_send()
        for m in range(3):
            o_copy(b, m).wait_send()
            g_copy(b, m).wait_send()

        def leave(h, carry, b=b):
            for m in range(3):
                gp_copy(b, m, h).wait_send()
            return carry

        lax.fori_loop(0, OWN, leave, 0)
    for stage in range(len(red_peers)):
        for k in range(len(red_peers[stage])):
            red_copy(stage, k).wait_send()
    den_out.wait()
    gui_out.wait()


def local(n_shot, n_rec, noisy, misfit, timestep, segment_ids, w_qkv, w_out):
    stages = reduction_stages(n_shot, n_rec)
    shape = noisy.shape
    any_space = pl.BlockSpec(memory_space=pl.ANY)
    scalars = pl.BlockSpec(memory_space=pltpu.SMEM)
    dma = pltpu.SemaphoreType.DMA
    scratch = [
        pltpu.VMEM((TOK, D), bf16),
        pltpu.VMEM((TOK, D), bf16),
        pltpu.VMEM((D, TOK), f32),
        pltpu.VMEM((D, TOK), f32),
        pltpu.VMEM((D, TOK), f32),
        pltpu.VMEM((2, 1, TOK), f32),
        pltpu.VMEM((2, D, 3 * D), bf16),
        pltpu.VMEM((2, D, D), bf16),
        pltpu.VMEM((2, 3, D, TOK), bf16),
        pltpu.VMEM((2, 3 * TOK, D), bf16),
        pltpu.VMEM((2, D, D), bf16),
        pltpu.VMEM((2, 4, D, TOK), bf16),
        pltpu.VMEM((2, OWN, 4, 3 * HS, TOK), bf16),
        pltpu.VMEM((2, OWN, 4, 3 * HS, TOK), bf16),
        pltpu.VMEM((2, OWN, 4, 3 * HS, TOK), bf16),
        pltpu.VMEM((2, OWN, 4, TOK, 8 * HS), bf16),
        pltpu.VMEM((2, OWN, 4, TOK, 4 * HS), bf16),
        pltpu.VMEM((2, 4, 4 * TOK, TOK), f32),
        pltpu.VMEM((OWN, 4, 4 * TOK, TOK), f32),
        pltpu.VMEM((4, 4 * TOK, TOK), bf16),
        pltpu.VMEM((4, 4 * TOK, TOK), bf16),
        pltpu.VMEM((2, 4, TOK, TOK), bf16),
        pltpu.VMEM((2, 4, TOK, TOK), bf16),
        pltpu.VMEM((2, 4, TOK, TOK), bf16),
        pltpu.VMEM((2, 4, TOK, TOK), bf16),
        pltpu.VMEM((2, OWN, 4, 3 * HS, TOK), bf16),
        pltpu.VMEM((2, 4, OWN, 3 * HS, TOK), bf16),
        pltpu.VMEM((len(stages) + 1, 4, 8, 128), f32),
        pltpu.VMEM((2, TOK, D), bf16),
        dma((2,)),
        dma((10,)),
        dma((2,)),
        dma((2,)),
        dma((2,)),
        dma((2, CHUNKS)),
        dma((2, CHUNKS)),
        dma((2, CHUNKS)),
        dma((2, CHUNKS)),
        dma((2, 3)),
        dma((2, 3)),
        dma((2, 3)),
        dma((2, 3)),
        dma((2, 3, OWN)),
        dma((2, 3, OWN)),
        dma((len(stages) + 1, 3)),
        dma((len(stages) + 1, 3)),
    ]
    den, gui = pl.pallas_call(
        functools.partial(kernel, n_shot, n_rec, stages),
        out_shape=[jax.ShapeDtypeStruct((TOK, D), bf16)] * 2,
        in_specs=[any_space, any_space, scalars, scalars, any_space, any_space],
        out_specs=[any_space, any_space],
        scratch_shapes=scratch,
        compiler_params=pltpu.CompilerParams(
            collective_id=0, has_side_effects=True, vmem_limit_bytes=62 * 1024 * 1024
        ),
        cost_estimate=pl.CostEstimate(
            flops=2_000_000_000, bytes_accessed=6_000_000, transcendentals=2_000_000
        ),
        name="window_pair",
    )(noisy.reshape(TOK, D), misfit.reshape(TOK, D), timestep, segment_ids, w_qkv, w_out)
    return den.reshape(shape), gui.reshape(shape)


def solution(mesh):
    tokens = P(None, "shot", "rec", None, None)
    return jax.shard_map(
        functools.partial(local, mesh.shape["shot"], mesh.shape["rec"]),
        mesh=mesh,
        in_specs=(tokens, tokens, P(), P(), P(), P()),
        out_specs=(tokens, tokens),
        check_vma=False,
    )
```

```python
import functools
import math

import jax
import jax.numpy as jnp
from jax import lax
from jax.experimental import pallas as pl
from jax.experimental.pallas import tpu as pltpu
from jax.sharding import PartitionSpec as P

HEADS = 16
HS = 32
STEPS = 1000
D = 512
TOK = 128
HALF = 4
OWN = 4
GROUPS = 64
CHUNKS = 4

sigma_low = 0.5
sigma_high = 8.0
sigma_data = 0.5
norm_eps = 1e-06
SCALE = HS ** (-0.5)
LOG2E = math.log2(math.e)
MASKED = -1e30
VMEM_LIMIT = 62 * 1024 * 1024

f32 = jnp.float32
bf16 = jnp.bfloat16
MESH = pl.DeviceIdType.MESH


def reduction_stages(n_shot, n_rec):
    digits = []
    for axis, size in ((0, n_shot), (1, n_rec)):
        stride = 2
        while stride < size:
            digits.append((axis, stride, 2))
            stride *= 2
    return [digits[i : i + 2] for i in range(0, len(digits), 2)]


def stage_peers(stage, shot, rec):
    place = [shot, rec]
    now, size = 0, 1
    for axis, stride, radix in stage:
        now = now + size * ((place[axis] // stride) % radix)
        size *= radix
    peers = []
    for k in range(1, size):
        later = (now + k) % size
        at = list(place)
        for axis, stride, radix in stage:
            digit = (place[axis] // stride) % radix
            at[axis] = at[axis] + stride * (later % radix - digit)
            later = later // radix
        peers.append((at[0], at[1]))
    return peers


def window_places(shot, rec, n_shot, n_rec):
    places = []
    near, far = shot % 2, rec % 2
    step_n, step_f = 1 - 2 * near, 1 - 2 * far
    places.append(
        (
            near,
            far,
            [(shot + step_n, rec), (shot, rec + step_f), (shot + step_n, rec + step_f)],
            [(shot - near + i % 2, 0) for i in range(4)],
        )
    )
    end = 1 - (rec % (n_rec - 1) + n_rec - 2) // (n_rec - 1)
    near = (shot + 1) % 2
    far = (1 - end) * ((rec + 1) % 2) + end * (((shot + 3) % 4) // 2)
    step_n, step_f = 1 - 2 * near, 1 - 2 * far
    move_s, move_r = 2 * end * step_f, (1 - end) * step_f
    near_shot = (shot + step_n + n_shot) % n_shot
    far_shot = (shot + move_s + n_shot) % n_shot
    diag_shot = (shot + step_n + move_s + n_shot) % n_shot
    first = shot - near - 2 * end * far + n_shot
    parts = []
    for i in range(4):
        at = (first + i % 2 + 2 * end * (i // 2)) % n_shot
        wrapped = 1 - (at + n_shot - 1) // n_shot
        parts.append((at, 2 * wrapped + end * (i // 2)))
    places.append(
        (near, far, [(near_shot, rec), (far_shot, rec + move_r), (diag_shot, rec + move_r)], parts)
    )
    return places


def split3(x):
    high = x.astype(bf16)
    rest = x - high.astype(f32)
    mid = rest.astype(bf16)
    low = (rest - mid.astype(f32)).astype(bf16)
    return high, mid, low


def dot(a, b):
    return lax.dot_general(a, b, (((1,), (0,)), ((), ())), preferred_element_type=f32)


def dot_nt(a, b):
    return lax.dot_general(a, b, (((1,), (1,)), ((), ())), preferred_element_type=f32)


def fold3(x):
    return x[:HS] + x[HS : 2 * HS] + x[2 * HS :]


def kernel(
    n_shot,
    n_rec,
    stages,
    noisy,
    misfit,
    timestep,
    segs,
    w_qkv,
    w_out,
    den,
    gui,
    noisy_v,
    noisy_t,
    misfit_t,
    stream1,
    inverse,
    wfull,
    wofull,
    wcol,
    wt,
    wot,
    nbuf,
    mbuf,
    q3,
    k3,
    v3,
    k8t,
    v4t,
    mrow,
    prob,
    pbuf,
    dbuf,
    sbuf,
    tbuf,
    ost,
    obuf,
    gst,
    gbuf,
    gpst,
    gpbuf,
    part,
    out_v,
    in_sem,
    w_sem,
    out_sem,
    near_s,
    near_r,
    far_s,
    far_r,
    rel_s,
    rel_r,
    mis_s,
    mis_r,
    o_s,
    o_r,
    g_s,
    g_r,
    gp_s,
    gp_r,
    red_s,
    red_r,
):
    shot, rec = lax.axis_index("shot"), lax.axis_index("rec")
    places = window_places(shot, rec, n_shot, n_rec)
    own, blocks, peers = [], [], []
    for near, far, partners, _ in places:
        here = 2 * far + near
        own.append(here)
        blocks.append([2 * far + 1 - near, 2 - 2 * far + near, 3 - 2 * far - near])
        peers.append(partners)
    def block_at(b, i):
        near, far = places[b][:2]
        return 2 * (far + (i // 2) * (1 - 2 * far)) + near + (i % 2) * (1 - 2 * near)

    red_peers = [peers[0]] + [stage_peers(stage, shot, rec) for stage in stages]

    barrier = pltpu.get_barrier_semaphore()
    greeted = peers[0] + peers[1] + [peer for some in red_peers[1:] for peer in some]
    for peer in greeted:
        pl.semaphore_signal(barrier, inc=1, device_id=peer, device_id_type=MESH)

    noisy_in = pltpu.make_async_copy(noisy, noisy_v, in_sem.at[0])
    misfit_in = pltpu.make_async_copy(misfit, mbuf.at[own[1]], in_sem.at[1])
    noisy_in.start()
    misfit_in.start()
    col_in = [
        [
            pltpu.make_async_copy(
                w_qkv.at[b, :, pl.ds(pl.multiple_of(third * D + own[b] * TOK, TOK), TOK)],
                wcol.at[b, third],
                w_sem.at[3 * b + third],
            )
            for third in range(3)
        ]
        for b in range(2)
    ]
    out_in = [pltpu.make_async_copy(w_out.at[b], wofull.at[b], w_sem.at[6 + b]) for b in range(2)]
    full_in = [pltpu.make_async_copy(w_qkv.at[b], wfull.at[b], w_sem.at[8 + b]) for b in range(2)]
    for copy in col_in[0]:
        copy.start()

    def remote(src, dst, send, recv, peer):
        return pltpu.make_async_remote_copy(
            src_ref=src, dst_ref=dst, send_sem=send, recv_sem=recv, device_id=peer, device_id_type=MESH
        )

    rows = D // CHUNKS

    def near_copy(b):
        block = nbuf.at[b, own[b]]
        return remote(block, block, near_s.at[b], near_r.at[b], peers[b][0])

    def far_copy(b, k):
        block = nbuf.at[b, own[b], pl.ds(k * rows, rows)]
        return remote(block, block, far_s.at[b, k], far_r.at[b, k], peers[b][1])

    def relay_copy(b, k):
        block = nbuf.at[b, blocks[b][1], pl.ds(k * rows, rows)]
        return remote(block, block, rel_s.at[b, k], rel_r.at[b, k], peers[b][0])

    def misfit_copy(m):
        block = mbuf.at[blocks[1][1] if m == 2 else own[1]]
        return remote(block, block, mis_s.at[m], mis_r.at[m], peers[1][m % 2])

    def o_copy(b, m):
        return remote(
            ost.at[b, blocks[b][m]], obuf.at[b, own[b]], o_s.at[b, m], o_r.at[b, m], peers[b][m]
        )

    def g_copy(m):
        return remote(
            gst.at[blocks[0][m]], gbuf.at[0, own[0]], g_s.at[m], g_r.at[m], peers[0][m]
        )

    def gp_copy(b, m, h):
        return remote(
            gpst.at[b, h, blocks[b][m]],
            gpbuf.at[b, own[b], h],
            gp_s.at[b, m, h],
            gp_r.at[b, m, h],
            peers[b][m],
        )

    def red_copy(stage, k):
        return remote(
            part.at[stage, 0],
            part.at[stage, k + 1],
            red_s.at[stage, k],
            red_r.at[stage, k],
            red_peers[stage][k],
        )

    def red_send(stage, value):
        part[stage, 0] = value
        for k in range(len(red_peers[stage])):
            red_copy(stage, k).start()

    def red_take(stage):
        total = part[stage, 0]
        for k in range(len(red_peers[stage])):
            red_copy(stage, k).wait_recv()
            total = total + part[stage, k + 1]
        return total

    fraction = jnp.full((1, TOK), timestep[0].astype(f32), f32) / (STEPS - 1)
    noise_level = sigma_low * jnp.exp(fraction * math.log(sigma_high / sigma_low))
    spread = noise_level * noise_level + sigma_data * sigma_data
    c_skip = sigma_data * sigma_data / spread
    c_out = noise_level * sigma_data * lax.rsqrt(spread)
    c_in = lax.rsqrt(spread)

    def normalise(b, stream):
        inv = lax.rsqrt(jnp.sum(stream * stream, axis=0, keepdims=True) * (1.0 / D) + norm_eps)
        inverse[b] = inv
        nbuf[b, own[b]] = (stream * inv).astype(bf16)

    noisy_in.wait()
    noisy_t[...] = noisy_v[...].astype(f32).T
    normalise(0, c_in * noisy_t[...])
    pl.semaphore_wait(barrier, len(greeted))

    def gather_start(b):
        for k in range(CHUNKS):
            far_copy(b, k).start()
        near_copy(b).start()

    def prepare_weights(b):
        for third in range(3):
            col_in[b][third].wait()
            wt[b, third * TOK : (third + 1) * TOK, :] = wcol[b, third].T

    def project(b, block):
        packed = dot(wt[b], nbuf[b, block])
        q = split3(packed[:TOK] * (SCALE * LOG2E))
        k = split3(packed[TOK : 2 * TOK])
        v = split3(packed[2 * TOK :])
        zero = jnp.zeros((HS, TOK), bf16)
        lane = lax.broadcasted_iota(jnp.int32, (GROUPS, TOK), 1)
        row = lax.broadcasted_iota(jnp.int32, (GROUPS, TOK), 0)
        member = jnp.where(row == HALF * block + lane // HS, 1.0, 0.0).astype(bf16)
        for h in range(OWN):
            at = slice(h * HS, (h + 1) * HS)
            kh, km, kl = [x[at] for x in k]
            vh, vm, vl = [x[at] for x in v]
            q3[b, h, block] = jnp.concatenate([x[at] for x in q], axis=0)
            k3[b, h, block] = jnp.concatenate([kh, km, kl], axis=0)
            v3[b, h, block] = jnp.concatenate([vh, vm, vl], axis=0)
            k8t[b, h, block] = jnp.concatenate([kh, kh, kh, km, km, kl, member], axis=0).T
            v4t[b, h, block] = jnp.concatenate([vh, vm, vl, zero], axis=0).T

    def make_mask(b):
        ids = [[segs[HALF * at + s] * 4 + mark for s in range(HALF)] for at, mark in places[b][3]]
        lane = lax.broadcasted_iota(jnp.int32, (GROUPS, TOK), 1)
        row = lax.broadcasted_iota(jnp.int32, (GROUPS, TOK), 0)
        group_id = jnp.full((GROUPS, TOK), -1, jnp.int32)
        for g in range(4 * HALF):
            group_id = jnp.where(row == g, ids[g // HALF][g % HALF], group_id)
        for j in range(4):
            line = jnp.where(
                lane < 64,
                jnp.where(lane < 32, ids[j][0], ids[j][1]),
                jnp.where(lane < 96, ids[j][2], ids[j][3]),
            )
            apart = (line != group_id) & (row < 4 * HALF)
            mrow[b, j] = jnp.where(apart, MASKED, 0.0).astype(bf16)

    def relay(b):
        for k in range(CHUNKS):
            far_copy(b, k).wait_recv()
            relay_copy(b, k).start()

    def relayed(b):
        for k in range(CHUNKS):
            relay_copy(b, k).wait_recv()

    def scores_of(b, h, side):
        parts = []
        for i in range(2):
            q = q3[b, h, 2 * side + i]
            qh, qm, ql = q[:HS], q[HS : 2 * HS], q[2 * HS :]
            parts.append(
                jnp.concatenate([qh, qm, ql, qh, qm, qh, mrow[b, 2 * side + i]], axis=0)
            )
        return dot(k8t[b, h].reshape(4 * TOK, 8 * HS), jnp.concatenate(parts, axis=1))

    def softmax(scores):
        shifted = jnp.exp2(scores - jnp.max(scores, axis=0, keepdims=True))
        return shifted * (1.0 / jnp.sum(shifted, axis=0, keepdims=True))

    def wide(ref, b, h):
        return jnp.concatenate([ref[b, h, i] for i in range(4)], axis=1)

    def head_rows(h):
        return pl.ds(pl.multiple_of(h * HS, HS), HS)

    def prob_grad(b, h, side):
        parts = []
        for i in range(2):
            g = gbuf[b, 2 * side + i, head_rows(h), :]
            parts.append(jnp.concatenate([g, g, g, g], axis=0))
        return dot(v4t[b, h].reshape(4 * TOK, 4 * HS), jnp.concatenate(parts, axis=1))

    def score_grad(p, grad_prob):
        row_dot = jnp.sum(p * grad_prob, axis=0, keepdims=True)
        return (p * (grad_prob - row_dot)).astype(bf16)

    def head_back(b, h):
        pw = jnp.concatenate([pbuf[b, h, 0], pbuf[b, h, 1]], axis=1)
        dw = jnp.concatenate([dbuf[h, 0], dbuf[h, 1]], axis=1)
        g = jnp.concatenate([gbuf[b, i, head_rows(h), :] for i in range(4)], axis=1)
        grad_q = (fold3(dot(wide(k3, b, h), dw)) * SCALE).astype(bf16)
        grad_k = (fold3(dot_nt(wide(q3, b, h), dw)) * (1.0 / LOG2E)).astype(bf16)
        grad_v = dot_nt(g, pw).astype(bf16)
        for j in range(4):
            at = slice(j * TOK, (j + 1) * TOK)
            gpst[b, h, j] = jnp.concatenate([grad_q[:, at], grad_k[:, at], grad_v[:, at]], axis=0)
        for m in (2, 1, 0):
            gp_copy(b, m, h).start()
        gpbuf[b, own[b], h] = gpst[b, h, own[b]]
        if b == 1:
            o = fold3(dot(wide(v3, b, h), pw)).astype(bf16)
            for j in range(4):
                ost[b, j, head_rows(h), :] = o[:, j * TOK : (j + 1) * TOK]

    def packed_back(b, stream, grad_next):
        def arrive(h, carry):
            for m in range(3):
                gp_copy(b, m, h).wait_recv()
            return carry

        lax.fori_loop(0, OWN, arrive, 0)
        pieces = []
        for third in range(3):
            for i in range(4):
                for h in range(OWN):
                    pieces.append(gpbuf[b, i, h, third * HS : (third + 1) * HS, :])
        grad_normed = dot(wfull[b], jnp.concatenate(pieces, axis=0))
        inv = inverse[b]
        normed = stream * inv
        mean = jnp.sum(grad_normed * normed, axis=0, keepdims=True) * (1.0 / D)
        return grad_next + inv * (grad_normed - normed * mean)

    def send_grads(grad_next):
        grads = dot(wofull[0], grad_next.astype(bf16)).astype(bf16)
        gst[...] = grads.reshape(4, TOK, TOK)
        for m in (2, 1, 0):
            g_copy(m).start()
        gbuf[0, own[0]] = gst[own[0]]

    def second_grads(block):
        weight = mbuf[block].astype(f32) * jnp.broadcast_to(misfit_scale, (1, D))
        grad_next = (jnp.concatenate([c_out] * 4, axis=1) * weight).astype(bf16)
        rows = wofull[1, pl.ds(pl.multiple_of(own[1] * TOK, TOK), TOK), :]
        gbuf[1, block] = dot_nt(rows, grad_next).astype(bf16)

    def branch(b):
        return dot(wot[b], obuf[b].reshape(D, TOK))

    def forward(stage):
        if stage < len(stages):
            red_send(stage + 1, red_take(stage))

    gather_start(0)
    misfit_in.wait()
    misfit_copy(1).start()
    misfit_copy(0).start()
    misfit_f = mbuf[own[1]].astype(f32)
    squares = jnp.sum(misfit_f * misfit_f, axis=0, keepdims=True)
    squares = squares[:, :128] + squares[:, 128:256] + squares[:, 256:384] + squares[:, 384:]
    red_send(0, jnp.broadcast_to(squares, (8, 128)))
    out_in[0].start()
    prepare_weights(0)

    def project_first(i, carry):
        @pl.when(i == 1)
        def _():
            make_mask(0)
            misfit_t[...] = mbuf[own[1]].astype(f32).T
            relay(0)
            near_copy(0).wait_recv()
            out_in[1].start()
            for copy in col_in[1]:
                copy.start()

        @pl.when(i == 2)
        def _():
            forward(0)

        @pl.when(i == 3)
        def _():
            out_in[0].wait()
            wot[0] = wofull[0].T
            relayed(0)

        project(0, block_at(0, i))
        return carry

    lax.fori_loop(0, 4, project_first, 0)
    own_side = own[0] // 2

    def first_place(i):
        return i % OWN, own_side + (1 - i // OWN) * (1 - 2 * own_side)

    sbuf[0] = scores_of(0, *first_place(0))

    def first_ahead(i, carry):
        h, side = first_place(i)
        sbuf[(i + 1) % 2] = scores_of(0, *first_place((i + 1) % (2 * OWN)))
        p = softmax(sbuf[i % 2])
        prob[h, side] = p
        p = p.astype(bf16)
        pbuf[0, h, side] = p
        o = fold3(dot(wide(v3, 0, h), p)).astype(bf16)
        for j in range(2):
            ost[0, 2 * side + j, head_rows(h), :] = o[:, j * TOK : (j + 1) * TOK]

        @pl.when(i == 1)
        def _():
            forward(1)

        @pl.when(i == 3)
        def _():
            o_copy(0, 2).start()
            o_copy(0, 1).start()
            misfit_copy(1).wait_recv()
            misfit_copy(2).start()

        @pl.when(i == 5)
        def _():
            forward(2)

        return carry

    lax.fori_loop(0, 2 * OWN, first_ahead, 0)
    o_copy(0, 0).start()
    obuf[0, own[0]] = ost[0, own[0]]
    prepare_weights(1)
    forward(3)
    for m in range(3):
        o_copy(0, m).wait_recv()
    stream1[...] = c_in * noisy_t[...] + branch(0)
    normalise(1, stream1[...])

    gather_start(1)
    make_mask(1)
    full_in[1].start()
    square_sum = jnp.sum(red_take(len(stages))[:1], axis=1, keepdims=True)
    entries = float(n_shot * n_rec * TOK * D)
    misfit_scale = lax.rsqrt(square_sum / entries + norm_eps)
    out_in[1].wait()
    misfit_copy(0).wait_recv()
    misfit_copy(2).wait_recv()

    def project_second(i, carry):
        @pl.when(i == 1)
        def _():
            near_copy(1).wait_recv()

        @pl.when(i == 2)
        def _():
            relay(1)

        @pl.when(i == 3)
        def _():
            wot[1] = wofull[1].T
            full_in[0].start()
            relayed(1)

        second_grads(block_at(1, i))
        project(1, block_at(1, i))
        return carry

    lax.fori_loop(0, 4, project_second, 0)
    sbuf[0] = scores_of(1, 0, 0)
    tbuf[0] = prob_grad(1, 0, 0)

    def second(i, carry):
        h, side = i // 2, i % 2
        later = (i + 1) % (2 * OWN)
        sbuf[(i + 1) % 2] = scores_of(1, later // 2, later % 2)
        tbuf[(i + 1) % 2] = prob_grad(1, later // 2, later % 2)
        p = softmax(sbuf[i % 2])
        pbuf[1, h, side] = p.astype(bf16)
        dbuf[h, side] = score_grad(p, tbuf[i % 2])

        @pl.when(side == 1)
        def _():
            head_back(1, h)

        return carry

    lax.fori_loop(0, 2 * OWN, second, 0)
    for m in (2, 1, 0):
        o_copy(1, m).start()
    obuf[1, own[1]] = ost[1, own[1]]
    for b in (1, 0):
        full_in[b].wait()
    weight = misfit_t[...] * misfit_scale
    grad1 = packed_back(1, stream1[...], c_out * weight)
    send_grads(grad1)
    for m in range(3):
        o_copy(1, m).wait_recv()
    final = stream1[...] + branch(1)
    out_v[0] = (c_skip * noisy_t[...] + c_out * final).T.astype(bf16)
    den_out = pltpu.make_async_copy(out_v.at[0], den, out_sem.at[0])
    den_out.start()
    stream1[...] = grad1

    def first(h, carry, side):
        dbuf[h, side] = score_grad(prob[h, side], prob_grad(0, h, side))
        return carry

    def first_last(h, carry):
        first(h, carry, 1 - own_side)
        head_back(0, h)
        return carry

    g_copy(0).wait_recv()
    lax.fori_loop(0, OWN, functools.partial(first, side=own_side), 0)
    g_copy(1).wait_recv()
    g_copy(2).wait_recv()
    lax.fori_loop(0, OWN, first_last, 0)
    grad0 = packed_back(0, c_in * noisy_t[...], stream1[...])
    weight = misfit_t[...] * misfit_scale
    out_v[1] = (c_skip * weight + c_in * grad0).T.astype(bf16)
    gui_out = pltpu.make_async_copy(out_v.at[1], gui, out_sem.at[1])
    gui_out.start()

    for b in range(2):
        near_copy(b).wait_send()
        for k in range(CHUNKS):
            far_copy(b, k).wait_send()
            relay_copy(b, k).wait_send()
        for m in range(3):
            o_copy(b, m).wait_send()

        def leave(h, carry, b=b):
            for m in range(3):
                gp_copy(b, m, h).wait_send()
            return carry

        lax.fori_loop(0, OWN, leave, 0)
    for m in range(3):
        g_copy(m).wait_send()
        misfit_copy(m).wait_send()
    for stage in range(len(red_peers)):
        for k in range(len(red_peers[stage])):
            red_copy(stage, k).wait_send()
    den_out.wait()
    gui_out.wait()


def copy_pair(den, gui, den_out, gui_out, den_v, gui_v, sem):
    into = [
        pltpu.make_async_copy(den, den_v, sem.at[0]),
        pltpu.make_async_copy(gui, gui_v, sem.at[1]),
    ]
    away = [
        pltpu.make_async_copy(den_v, den_out, sem.at[2]),
        pltpu.make_async_copy(gui_v, gui_out, sem.at[3]),
    ]
    for copy in into:
        copy.start()
    for i in range(2):
        into[i].wait()
        away[i].start()
    for copy in away:
        copy.wait()


def local(n_shot, n_rec, noisy, misfit, timestep, segment_ids, w_qkv, w_out):
    stages = reduction_stages(n_shot, n_rec)
    shape = noisy.shape
    any_space = pl.BlockSpec(memory_space=pl.ANY)
    scalars = pl.BlockSpec(memory_space=pltpu.SMEM)
    dma = pltpu.SemaphoreType.DMA
    scratch = [
        pltpu.VMEM((TOK, D), bf16),
        pltpu.VMEM((D, TOK), f32),
        pltpu.VMEM((D, TOK), f32),
        pltpu.VMEM((D, TOK), f32),
        pltpu.VMEM((2, 1, TOK), f32),
        pltpu.VMEM((2, D, 3 * D), bf16),
        pltpu.VMEM((2, D, D), bf16),
        pltpu.VMEM((2, 3, D, TOK), bf16),
        pltpu.VMEM((2, 3 * TOK, D), bf16),
        pltpu.VMEM((2, D, D), bf16),
        pltpu.VMEM((2, 4, D, TOK), bf16),
        pltpu.VMEM((4, TOK, D), bf16),
        pltpu.VMEM((2, OWN, 4, 3 * HS, TOK), bf16),
        pltpu.VMEM((2, OWN, 4, 3 * HS, TOK), bf16),
        pltpu.VMEM((2, OWN, 4, 3 * HS, TOK), bf16),
        pltpu.VMEM((2, OWN, 4, TOK, 8 * HS), bf16),
        pltpu.VMEM((2, OWN, 4, TOK, 4 * HS), bf16),
        pltpu.VMEM((2, 4, GROUPS, TOK), bf16),
        pltpu.VMEM((OWN, 2, 4 * TOK, 2 * TOK), f32),
        pltpu.VMEM((2, OWN, 2, 4 * TOK, 2 * TOK), bf16),
        pltpu.VMEM((OWN, 2, 4 * TOK, 2 * TOK), bf16),
        pltpu.VMEM((2, 4 * TOK, 2 * TOK), f32),
        pltpu.VMEM((2, 4 * TOK, 2 * TOK), f32),
        pltpu.VMEM((2, 4, TOK, TOK), bf16),
        pltpu.VMEM((2, 4, TOK, TOK), bf16),
        pltpu.VMEM((4, TOK, TOK), bf16),
        pltpu.VMEM((2, 4, TOK, TOK), bf16),
        pltpu.VMEM((2, OWN, 4, 3 * HS, TOK), bf16),
        pltpu.VMEM((2, 4, OWN, 3 * HS, TOK), bf16),
        pltpu.VMEM((len(stages) + 1, 4, 8, 128), f32),
        pltpu.VMEM((2, TOK, D), bf16),
        dma((2,)),
        dma((10,)),
        dma((2,)),
        dma((2,)),
        dma((2,)),
        dma((2, CHUNKS)),
        dma((2, CHUNKS)),
        dma((2, CHUNKS)),
        dma((2, CHUNKS)),
        dma((3,)),
        dma((3,)),
        dma((2, 3)),
        dma((2, 3)),
        dma((3,)),
        dma((3,)),
        dma((2, 3, OWN)),
        dma((2, 3, OWN)),
        dma((len(stages) + 1, 3)),
        dma((len(stages) + 1, 3)),
    ]
    den, gui = pl.pallas_call(
        functools.partial(kernel, n_shot, n_rec, stages),
        out_shape=[jax.ShapeDtypeStruct((TOK, D), bf16)] * 2,
        in_specs=[any_space, any_space, scalars, scalars, any_space, any_space],
        out_specs=[any_space, any_space],
        scratch_shapes=scratch,
        compiler_params=pltpu.CompilerParams(
            collective_id=0, has_side_effects=True, vmem_limit_bytes=VMEM_LIMIT
        ),
        cost_estimate=pl.CostEstimate(
            flops=2_000_000_000, bytes_accessed=6_000_000, transcendentals=2_000_000
        ),
        name="window_pair",
    )(noisy.reshape(TOK, D), misfit.reshape(TOK, D), timestep, segment_ids, w_qkv, w_out)
    den, gui = pl.pallas_call(
        copy_pair,
        out_shape=[jax.ShapeDtypeStruct((TOK, D), bf16)] * 2,
        in_specs=[any_space, any_space],
        out_specs=[any_space, any_space],
        scratch_shapes=[pltpu.VMEM((TOK, D), bf16), pltpu.VMEM((TOK, D), bf16), dma((4,))],
        compiler_params=pltpu.CompilerParams(vmem_limit_bytes=VMEM_LIMIT),
        name="copy_pair",
    )(den, gui)
    return den.reshape(shape), gui.reshape(shape)


def solution(mesh):
    tokens = P(None, "shot", "rec", None, None)
    return jax.shard_map(
        functools.partial(local, mesh.shape["shot"], mesh.shape["rec"]),
        mesh=mesh,
        in_specs=(tokens, tokens, P(), P(), P(), P()),
        out_specs=(tokens, tokens),
        check_vma=False,
    )
```

```python
import functools
import math

import jax
import jax.numpy as jnp
from jax import lax
from jax.experimental import pallas as pl
from jax.experimental.pallas import tpu as pltpu
from jax.sharding import PartitionSpec as P

HEADS = 16
HS = 32
STEPS = 1000
D = 512
TOK = 128
HALF = 4
OWN = 4
GROUPS = 64
CHUNKS = 4

sigma_low = 0.5
sigma_high = 8.0
sigma_data = 0.5
norm_eps = 1e-06
SCALE = HS ** (-0.5)
LOG2E = math.log2(math.e)
MASKED = -1e30
VMEM_LIMIT = 62 * 1024 * 1024

f32 = jnp.float32
bf16 = jnp.bfloat16
MESH = pl.DeviceIdType.MESH


def reduction_stages(n_shot, n_rec):
    digits = []
    for axis, size in ((0, n_shot), (1, n_rec)):
        stride = 2
        while stride < size:
            digits.append((axis, stride, 2))
            stride *= 2
    return [digits[i : i + 2] for i in range(0, len(digits), 2)]


def stage_peers(stage, shot, rec):
    place = [shot, rec]
    now, size = 0, 1
    for axis, stride, radix in stage:
        now = now + size * ((place[axis] // stride) % radix)
        size *= radix
    peers = []
    for k in range(1, size):
        later = (now + k) % size
        at = list(place)
        for axis, stride, radix in stage:
            digit = (place[axis] // stride) % radix
            at[axis] = at[axis] + stride * (later % radix - digit)
            later = later // radix
        peers.append((at[0], at[1]))
    return peers


def window_places(shot, rec, n_shot, n_rec):
    places = []
    near, far = shot % 2, rec % 2
    step_n, step_f = 1 - 2 * near, 1 - 2 * far
    places.append(
        (
            near,
            far,
            [(shot + step_n, rec), (shot, rec + step_f), (shot + step_n, rec + step_f)],
            [(shot - near + i % 2, 0) for i in range(4)],
        )
    )
    end = 1 - (rec % (n_rec - 1) + n_rec - 2) // (n_rec - 1)
    near = (shot + 1) % 2
    far = (1 - end) * ((rec + 1) % 2) + end * (((shot + 3) % 4) // 2)
    step_n, step_f = 1 - 2 * near, 1 - 2 * far
    move_s, move_r = 2 * end * step_f, (1 - end) * step_f
    near_shot = (shot + step_n + n_shot) % n_shot
    far_shot = (shot + move_s + n_shot) % n_shot
    diag_shot = (shot + step_n + move_s + n_shot) % n_shot
    first = shot - near - 2 * end * far + n_shot
    parts = []
    for i in range(4):
        at = (first + i % 2 + 2 * end * (i // 2)) % n_shot
        wrapped = 1 - (at + n_shot - 1) // n_shot
        parts.append((at, 2 * wrapped + end * (i // 2)))
    places.append(
        (near, far, [(near_shot, rec), (far_shot, rec + move_r), (diag_shot, rec + move_r)], parts)
    )
    return places


def split3(x):
    high = x.astype(bf16)
    rest = x - high.astype(f32)
    mid = rest.astype(bf16)
    low = (rest - mid.astype(f32)).astype(bf16)
    return high, mid, low


def dot(a, b):
    return lax.dot_general(a, b, (((1,), (0,)), ((), ())), preferred_element_type=f32)


def dot_nt(a, b):
    return lax.dot_general(a, b, (((1,), (1,)), ((), ())), preferred_element_type=f32)


def fold3(x):
    return x[:HS] + x[HS : 2 * HS] + x[2 * HS :]


def kernel(
    n_shot,
    n_rec,
    stages,
    noisy,
    misfit,
    timestep,
    segs,
    w_qkv,
    w_out,
    den,
    gui,
    noisy_v,
    noisy_t,
    misfit_t,
    stream1,
    grad_mid,
    inverse,
    wfull,
    wofull,
    wcol,
    wt,
    wot,
    nbuf,
    mbuf,
    q3,
    k3,
    v3,
    k8t,
    v4t,
    mrow,
    prob,
    pbuf,
    dbuf,
    ost,
    obuf,
    gst,
    gbuf,
    gpst,
    gpbuf,
    part,
    out_v,
    in_sem,
    w_sem,
    out_sem,
    near_s,
    near_r,
    far_s,
    far_r,
    rel_s,
    rel_r,
    mis_s,
    mis_r,
    o_s,
    o_r,
    g_s,
    g_r,
    gp_s,
    gp_r,
    red_s,
    red_r,
):
    shot, rec = lax.axis_index("shot"), lax.axis_index("rec")
    places = window_places(shot, rec, n_shot, n_rec)
    own, blocks, peers = [], [], []
    for near, far, partners, _ in places:
        here = 2 * far + near
        own.append(here)
        blocks.append([2 * far + 1 - near, 2 - 2 * far + near, 3 - 2 * far - near])
        peers.append(partners)
    red_peers = [peers[0]] + [stage_peers(stage, shot, rec) for stage in stages]

    barrier = pltpu.get_barrier_semaphore()
    greeted = peers[0] + peers[1] + [peer for some in red_peers[1:] for peer in some]
    for peer in greeted:
        pl.semaphore_signal(barrier, inc=1, device_id=peer, device_id_type=MESH)

    noisy_in = pltpu.make_async_copy(noisy, noisy_v, in_sem.at[0])
    misfit_in = pltpu.make_async_copy(misfit, mbuf.at[own[1]], in_sem.at[1])
    noisy_in.start()
    misfit_in.start()
    col_in = [
        [
            pltpu.make_async_copy(
                w_qkv.at[b, :, pl.ds(pl.multiple_of(third * D + own[b] * TOK, TOK), TOK)],
                wcol.at[b, third],
                w_sem.at[3 * b + third],
            )
            for third in range(3)
        ]
        for b in range(2)
    ]
    out_in = [pltpu.make_async_copy(w_out.at[b], wofull.at[b], w_sem.at[6 + b]) for b in range(2)]
    full_in = [pltpu.make_async_copy(w_qkv.at[b], wfull.at[b], w_sem.at[8 + b]) for b in range(2)]
    for copy in col_in[0]:
        copy.start()

    def remote(src, dst, send, recv, peer):
        return pltpu.make_async_remote_copy(
            src_ref=src, dst_ref=dst, send_sem=send, recv_sem=recv, device_id=peer, device_id_type=MESH
        )

    rows = D // CHUNKS

    def near_copy(b):
        block = nbuf.at[b, own[b]]
        return remote(block, block, near_s.at[b], near_r.at[b], peers[b][0])

    def far_copy(b, k):
        block = nbuf.at[b, own[b], pl.ds(k * rows, rows)]
        return remote(block, block, far_s.at[b], far_r.at[b, k], peers[b][1])

    def far_sent(b):
        block = nbuf.at[b, own[b]]
        remote(block, block, far_s.at[b], far_r.at[b, 0], peers[b][1]).wait_send()

    def relay_copy(b, k):
        block = nbuf.at[b, blocks[b][1], pl.ds(k * rows, rows)]
        return remote(block, block, rel_s.at[b], rel_r.at[b], peers[b][0])

    def relay_all(b):
        source, arrived = nbuf.at[b, blocks[b][1]], nbuf.at[b, blocks[b][2]]
        return remote(source, arrived, rel_s.at[b], rel_r.at[b], peers[b][0])

    def misfit_copy(m):
        block = mbuf.at[blocks[1][1] if m == 2 else own[1]]
        return remote(block, block, mis_s.at[0], mis_r.at[m], peers[1][m % 2])

    def misfit_sent():
        block = mbuf.at[pl.ds(0, 3)]
        remote(block, block, mis_s.at[0], mis_r.at[0], peers[1][0]).wait_send()

    def o_copy(b, m):
        return remote(
            ost.at[b, blocks[b][m]], obuf.at[b, own[b]], o_s.at[b], o_r.at[b], peers[b][m]
        )

    def o_all(b):
        source, arrived = ost.at[b, pl.ds(0, 3)], obuf.at[b, pl.ds(0, 3)]
        return remote(source, arrived, o_s.at[b], o_r.at[b], peers[b][0])

    def g_copy(m):
        return remote(
            gst.at[blocks[0][m]], gbuf.at[0, own[0]], g_s.at[0], g_r.at[m], peers[0][m]
        )

    def g_sent():
        source, arrived = gst.at[pl.ds(0, 3)], gbuf.at[0, pl.ds(0, 3)]
        remote(source, arrived, g_s.at[0], g_r.at[0], peers[0][0]).wait_send()

    def gp_copy(b, m, h):
        return remote(
            gpst.at[b, h, blocks[b][m]],
            gpbuf.at[b, own[b], h],
            gp_s.at[b, m],
            gp_r.at[b, m],
            peers[b][m],
        )

    def gp_all(b, m):
        source, arrived = gpst.at[b, :, blocks[b][m]], gpbuf.at[b, blocks[b][m]]
        return remote(source, arrived, gp_s.at[b, m], gp_r.at[b, m], peers[b][m])

    def red_copy(stage, k):
        return remote(
            part.at[stage, 0],
            part.at[stage, k + 1],
            red_s.at[stage],
            red_r.at[stage],
            red_peers[stage][k],
        )

    def red_all(stage):
        peers_of = red_peers[stage]
        block = part.at[stage, pl.ds(1, len(peers_of))]
        return remote(block, block, red_s.at[stage], red_r.at[stage], peers_of[0])

    def red_send(stage, value):
        part[stage, 0] = value
        for k in range(len(red_peers[stage])):
            red_copy(stage, k).start()

    def red_take(stage):
        red_all(stage).wait_recv()
        total = part[stage, 0]
        for k in range(len(red_peers[stage])):
            total = total + part[stage, k + 1]
        return total

    fraction = jnp.full((1, TOK), timestep[0].astype(f32), f32) / (STEPS - 1)
    noise_level = sigma_low * jnp.exp(fraction * math.log(sigma_high / sigma_low))
    spread = noise_level * noise_level + sigma_data * sigma_data
    c_skip = sigma_data * sigma_data / spread
    c_out = noise_level * sigma_data * lax.rsqrt(spread)
    c_in = lax.rsqrt(spread)

    def normalise(b, stream):
        inv = lax.rsqrt(jnp.sum(stream * stream, axis=0, keepdims=True) * (1.0 / D) + norm_eps)
        inverse[b] = inv
        nbuf[b, own[b]] = (stream * inv).astype(bf16)

    noisy_in.wait()
    noisy_t[...] = noisy_v[...].astype(f32).T
    normalise(0, c_in * noisy_t[...])
    pl.semaphore_wait(barrier, len(greeted))

    def gather_start(b):
        for k in range(CHUNKS):
            far_copy(b, k).start()
        near_copy(b).start()

    def prepare_weights(b):
        for third in range(3):
            col_in[b][third].wait()
            wt[b, third * TOK : (third + 1) * TOK, :] = wcol[b, third].T

    def project(b, block):
        packed = dot(wt[b], nbuf[b, block])
        q = split3(packed[:TOK] * (SCALE * LOG2E))
        k = split3(packed[TOK : 2 * TOK])
        v = split3(packed[2 * TOK :])
        zero = jnp.zeros((HS, TOK), bf16)
        lane = lax.broadcasted_iota(jnp.int32, (GROUPS, TOK), 1)
        row = lax.broadcasted_iota(jnp.int32, (GROUPS, TOK), 0)
        member = jnp.where(row == HALF * block + lane // HS, 1.0, 0.0).astype(bf16)
        for h in range(OWN):
            at = slice(h * HS, (h + 1) * HS)
            kh, km, kl = [x[at] for x in k]
            vh, vm, vl = [x[at] for x in v]
            q3[b, h, block] = jnp.concatenate([x[at] for x in q], axis=0)
            k3[b, h, block] = jnp.concatenate([kh, km, kl], axis=0)
            v3[b, h, block] = jnp.concatenate([vh, vm, vl], axis=0)
            k8t[b, h, block] = jnp.concatenate([kh, kh, kh, km, km, kl, member], axis=0).T
            v4t[b, h, block] = jnp.concatenate([vh, vm, vl, zero], axis=0).T

    def make_mask(b):
        ids = [[segs[HALF * at + s] * 4 + mark for s in range(HALF)] for at, mark in places[b][3]]
        lane = lax.broadcasted_iota(jnp.int32, (GROUPS, TOK), 1)
        row = lax.broadcasted_iota(jnp.int32, (GROUPS, TOK), 0)
        group_id = jnp.full((GROUPS, TOK), -1, jnp.int32)
        for g in range(4 * HALF):
            group_id = jnp.where(row == g, ids[g // HALF][g % HALF], group_id)
        for j in range(4):
            line = jnp.where(
                lane < 64,
                jnp.where(lane < 32, ids[j][0], ids[j][1]),
                jnp.where(lane < 96, ids[j][2], ids[j][3]),
            )
            apart = (line != group_id) & (row < 4 * HALF)
            mrow[b, j] = jnp.where(apart, MASKED, 0.0).astype(bf16)

    def relay(b):
        for k in range(CHUNKS):
            far_copy(b, k).wait_recv()
            relay_copy(b, k).start()

    def gather_last(b):
        relay_all(b).wait_recv()
        project(b, blocks[b][2])

    def scores_of(b, h, side):
        parts = []
        for i in range(2):
            q = q3[b, h, 2 * side + i]
            qh, qm, ql = q[:HS], q[HS : 2 * HS], q[2 * HS :]
            parts.append(
                jnp.concatenate([qh, qm, ql, qh, qm, qh, mrow[b, 2 * side + i]], axis=0)
            )
        return dot(k8t[b, h].reshape(4 * TOK, 8 * HS), jnp.concatenate(parts, axis=1))

    def softmax(scores):
        shifted = jnp.exp2(scores - jnp.max(scores, axis=0, keepdims=True))
        return shifted * (1.0 / jnp.sum(shifted, axis=0, keepdims=True))

    def wide(ref, b, h):
        return jnp.concatenate([ref[b, h, i] for i in range(4)], axis=1)

    def head_rows(h):
        return pl.ds(pl.multiple_of(h * HS, HS), HS)

    def prob_grad(b, h, side):
        parts = []
        for i in range(2):
            g = gbuf[b, 2 * side + i, head_rows(h), :]
            parts.append(jnp.concatenate([g, g, g, g], axis=0))
        return dot(v4t[b, h].reshape(4 * TOK, 4 * HS), jnp.concatenate(parts, axis=1))

    def score_grad(p, grad_prob):
        row_dot = jnp.sum(p * grad_prob, axis=0, keepdims=True)
        return (p * (grad_prob - row_dot)).astype(bf16)

    def head_back(b, h):
        pw = jnp.concatenate([pbuf[b, h, 0], pbuf[b, h, 1]], axis=1)
        dw = jnp.concatenate([dbuf[h, 0], dbuf[h, 1]], axis=1)
        g = jnp.concatenate([gbuf[b, i, head_rows(h), :] for i in range(4)], axis=1)
        grad_q = (fold3(dot(wide(k3, b, h), dw)) * SCALE).astype(bf16)
        grad_k = (fold3(dot_nt(wide(q3, b, h), dw)) * (1.0 / LOG2E)).astype(bf16)
        grad_v = dot_nt(g, pw).astype(bf16)
        for j in range(4):
            at = slice(j * TOK, (j + 1) * TOK)
            gpst[b, h, j] = jnp.concatenate([grad_q[:, at], grad_k[:, at], grad_v[:, at]], axis=0)
        for m in (2, 1, 0):
            gp_copy(b, m, h).start()
        gpbuf[b, own[b], h] = gpst[b, h, own[b]]

    def packed_back(b, stream, grad_next):
        own_side = own[b] // 2
        grad_normed = None
        for side, arrivals in ((own_side, (0,)), (1 - own_side, (1, 2))):
            for m in arrivals:
                gp_all(b, m).wait_recv()
            for third in range(3):
                pieces = []
                for i in range(2):
                    for h in range(OWN):
                        pieces.append(gpbuf[b, 2 * side + i, h, third * HS : (third + 1) * HS, :])
                at = pl.multiple_of(third * D + side * 2 * TOK, TOK)
                some = dot(wfull[b, :, pl.ds(at, 2 * TOK)], jnp.concatenate(pieces, axis=0))
                grad_normed = some if grad_normed is None else grad_normed + some
        inv = inverse[b]
        normed = stream * inv
        mean = jnp.sum(grad_normed * normed, axis=0, keepdims=True) * (1.0 / D)
        return grad_next + inv * (grad_normed - normed * mean)

    def send_grads(grad_next):
        grads = dot(wofull[0], grad_next.astype(bf16)).astype(bf16)
        gst[...] = grads.reshape(4, TOK, TOK)
        for m in (2, 1, 0):
            g_copy(m).start()
        gbuf[0, own[0]] = gst[own[0]]

    def second_grads(block):
        weight = mbuf[block].astype(f32) * jnp.broadcast_to(misfit_scale, (1, D))
        grad_next = (jnp.concatenate([c_out] * 4, axis=1) * weight).astype(bf16)
        rows = wofull[1, pl.ds(pl.multiple_of(own[1] * TOK, TOK), TOK), :]
        gbuf[1, block] = dot_nt(rows, grad_next).astype(bf16)

    def branch(b):
        return dot(wot[b], obuf[b].reshape(D, TOK))

    gather_start(0)
    misfit_in.wait()
    misfit_copy(1).start()
    misfit_copy(0).start()
    misfit_f = mbuf[own[1]].astype(f32)
    squares = jnp.sum(misfit_f * misfit_f, axis=0, keepdims=True)
    squares = squares[:, :128] + squares[:, 128:256] + squares[:, 256:384] + squares[:, 384:]
    red_send(0, jnp.broadcast_to(squares, (8, 128)))
    for copy in out_in + col_in[1]:
        copy.start()
    prepare_weights(0)
    project(0, own[0])
    make_mask(0)
    misfit_t[...] = misfit_f.T
    near_copy(0).wait_recv()
    project(0, blocks[0][0])
    relay(0)
    red_send(1, red_take(0))
    project(0, blocks[0][1])
    for b in range(2):
        out_in[b].wait()
    wot[0] = wofull[0].T
    gather_last(0)
    takes = list(range(1, len(stages)))

    def next_stage():
        if takes:
            stage = takes.pop(0)
            red_send(stage + 1, red_take(stage))

    own_side = own[0] // 2
    order = [(side, h) for side in (1 - own_side, own_side) for h in range(OWN)]
    scores = [scores_of(0, order[0][1], order[0][0])]
    for at, (side, h) in enumerate(order):
        if at + 1 < len(order):
            scores.append(scores_of(0, order[at + 1][1], order[at + 1][0]))
        p = softmax(scores.pop(0))
        prob[h, side] = p
        p = p.astype(bf16)
        pbuf[0, h, side] = p
        o = fold3(dot(wide(v3, 0, h), p)).astype(bf16)
        for i in range(2):
            ost[0, 2 * side + i, h * HS : (h + 1) * HS, :] = o[:, i * TOK : (i + 1) * TOK]
        if at == 1 or at == 5:
            next_stage()
        if at == 3:
            o_copy(0, 2).start()
            o_copy(0, 1).start()
            misfit_copy(1).wait_recv()
            misfit_copy(2).start()
    o_copy(0, 0).start()
    obuf[0, own[0]] = ost[0, own[0]]
    prepare_weights(1)
    next_stage()
    o_all(0).wait_recv()
    stream1[...] = c_in * noisy_t[...] + branch(0)
    normalise(1, stream1[...])

    gather_start(1)
    full_in[1].start()
    full_in[0].start()
    project(1, own[1])
    make_mask(1)
    while takes:
        next_stage()
    square_sum = jnp.sum(red_take(len(stages))[:1], axis=1, keepdims=True)
    entries = float(n_shot * n_rec * TOK * D)
    misfit_scale = lax.rsqrt(square_sum / entries + norm_eps)
    near_copy(1).wait_recv()
    project(1, blocks[1][0])
    second_grads(own[1])
    misfit_copy(0).wait_recv()
    second_grads(blocks[1][0])
    second_grads(blocks[1][1])
    misfit_copy(2).wait_recv()
    second_grads(blocks[1][2])
    relay(1)
    project(1, blocks[1][1])
    wot[1] = wofull[1].T
    gather_last(1)

    def second(pair, carry):
        todo = [(2 * pair + u, side) for u in range(2) for side in range(2)]
        ahead = [(scores_of(1, *at), prob_grad(1, *at)) for at in todo[:2]]
        for step, (h, side) in enumerate(todo):
            scores, grad_prob = ahead.pop(0)
            p = softmax(scores)
            pbuf[1, h, side] = p.astype(bf16)
            dbuf[h, side] = score_grad(p, grad_prob)
            if step + 2 < len(todo):
                at = todo[step + 2]
                ahead.append((scores_of(1, *at), prob_grad(1, *at)))
            if side == 1:
                head_back(1, h)
        return carry

    lax.fori_loop(0, OWN // 2, second, 0)

    for h in range(OWN):
        for side in range(2):
            o = fold3(dot(wide(v3, 1, h), pbuf[1, h, side])).astype(bf16)
            for i in range(2):
                ost[1, 2 * side + i, h * HS : (h + 1) * HS, :] = o[:, i * TOK : (i + 1) * TOK]
    for m in (2, 1, 0):
        o_copy(1, m).start()
    obuf[1, own[1]] = ost[1, own[1]]
    for b in (1, 0):
        full_in[b].wait()
    weight = misfit_t[...] * misfit_scale
    grad1 = packed_back(1, stream1[...], c_out * weight)
    send_grads(grad1)
    grad_mid[...] = grad1

    def first(pair, carry, side):
        todo = [2 * pair + u for u in range(2)]
        grad_probs = [prob_grad(0, h, side) for h in todo]
        for h, grad_prob in zip(todo, grad_probs):
            dbuf[h, side] = score_grad(prob[h, side], grad_prob)
        return carry

    def first_last(pair, carry):
        first(pair, carry, 1 - own_side)
        for u in range(2):
            head_back(0, 2 * pair + u)
        return carry

    g_copy(0).wait_recv()
    lax.fori_loop(0, OWN // 2, functools.partial(first, side=own_side), 0)
    g_copy(1).wait_recv()
    g_copy(2).wait_recv()
    lax.fori_loop(0, OWN // 2, first_last, 0)

    o_all(1).wait_recv()
    final = stream1[...] + branch(1)
    out_v[0] = (c_skip * noisy_t[...] + c_out * final).T.astype(bf16)
    den_out = pltpu.make_async_copy(out_v.at[0], den, out_sem.at[0])
    den_out.start()
    for b in range(2):
        near_copy(b).wait_send()
        far_sent(b)
        relay_all(b).wait_send()
        o_all(b).wait_send()
    g_sent()
    misfit_sent()
    for stage in range(len(red_peers)):
        red_all(stage).wait_send()
    for m in range(3):
        gp_all(1, m).wait_send()
    grad0 = packed_back(0, c_in * noisy_t[...], grad_mid[...])
    weight = misfit_t[...] * misfit_scale
    out_v[1] = (c_skip * weight + c_in * grad0).T.astype(bf16)
    gui_out = pltpu.make_async_copy(out_v.at[1], gui, out_sem.at[1])
    gui_out.start()

    for m in range(3):
        gp_all(0, m).wait_send()
    den_out.wait()
    gui_out.wait()


def copy_pair(den, gui, den_out, gui_out, den_v, gui_v, sem):
    into = [
        pltpu.make_async_copy(den, den_v, sem.at[0]),
        pltpu.make_async_copy(gui, gui_v, sem.at[1]),
    ]
    away = [
        pltpu.make_async_copy(den_v, den_out, sem.at[2]),
        pltpu.make_async_copy(gui_v, gui_out, sem.at[3]),
    ]
    for copy in into:
        copy.start()
    for i in range(2):
        into[i].wait()
        away[i].start()
    for copy in away:
        copy.wait()


def local(n_shot, n_rec, noisy, misfit, timestep, segment_ids, w_qkv, w_out):
    stages = reduction_stages(n_shot, n_rec)
    shape = noisy.shape
    any_space = pl.BlockSpec(memory_space=pl.ANY)
    scalars = pl.BlockSpec(memory_space=pltpu.SMEM)
    dma = pltpu.SemaphoreType.DMA
    scratch = [
        pltpu.VMEM((TOK, D), bf16),
        pltpu.VMEM((D, TOK), f32),
        pltpu.VMEM((D, TOK), f32),
        pltpu.VMEM((D, TOK), f32),
        pltpu.VMEM((D, TOK), f32),
        pltpu.VMEM((2, 1, TOK), f32),
        pltpu.VMEM((2, D, 3 * D), bf16),
        pltpu.VMEM((2, D, D), bf16),
        pltpu.VMEM((2, 3, D, TOK), bf16),
        pltpu.VMEM((2, 3 * TOK, D), bf16),
        pltpu.VMEM((2, D, D), bf16),
        pltpu.VMEM((2, 4, D, TOK), bf16),
        pltpu.VMEM((4, TOK, D), bf16),
        pltpu.VMEM((2, OWN, 4, 3 * HS, TOK), bf16),
        pltpu.VMEM((2, OWN, 4, 3 * HS, TOK), bf16),
        pltpu.VMEM((2, OWN, 4, 3 * HS, TOK), bf16),
        pltpu.VMEM((2, OWN, 4, TOK, 8 * HS), bf16),
        pltpu.VMEM((2, OWN, 4, TOK, 4 * HS), bf16),
        pltpu.VMEM((2, 4, GROUPS, TOK), bf16),
        pltpu.VMEM((OWN, 2, 4 * TOK, 2 * TOK), f32),
        pltpu.VMEM((2, OWN, 2, 4 * TOK, 2 * TOK), bf16),
        pltpu.VMEM((OWN, 2, 4 * TOK, 2 * TOK), bf16),
        pltpu.VMEM((2, 4, TOK, TOK), bf16),
        pltpu.VMEM((2, 4, TOK, TOK), bf16),
        pltpu.VMEM((4, TOK, TOK), bf16),
        pltpu.VMEM((2, 4, TOK, TOK), bf16),
        pltpu.VMEM((2, OWN, 4, 3 * HS, TOK), bf16),
        pltpu.VMEM((2, 4, OWN, 3 * HS, TOK), bf16),
        pltpu.VMEM((len(stages) + 1, 4, 8, 128), f32),
        pltpu.VMEM((2, TOK, D), bf16),
        dma((2,)),
        dma((10,)),
        dma((2,)),
        dma((2,)),
        dma((2,)),
        dma((2,)),
        dma((2, CHUNKS)),
        dma((2,)),
        dma((2,)),
        dma((1,)),
        dma((3,)),
        dma((2,)),
        dma((2,)),
        dma((1,)),
        dma((3,)),
        dma((2, 3)),
        dma((2, 3)),
        dma((len(stages) + 1,)),
        dma((len(stages) + 1,)),
    ]
    den, gui = pl.pallas_call(
        functools.partial(kernel, n_shot, n_rec, stages),
        out_shape=[jax.ShapeDtypeStruct((TOK, D), bf16)] * 2,
        in_specs=[any_space, any_space, scalars, scalars, any_space, any_space],
        out_specs=[any_space, any_space],
        scratch_shapes=scratch,
        compiler_params=pltpu.CompilerParams(
            collective_id=0, has_side_effects=True, vmem_limit_bytes=VMEM_LIMIT
        ),
        cost_estimate=pl.CostEstimate(
            flops=2_000_000_000, bytes_accessed=6_000_000, transcendentals=2_000_000
        ),
        name="window_pair",
    )(noisy.reshape(TOK, D), misfit.reshape(TOK, D), timestep, segment_ids, w_qkv, w_out)
    den, gui = pl.pallas_call(
        copy_pair,
        out_shape=[jax.ShapeDtypeStruct((TOK, D), bf16)] * 2,
        in_specs=[any_space, any_space],
        out_specs=[any_space, any_space],
        scratch_shapes=[pltpu.VMEM((TOK, D), bf16), pltpu.VMEM((TOK, D), bf16), dma((4,))],
        compiler_params=pltpu.CompilerParams(vmem_limit_bytes=VMEM_LIMIT),
        name="copy_pair",
    )(den, gui)
    return den.reshape(shape), gui.reshape(shape)


def solution(mesh):
    tokens = P(None, "shot", "rec", None, None)
    return jax.shard_map(
        functools.partial(local, mesh.shape["shot"], mesh.shape["rec"]),
        mesh=mesh,
        in_specs=(tokens, tokens, P(), P(), P(), P()),
        out_specs=(tokens, tokens),
        check_vma=False,
    )
```

```python
import functools
import math

import jax
import jax.numpy as jnp
from jax import lax
from jax.experimental import pallas as pl
from jax.experimental.pallas import tpu as pltpu
from jax.sharding import PartitionSpec as P

HEADS = 16
HS = 32
STEPS = 1000
D = 512
TOK = 128
HALF = 4
OWN = 4
GROUPS = 64
CHUNKS = 4

sigma_low = 0.5
sigma_high = 8.0
sigma_data = 0.5
norm_eps = 1e-06
SCALE = HS ** (-0.5)
LOG2E = math.log2(math.e)
MASKED = -1e30
VMEM_LIMIT = 62 * 1024 * 1024

f32 = jnp.float32
bf16 = jnp.bfloat16
MESH = pl.DeviceIdType.MESH


def reduction_stages(n_shot, n_rec):
    stages = [
        [(1, 1, min(n_rec, 4)), (0, 1, 2)],
        [(0, 16, n_shot // 16), (1, 4, n_rec // 4)],
        [(0, 2, min(n_shot // 2, 8))],
    ]
    stages = [[digit for digit in stage if digit[2] > 1] for stage in stages]
    return [stage for stage in stages if stage]


def stage_peers(stage, shot, rec):
    place = [shot, rec]
    now, size = 0, 1
    for axis, stride, radix in stage:
        now = now + size * ((place[axis] // stride) % radix)
        size *= radix
    peers = []
    for k in range(1, size):
        later = (now + k) % size
        at = list(place)
        for axis, stride, radix in stage:
            digit = (place[axis] // stride) % radix
            at[axis] = at[axis] + stride * (later % radix - digit)
            later = later // radix
        peers.append((at[0], at[1]))
    return peers


def window_places(shot, rec, n_shot, n_rec):
    places = []
    near, far = shot % 2, rec % 2
    step_n, step_f = 1 - 2 * near, 1 - 2 * far
    places.append(
        (
            near,
            far,
            [(shot + step_n, rec), (shot, rec + step_f), (shot + step_n, rec + step_f)],
            [(shot - near + i % 2, 0) for i in range(4)],
        )
    )
    end = 1 - (rec % (n_rec - 1) + n_rec - 2) // (n_rec - 1)
    near = (shot + 1) % 2
    far = (1 - end) * ((rec + 1) % 2) + end * (((shot + 3) % 4) // 2)
    step_n, step_f = 1 - 2 * near, 1 - 2 * far
    move_s, move_r = 2 * end * step_f, (1 - end) * step_f
    near_shot = (shot + step_n + n_shot) % n_shot
    far_shot = (shot + move_s + n_shot) % n_shot
    diag_shot = (shot + step_n + move_s + n_shot) % n_shot
    first = shot - near - 2 * end * far + n_shot
    parts = []
    for i in range(4):
        at = (first + i % 2 + 2 * end * (i // 2)) % n_shot
        wrapped = 1 - (at + n_shot - 1) // n_shot
        parts.append((at, 2 * wrapped + end * (i // 2)))
    places.append(
        (near, far, [(near_shot, rec), (far_shot, rec + move_r), (diag_shot, rec + move_r)], parts)
    )
    return places


def split3(x):
    high = x.astype(bf16)
    rest = x - high.astype(f32)
    mid = rest.astype(bf16)
    low = (rest - mid.astype(f32)).astype(bf16)
    return high, mid, low


def dot(a, b):
    return lax.dot_general(a, b, (((1,), (0,)), ((), ())), preferred_element_type=f32)


def dot_nt(a, b):
    return lax.dot_general(a, b, (((1,), (1,)), ((), ())), preferred_element_type=f32)


def fold3(x):
    return x[:HS] + x[HS : 2 * HS] + x[2 * HS :]


def kernel(
    n_shot,
    n_rec,
    stages,
    noisy,
    misfit,
    timestep,
    segs,
    w_qkv,
    w_out,
    den,
    gui,
    noisy_v,
    noisy_t,
    misfit_t,
    stream1,
    grad_mid,
    inverse,
    wfull,
    wofull,
    wcol,
    wt,
    wot,
    nbuf,
    mbuf,
    q3,
    k3,
    v3,
    k8t,
    v4t,
    mrow,
    prob,
    pbuf,
    dbuf,
    ost,
    obuf,
    gst,
    gbuf,
    gpst,
    gpbuf,
    part,
    out_v,
    in_sem,
    w_sem,
    out_sem,
    near_s,
    near_r,
    far_s,
    far_r,
    rel_s,
    rel_r,
    mis_s,
    mis_r,
    o_s,
    o_r,
    g_s,
    g_r,
    gp_s,
    gp_r,
    red_s,
    red_r,
):
    shot, rec = lax.axis_index("shot"), lax.axis_index("rec")
    places = window_places(shot, rec, n_shot, n_rec)
    own, blocks, peers = [], [], []
    for near, far, partners, _ in places:
        here = 2 * far + near
        own.append(here)
        blocks.append([2 * far + 1 - near, 2 - 2 * far + near, 3 - 2 * far - near])
        peers.append(partners)
    red_peers = [stage_peers(stage, shot, rec) for stage in stages]

    barrier = pltpu.get_barrier_semaphore()
    greeted = peers[0] + peers[1] + [peer for some in red_peers for peer in some]
    for peer in greeted:
        pl.semaphore_signal(barrier, inc=1, device_id=peer, device_id_type=MESH)

    noisy_in = pltpu.make_async_copy(noisy, noisy_v, in_sem.at[0])
    misfit_in = pltpu.make_async_copy(misfit, mbuf.at[own[1]], in_sem.at[1])
    noisy_in.start()
    misfit_in.start()
    col_in = [
        [
            pltpu.make_async_copy(
                w_qkv.at[b, :, pl.ds(pl.multiple_of(third * D + own[b] * TOK, TOK), TOK)],
                wcol.at[b, third],
                w_sem.at[3 * b + third],
            )
            for third in range(3)
        ]
        for b in range(2)
    ]
    out_in = [pltpu.make_async_copy(w_out.at[b], wofull.at[b], w_sem.at[6 + b]) for b in range(2)]
    full_in = [pltpu.make_async_copy(w_qkv.at[b], wfull.at[b], w_sem.at[8 + b]) for b in range(2)]
    for copy in col_in[0]:
        copy.start()

    def remote(src, dst, send, recv, peer):
        return pltpu.make_async_remote_copy(
            src_ref=src, dst_ref=dst, send_sem=send, recv_sem=recv, device_id=peer, device_id_type=MESH
        )

    rows = D // CHUNKS

    def near_copy(b):
        block = nbuf.at[b, own[b]]
        return remote(block, block, near_s.at[b], near_r.at[b], peers[b][0])

    def far_copy(b, k):
        block = nbuf.at[b, own[b], pl.ds(k * rows, rows)]
        return remote(block, block, far_s.at[b], far_r.at[b, k], peers[b][1])

    def far_sent(b):
        block = nbuf.at[b, own[b]]
        remote(block, block, far_s.at[b], far_r.at[b, 0], peers[b][1]).wait_send()

    def relay_copy(b, k):
        block = nbuf.at[b, blocks[b][1], pl.ds(k * rows, rows)]
        return remote(block, block, rel_s.at[b], rel_r.at[b], peers[b][0])

    def relay_all(b):
        source, arrived = nbuf.at[b, blocks[b][1]], nbuf.at[b, blocks[b][2]]
        return remote(source, arrived, rel_s.at[b], rel_r.at[b], peers[b][0])

    def misfit_copy(m):
        block = mbuf.at[blocks[1][1] if m == 2 else own[1]]
        return remote(block, block, mis_s.at[0], mis_r.at[m], peers[1][m % 2])

    def misfit_sent():
        block = mbuf.at[pl.ds(0, 3)]
        remote(block, block, mis_s.at[0], mis_r.at[0], peers[1][0]).wait_send()

    def o_copy(b, m):
        return remote(
            ost.at[b, blocks[b][m]], obuf.at[b, own[b]], o_s.at[b], o_r.at[b], peers[b][m]
        )

    def o_all(b):
        source, arrived = ost.at[b, pl.ds(0, 3)], obuf.at[b, pl.ds(0, 3)]
        return remote(source, arrived, o_s.at[b], o_r.at[b], peers[b][0])

    def g_copy(m):
        return remote(
            gst.at[blocks[0][m]], gbuf.at[0, own[0]], g_s.at[0], g_r.at[m], peers[0][m]
        )

    def g_sent():
        source, arrived = gst.at[pl.ds(0, 3)], gbuf.at[0, pl.ds(0, 3)]
        remote(source, arrived, g_s.at[0], g_r.at[0], peers[0][0]).wait_send()

    def gp_copy(b, m, h):
        return remote(
            gpst.at[b, h, blocks[b][m]],
            gpbuf.at[b, own[b], h],
            gp_s.at[b, m],
            gp_r.at[b, m],
            peers[b][m],
        )

    def gp_all(b, m):
        source, arrived = gpst.at[b, :, blocks[b][m]], gpbuf.at[b, blocks[b][m]]
        return remote(source, arrived, gp_s.at[b, m], gp_r.at[b, m], peers[b][m])

    def red_copy(stage, k):
        return remote(
            part.at[stage, 0],
            part.at[stage, k + 1],
            red_s.at[stage],
            red_r.at[stage],
            red_peers[stage][k],
        )

    def red_all(stage):
        peers_of = red_peers[stage]
        block = part.at[stage, pl.ds(1, len(peers_of))]
        return remote(block, block, red_s.at[stage], red_r.at[stage], peers_of[0])

    def red_send(stage, value):
        part[stage, 0] = value
        for k in range(len(red_peers[stage])):
            red_copy(stage, k).start()

    def red_take(stage):
        red_all(stage).wait_recv()
        total = part[stage, 0]
        for k in range(len(red_peers[stage])):
            total = total + part[stage, k + 1]
        return total

    fraction = jnp.full((1, TOK), timestep[0].astype(f32), f32) / (STEPS - 1)
    noise_level = sigma_low * jnp.exp(fraction * math.log(sigma_high / sigma_low))
    spread = noise_level * noise_level + sigma_data * sigma_data
    c_skip = sigma_data * sigma_data / spread
    c_out = noise_level * sigma_data * lax.rsqrt(spread)
    c_in = lax.rsqrt(spread)

    def normalise(b, stream):
        inv = lax.rsqrt(jnp.sum(stream * stream, axis=0, keepdims=True) * (1.0 / D) + norm_eps)
        inverse[b] = inv
        nbuf[b, own[b]] = (stream * inv).astype(bf16)

    noisy_in.wait()
    noisy_t[...] = noisy_v[...].astype(f32).T
    normalise(0, c_in * noisy_t[...])
    pl.semaphore_wait(barrier, len(greeted))

    def gather_start(b):
        for k in range(CHUNKS):
            far_copy(b, k).start()
        near_copy(b).start()

    def prepare_weights(b):
        for third in range(3):
            col_in[b][third].wait()
            wt[b, third * TOK : (third + 1) * TOK, :] = wcol[b, third].T

    def project(b, block):
        packed = dot(wt[b], nbuf[b, block])
        q = split3(packed[:TOK] * (SCALE * LOG2E))
        k = split3(packed[TOK : 2 * TOK])
        v = split3(packed[2 * TOK :])
        zero = jnp.zeros((HS, TOK), bf16)
        lane = lax.broadcasted_iota(jnp.int32, (GROUPS, TOK), 1)
        row = lax.broadcasted_iota(jnp.int32, (GROUPS, TOK), 0)
        member = jnp.where(row == HALF * block + lane // HS, 1.0, 0.0).astype(bf16)
        for h in range(OWN):
            at = slice(h * HS, (h + 1) * HS)
            kh, km, kl = [x[at] for x in k]
            vh, vm, vl = [x[at] for x in v]
            q3[b, h, block] = jnp.concatenate([x[at] for x in q], axis=0)
            k3[b, h, block] = jnp.concatenate([kh, km, kl], axis=0)
            v3[b, h, block] = jnp.concatenate([vh, vm, vl], axis=0)
            k8t[b, h, block] = jnp.concatenate([kh, kh, kh, km, km, kl, member], axis=0).T
            v4t[b, h, block] = jnp.concatenate([vh, vm, vl, zero], axis=0).T

    def make_mask(b):
        ids = [[segs[HALF * at + s] * 4 + mark for s in range(HALF)] for at, mark in places[b][3]]
        lane = lax.broadcasted_iota(jnp.int32, (GROUPS, TOK), 1)
        row = lax.broadcasted_iota(jnp.int32, (GROUPS, TOK), 0)
        group_id = jnp.full((GROUPS, TOK), -1, jnp.int32)
        for g in range(4 * HALF):
            group_id = jnp.where(row == g, ids[g // HALF][g % HALF], group_id)
        for j in range(4):
            line = jnp.where(
                lane < 64,
                jnp.where(lane < 32, ids[j][0], ids[j][1]),
                jnp.where(lane < 96, ids[j][2], ids[j][3]),
            )
            apart = (line != group_id) & (row < 4 * HALF)
            mrow[b, j] = jnp.where(apart, MASKED, 0.0).astype(bf16)

    def relay(b):
        for k in range(CHUNKS):
            far_copy(b, k).wait_recv()
            relay_copy(b, k).start()

    def gather_last(b):
        relay_all(b).wait_recv()
        project(b, blocks[b][2])

    def scores_of(b, h, side):
        parts = []
        for i in range(2):
            q = q3[b, h, 2 * side + i]
            qh, qm, ql = q[:HS], q[HS : 2 * HS], q[2 * HS :]
            parts.append(
                jnp.concatenate([qh, qm, ql, qh, qm, qh, mrow[b, 2 * side + i]], axis=0)
            )
        return dot(k8t[b, h].reshape(4 * TOK, 8 * HS), jnp.concatenate(parts, axis=1))

    def softmax(scores):
        shifted = jnp.exp2(scores - jnp.max(scores, axis=0, keepdims=True))
        return shifted * (1.0 / jnp.sum(shifted, axis=0, keepdims=True))

    def wide(ref, b, h):
        return jnp.concatenate([ref[b, h, i] for i in range(4)], axis=1)

    def head_rows(h):
        return pl.ds(pl.multiple_of(h * HS, HS), HS)

    def prob_grad(b, h, side):
        parts = []
        for i in range(2):
            g = gbuf[b, 2 * side + i, head_rows(h), :]
            parts.append(jnp.concatenate([g, g, g, g], axis=0))
        return dot(v4t[b, h].reshape(4 * TOK, 4 * HS), jnp.concatenate(parts, axis=1))

    def score_grad(p, grad_prob):
        row_dot = jnp.sum(p * grad_prob, axis=0, keepdims=True)
        return (p * (grad_prob - row_dot)).astype(bf16)

    def head_back(b, h):
        pw = jnp.concatenate([pbuf[b, h, 0], pbuf[b, h, 1]], axis=1)
        dw = jnp.concatenate([dbuf[h, 0], dbuf[h, 1]], axis=1)
        g = jnp.concatenate([gbuf[b, i, head_rows(h), :] for i in range(4)], axis=1)
        grad_q = (fold3(dot(wide(k3, b, h), dw)) * SCALE).astype(bf16)
        grad_k = (fold3(dot_nt(wide(q3, b, h), dw)) * (1.0 / LOG2E)).astype(bf16)
        grad_v = dot_nt(g, pw).astype(bf16)
        for j in range(4):
            at = slice(j * TOK, (j + 1) * TOK)
            gpst[b, h, j] = jnp.concatenate([grad_q[:, at], grad_k[:, at], grad_v[:, at]], axis=0)
        for m in (2, 1, 0):
            gp_copy(b, m, h).start()
        gpbuf[b, own[b], h] = gpst[b, h, own[b]]

    def packed_back(b, stream, grad_next):
        own_side = own[b] // 2
        grad_normed = None
        for side, arrivals in ((own_side, (0,)), (1 - own_side, (1, 2))):
            for m in arrivals:
                gp_all(b, m).wait_recv()
            for third in range(3):
                pieces = []
                for i in range(2):
                    for h in range(OWN):
                        pieces.append(gpbuf[b, 2 * side + i, h, third * HS : (third + 1) * HS, :])
                at = pl.multiple_of(third * D + side * 2 * TOK, TOK)
                some = dot(wfull[b, :, pl.ds(at, 2 * TOK)], jnp.concatenate(pieces, axis=0))
                grad_normed = some if grad_normed is None else grad_normed + some
        inv = inverse[b]
        normed = stream * inv
        mean = jnp.sum(grad_normed * normed, axis=0, keepdims=True) * (1.0 / D)
        return grad_next + inv * (grad_normed - normed * mean)

    def send_grads(grad_next):
        grads = dot(wofull[0], grad_next.astype(bf16)).astype(bf16)
        gst[...] = grads.reshape(4, TOK, TOK)
        for m in (2, 1, 0):
            g_copy(m).start()
        gbuf[0, own[0]] = gst[own[0]]

    def second_grads(block):
        weight = mbuf[block].astype(f32) * jnp.broadcast_to(misfit_scale, (1, D))
        grad_next = (jnp.concatenate([c_out] * 4, axis=1) * weight).astype(bf16)
        rows = wofull[1, pl.ds(pl.multiple_of(own[1] * TOK, TOK), TOK), :]
        gbuf[1, block] = dot_nt(rows, grad_next).astype(bf16)

    def branch(b):
        return dot(wot[b], obuf[b].reshape(D, TOK))

    def forward(stage):
        if stage + 1 < len(stages):
            red_send(stage + 1, red_take(stage))

    gather_start(0)
    misfit_in.wait()
    misfit_copy(1).start()
    misfit_copy(0).start()
    misfit_f = mbuf[own[1]].astype(f32)
    squares = jnp.sum(misfit_f * misfit_f, axis=0, keepdims=True)
    squares = squares[:, :128] + squares[:, 128:256] + squares[:, 256:384] + squares[:, 384:]
    red_send(0, jnp.broadcast_to(squares, (8, 128)))
    for copy in out_in + col_in[1]:
        copy.start()
    prepare_weights(0)
    project(0, own[0])
    make_mask(0)
    misfit_t[...] = misfit_f.T
    near_copy(0).wait_recv()
    project(0, blocks[0][0])
    relay(0)
    forward(0)
    project(0, blocks[0][1])
    for b in range(2):
        out_in[b].wait()
    wot[0] = wofull[0].T
    gather_last(0)
    own_side = own[0] // 2
    order = [(side, h) for side in (1 - own_side, own_side) for h in range(OWN)]
    scores = [scores_of(0, order[0][1], order[0][0])]
    for at, (side, h) in enumerate(order):
        if at + 1 < len(order):
            scores.append(scores_of(0, order[at + 1][1], order[at + 1][0]))
        p = softmax(scores.pop(0))
        prob[h, side] = p
        p = p.astype(bf16)
        pbuf[0, h, side] = p
        o = fold3(dot(wide(v3, 0, h), p)).astype(bf16)
        for i in range(2):
            ost[0, 2 * side + i, h * HS : (h + 1) * HS, :] = o[:, i * TOK : (i + 1) * TOK]
        if at == 4:
            forward(1)
        if at == 3:
            o_copy(0, 2).start()
            o_copy(0, 1).start()
    o_copy(0, 0).start()
    obuf[0, own[0]] = ost[0, own[0]]
    prepare_weights(1)
    misfit_copy(1).wait_recv()
    misfit_copy(2).start()
    o_all(0).wait_recv()
    stream1[...] = c_in * noisy_t[...] + branch(0)
    normalise(1, stream1[...])

    gather_start(1)
    full_in[1].start()
    full_in[0].start()
    project(1, own[1])
    make_mask(1)
    near_copy(1).wait_recv()
    project(1, blocks[1][0])
    square_sum = jnp.sum(red_take(len(stages) - 1)[:1], axis=1, keepdims=True)
    entries = float(n_shot * n_rec * TOK * D)
    misfit_scale = lax.rsqrt(square_sum / entries + norm_eps)
    second_grads(own[1])
    misfit_copy(0).wait_recv()
    second_grads(blocks[1][0])
    second_grads(blocks[1][1])
    misfit_copy(2).wait_recv()
    second_grads(blocks[1][2])
    relay(1)
    project(1, blocks[1][1])
    wot[1] = wofull[1].T
    gather_last(1)

    def second(pair, carry):
        todo = [(2 * pair + u, side) for u in range(2) for side in range(2)]
        ahead = [(scores_of(1, *at), prob_grad(1, *at)) for at in todo[:2]]
        for step, (h, side) in enumerate(todo):
            scores, grad_prob = ahead.pop(0)
            p = softmax(scores)
            pbuf[1, h, side] = p.astype(bf16)
            dbuf[h, side] = score_grad(p, grad_prob)
            if step + 2 < len(todo):
                at = todo[step + 2]
                ahead.append((scores_of(1, *at), prob_grad(1, *at)))
            if side == 1:
                head_back(1, h)
        return carry

    lax.fori_loop(0, OWN // 2, second, 0)

    for h in range(OWN):
        for side in range(2):
            o = fold3(dot(wide(v3, 1, h), pbuf[1, h, side])).astype(bf16)
            for i in range(2):
                ost[1, 2 * side + i, h * HS : (h + 1) * HS, :] = o[:, i * TOK : (i + 1) * TOK]
    for m in (2, 1, 0):
        o_copy(1, m).start()
    obuf[1, own[1]] = ost[1, own[1]]
    for b in (1, 0):
        full_in[b].wait()
    weight = misfit_t[...] * misfit_scale
    grad1 = packed_back(1, stream1[...], c_out * weight)
    send_grads(grad1)
    grad_mid[...] = grad1

    def first(pair, carry, side):
        todo = [2 * pair + u for u in range(2)]
        grad_probs = [prob_grad(0, h, side) for h in todo]
        for h, grad_prob in zip(todo, grad_probs):
            dbuf[h, side] = score_grad(prob[h, side], grad_prob)
        return carry

    def first_last(pair, carry):
        first(pair, carry, 1 - own_side)
        for u in range(2):
            head_back(0, 2 * pair + u)
        return carry

    g_copy(0).wait_recv()
    lax.fori_loop(0, OWN // 2, functools.partial(first, side=own_side), 0)
    g_copy(1).wait_recv()
    g_copy(2).wait_recv()
    lax.fori_loop(0, OWN // 2, first_last, 0)

    o_all(1).wait_recv()
    final = stream1[...] + branch(1)
    out_v[0] = (c_skip * noisy_t[...] + c_out * final).T.astype(bf16)
    den_out = pltpu.make_async_copy(out_v.at[0], den, out_sem.at[0])
    den_out.start()
    for b in range(2):
        near_copy(b).wait_send()
        far_sent(b)
        relay_all(b).wait_send()
        o_all(b).wait_send()
    g_sent()
    misfit_sent()
    for stage in range(len(red_peers)):
        red_all(stage).wait_send()
    for m in range(3):
        gp_all(1, m).wait_send()
    grad0 = packed_back(0, c_in * noisy_t[...], grad_mid[...])
    weight = misfit_t[...] * misfit_scale
    out_v[1] = (c_skip * weight + c_in * grad0).T.astype(bf16)
    gui_out = pltpu.make_async_copy(out_v.at[1], gui, out_sem.at[1])
    gui_out.start()

    for m in range(3):
        gp_all(0, m).wait_send()
    den_out.wait()
    gui_out.wait()


def copy_pair(den, gui, den_out, gui_out, den_v, gui_v, sem):
    into = [
        pltpu.make_async_copy(den, den_v, sem.at[0]),
        pltpu.make_async_copy(gui, gui_v, sem.at[1]),
    ]
    away = [
        pltpu.make_async_copy(den_v, den_out, sem.at[2]),
        pltpu.make_async_copy(gui_v, gui_out, sem.at[3]),
    ]
    for copy in into:
        copy.start()
    for i in range(2):
        into[i].wait()
        away[i].start()
    for copy in away:
        copy.wait()


def local(n_shot, n_rec, noisy, misfit, timestep, segment_ids, w_qkv, w_out):
    stages = reduction_stages(n_shot, n_rec)
    shape = noisy.shape
    any_space = pl.BlockSpec(memory_space=pl.ANY)
    scalars = pl.BlockSpec(memory_space=pltpu.SMEM)
    dma = pltpu.SemaphoreType.DMA
    scratch = [
        pltpu.VMEM((TOK, D), bf16),
        pltpu.VMEM((D, TOK), f32),
        pltpu.VMEM((D, TOK), f32),
        pltpu.VMEM((D, TOK), f32),
        pltpu.VMEM((D, TOK), f32),
        pltpu.VMEM((2, 1, TOK), f32),
        pltpu.VMEM((2, D, 3 * D), bf16),
        pltpu.VMEM((2, D, D), bf16),
        pltpu.VMEM((2, 3, D, TOK), bf16),
        pltpu.VMEM((2, 3 * TOK, D), bf16),
        pltpu.VMEM((2, D, D), bf16),
        pltpu.VMEM((2, 4, D, TOK), bf16),
        pltpu.VMEM((4, TOK, D), bf16),
        pltpu.VMEM((2, OWN, 4, 3 * HS, TOK), bf16),
        pltpu.VMEM((2, OWN, 4, 3 * HS, TOK), bf16),
        pltpu.VMEM((2, OWN, 4, 3 * HS, TOK), bf16),
        pltpu.VMEM((2, OWN, 4, TOK, 8 * HS), bf16),
        pltpu.VMEM((2, OWN, 4, TOK, 4 * HS), bf16),
        pltpu.VMEM((2, 4, GROUPS, TOK), bf16),
        pltpu.VMEM((OWN, 2, 4 * TOK, 2 * TOK), f32),
        pltpu.VMEM((2, OWN, 2, 4 * TOK, 2 * TOK), bf16),
        pltpu.VMEM((OWN, 2, 4 * TOK, 2 * TOK), bf16),
        pltpu.VMEM((2, 4, TOK, TOK), bf16),
        pltpu.VMEM((2, 4, TOK, TOK), bf16),
        pltpu.VMEM((4, TOK, TOK), bf16),
        pltpu.VMEM((2, 4, TOK, TOK), bf16),
        pltpu.VMEM((2, OWN, 4, 3 * HS, TOK), bf16),
        pltpu.VMEM((2, 4, OWN, 3 * HS, TOK), bf16),
        pltpu.VMEM((len(stages), 8, 8, 128), f32),
        pltpu.VMEM((2, TOK, D), bf16),
        dma((2,)),
        dma((10,)),
        dma((2,)),
        dma((2,)),
        dma((2,)),
        dma((2,)),
        dma((2, CHUNKS)),
        dma((2,)),
        dma((2,)),
        dma((1,)),
        dma((3,)),
        dma((2,)),
        dma((2,)),
        dma((1,)),
        dma((3,)),
        dma((2, 3)),
        dma((2, 3)),
        dma((len(stages),)),
        dma((len(stages),)),
    ]
    den, gui = pl.pallas_call(
        functools.partial(kernel, n_shot, n_rec, stages),
        out_shape=[jax.ShapeDtypeStruct((TOK, D), bf16)] * 2,
        in_specs=[any_space, any_space, scalars, scalars, any_space, any_space],
        out_specs=[any_space, any_space],
        scratch_shapes=scratch,
        compiler_params=pltpu.CompilerParams(
            collective_id=0, has_side_effects=True, vmem_limit_bytes=VMEM_LIMIT
        ),
        cost_estimate=pl.CostEstimate(
            flops=2_000_000_000, bytes_accessed=6_000_000, transcendentals=2_000_000
        ),
        name="window_pair",
    )(noisy.reshape(TOK, D), misfit.reshape(TOK, D), timestep, segment_ids, w_qkv, w_out)
    den, gui = pl.pallas_call(
        copy_pair,
        out_shape=[jax.ShapeDtypeStruct((TOK, D), bf16)] * 2,
        in_specs=[any_space, any_space],
        out_specs=[any_space, any_space],
        scratch_shapes=[pltpu.VMEM((TOK, D), bf16), pltpu.VMEM((TOK, D), bf16), dma((4,))],
        compiler_params=pltpu.CompilerParams(vmem_limit_bytes=VMEM_LIMIT),
        name="copy_pair",
    )(den, gui)
    return den.reshape(shape), gui.reshape(shape)


def solution(mesh):
    tokens = P(None, "shot", "rec", None, None)
    return jax.shard_map(
        functools.partial(local, mesh.shape["shot"], mesh.shape["rec"]),
        mesh=mesh,
        in_specs=(tokens, tokens, P(), P(), P(), P()),
        out_specs=(tokens, tokens),
        check_vma=False,
    )
```

```python
import functools
import math

import jax
import jax.numpy as jnp
from jax import lax
from jax.experimental import pallas as pl
from jax.experimental.pallas import tpu as pltpu
from jax.sharding import PartitionSpec as P

HEADS = 16
HS = 32
STEPS = 1000
D = 512
TOK = 128
HALF = 4
OWN = 4
GROUPS = 64
CHUNKS = 4

sigma_low = 0.5
sigma_high = 8.0
sigma_data = 0.5
norm_eps = 1e-06
SCALE = HS ** (-0.5)
LOG2E = math.log2(math.e)
MASKED = -1e30
VMEM_LIMIT = 62 * 1024 * 1024

f32 = jnp.float32
bf16 = jnp.bfloat16
MESH = pl.DeviceIdType.MESH


def reduction_stages(n_shot, n_rec):
    stages = [
        [(1, 1, min(n_rec, 4)), (0, 1, 2)],
        [(0, 16, n_shot // 16), (1, 4, n_rec // 4)],
    ]
    stages = [[digit for digit in stage if digit[2] > 1] for stage in stages]
    return [stage for stage in stages if stage]


def stage_peers(stage, shot, rec):
    place = [shot, rec]
    now, size = 0, 1
    for axis, stride, radix in stage:
        now = now + size * ((place[axis] // stride) % radix)
        size *= radix
    peers = []
    for k in range(1, size):
        later = (now + k) % size
        at = list(place)
        for axis, stride, radix in stage:
            digit = (place[axis] // stride) % radix
            at[axis] = at[axis] + stride * (later % radix - digit)
            later = later // radix
        peers.append((at[0], at[1]))
    return peers


def window_places(shot, rec, n_shot, n_rec):
    places = []
    near, far = shot % 2, rec % 2
    step_n, step_f = 1 - 2 * near, 1 - 2 * far
    places.append(
        (
            near,
            far,
            [(shot + step_n, rec), (shot, rec + step_f), (shot + step_n, rec + step_f)],
            [(shot - near + i % 2, 0) for i in range(4)],
        )
    )
    end = 1 - (rec % (n_rec - 1) + n_rec - 2) // (n_rec - 1)
    near = (shot + 1) % 2
    far = (1 - end) * ((rec + 1) % 2) + end * (((shot + 3) % 4) // 2)
    step_n, step_f = 1 - 2 * near, 1 - 2 * far
    move_s, move_r = 2 * end * step_f, (1 - end) * step_f
    near_shot = (shot + step_n + n_shot) % n_shot
    far_shot = (shot + move_s + n_shot) % n_shot
    diag_shot = (shot + step_n + move_s + n_shot) % n_shot
    first = shot - near - 2 * end * far + n_shot
    parts = []
    for i in range(4):
        at = (first + i % 2 + 2 * end * (i // 2)) % n_shot
        wrapped = 1 - (at + n_shot - 1) // n_shot
        parts.append((at, 2 * wrapped + end * (i // 2)))
    places.append(
        (near, far, [(near_shot, rec), (far_shot, rec + move_r), (diag_shot, rec + move_r)], parts)
    )
    return places


def split3(x):
    high = x.astype(bf16)
    rest = x - high.astype(f32)
    mid = rest.astype(bf16)
    low = (rest - mid.astype(f32)).astype(bf16)
    return high, mid, low


def dot(a, b):
    return lax.dot_general(a, b, (((1,), (0,)), ((), ())), preferred_element_type=f32)


def dot_nt(a, b):
    return lax.dot_general(a, b, (((1,), (1,)), ((), ())), preferred_element_type=f32)


def fold3(x):
    return x[:HS] + x[HS : 2 * HS] + x[2 * HS :]


def kernel(
    n_shot,
    n_rec,
    stages,
    noisy,
    misfit,
    timestep,
    segs,
    w_qkv,
    w_out,
    den,
    gui,
    noisy_v,
    noisy_t,
    misfit_t,
    stream1,
    grad_mid,
    inverse,
    wfull,
    wofull,
    wcol,
    wt,
    wot,
    nbuf,
    mbuf,
    q3,
    k3,
    v3,
    k8t,
    v4t,
    mrow,
    prob,
    pbuf,
    dbuf,
    ost,
    obuf,
    gst,
    gbuf,
    gpst,
    gpbuf,
    part,
    ring_own,
    ring,
    out_v,
    in_sem,
    w_sem,
    out_sem,
    near_s,
    near_r,
    far_s,
    far_r,
    rel_s,
    rel_r,
    mis_s,
    mis_r,
    o_s,
    o_r,
    g_s,
    g_r,
    gp_s,
    gp_r,
    red_s,
    red_r,
    ring_s,
    ring_r,
):
    shot, rec = lax.axis_index("shot"), lax.axis_index("rec")
    places = window_places(shot, rec, n_shot, n_rec)
    own, blocks, peers = [], [], []
    for near, far, partners, _ in places:
        here = 2 * far + near
        own.append(here)
        blocks.append([2 * far + 1 - near, 2 - 2 * far + near, 3 - 2 * far - near])
        peers.append(partners)
    red_peers = [stage_peers(stage, shot, rec) for stage in stages]
    n_z = min(n_shot // 2, 8)
    steps = n_z // 2
    at_z = (shot // 2) % n_z
    ring_peers = [
        (shot + 2 * ((at_z + 1) % n_z - at_z), rec),
        (shot + 2 * ((at_z + n_z - 1) % n_z - at_z), rec),
    ]

    barrier = pltpu.get_barrier_semaphore()
    greeted = peers[0] + peers[1] + ring_peers + [peer for some in red_peers for peer in some]
    for peer in greeted:
        pl.semaphore_signal(barrier, inc=1, device_id=peer, device_id_type=MESH)

    noisy_in = pltpu.make_async_copy(noisy, noisy_v, in_sem.at[0])
    misfit_in = pltpu.make_async_copy(misfit, mbuf.at[own[1]], in_sem.at[1])
    noisy_in.start()
    misfit_in.start()
    col_in = [
        [
            pltpu.make_async_copy(
                w_qkv.at[b, :, pl.ds(pl.multiple_of(third * D + own[b] * TOK, TOK), TOK)],
                wcol.at[b, third],
                w_sem.at[3 * b + third],
            )
            for third in range(3)
        ]
        for b in range(2)
    ]
    out_in = [pltpu.make_async_copy(w_out.at[b], wofull.at[b], w_sem.at[6 + b]) for b in range(2)]
    full_in = [pltpu.make_async_copy(w_qkv.at[b], wfull.at[b], w_sem.at[8 + b]) for b in range(2)]
    for copy in col_in[0]:
        copy.start()

    def remote(src, dst, send, recv, peer):
        return pltpu.make_async_remote_copy(
            src_ref=src, dst_ref=dst, send_sem=send, recv_sem=recv, device_id=peer, device_id_type=MESH
        )

    rows = D // CHUNKS

    def near_copy(b):
        block = nbuf.at[b, own[b]]
        return remote(block, block, near_s.at[b], near_r.at[b], peers[b][0])

    def far_copy(b, k):
        block = nbuf.at[b, own[b], pl.ds(k * rows, rows)]
        return remote(block, block, far_s.at[b], far_r.at[b, k], peers[b][1])

    def far_sent(b):
        block = nbuf.at[b, own[b]]
        remote(block, block, far_s.at[b], far_r.at[b, 0], peers[b][1]).wait_send()

    def relay_copy(b, k):
        block = nbuf.at[b, blocks[b][1], pl.ds(k * rows, rows)]
        return remote(block, block, rel_s.at[b], rel_r.at[b], peers[b][0])

    def relay_all(b):
        source, arrived = nbuf.at[b, blocks[b][1]], nbuf.at[b, blocks[b][2]]
        return remote(source, arrived, rel_s.at[b], rel_r.at[b], peers[b][0])

    def misfit_copy(m):
        block = mbuf.at[blocks[1][1] if m == 2 else own[1]]
        return remote(block, block, mis_s.at[0], mis_r.at[m], peers[1][m % 2])

    def misfit_sent():
        block = mbuf.at[pl.ds(0, 3)]
        remote(block, block, mis_s.at[0], mis_r.at[0], peers[1][0]).wait_send()

    def o_copy(b, m):
        return remote(
            ost.at[b, blocks[b][m]], obuf.at[b, own[b]], o_s.at[b], o_r.at[b], peers[b][m]
        )

    def o_all(b):
        source, arrived = ost.at[b, pl.ds(0, 3)], obuf.at[b, pl.ds(0, 3)]
        return remote(source, arrived, o_s.at[b], o_r.at[b], peers[b][0])

    def g_copy(m):
        return remote(
            gst.at[blocks[0][m]], gbuf.at[0, own[0]], g_s.at[0], g_r.at[m], peers[0][m]
        )

    def g_sent():
        source, arrived = gst.at[pl.ds(0, 3)], gbuf.at[0, pl.ds(0, 3)]
        remote(source, arrived, g_s.at[0], g_r.at[0], peers[0][0]).wait_send()

    def gp_copy(b, m, h):
        return remote(
            gpst.at[b, h, blocks[b][m]],
            gpbuf.at[b, own[b], h],
            gp_s.at[b, m],
            gp_r.at[b, m],
            peers[b][m],
        )

    def gp_all(b, m):
        source, arrived = gpst.at[b, :, blocks[b][m]], gpbuf.at[b, blocks[b][m]]
        return remote(source, arrived, gp_s.at[b, m], gp_r.at[b, m], peers[b][m])

    def red_copy(stage, k):
        return remote(
            part.at[stage, 0],
            part.at[stage, k + 1],
            red_s.at[stage],
            red_r.at[stage],
            red_peers[stage][k],
        )

    def red_all(stage):
        peers_of = red_peers[stage]
        block = part.at[stage, pl.ds(1, len(peers_of))]
        return remote(block, block, red_s.at[stage], red_r.at[stage], peers_of[0])

    def red_send(stage, value):
        part[stage, 0] = value
        for k in range(len(red_peers[stage])):
            red_copy(stage, k).start()

    def red_take(stage):
        red_all(stage).wait_recv()
        total = part[stage, 0]
        for k in range(len(red_peers[stage])):
            total = total + part[stage, k + 1]
        return total

    def ring_copy(t, d):
        source = ring_own if t == 0 else ring.at[t - 1, d]
        return remote(source, ring.at[t, d], ring_s.at[t, d], ring_r.at[t, d], ring_peers[d])

    def ring_ways(t):
        return (0,) if t == steps - 1 else (0, 1)

    def ring_step(t):
        if t > 0:
            for d in ring_ways(t - 1) if t <= steps else ():
                ring_copy(t - 1, d).wait_recv()
        if t < steps:
            for d in ring_ways(t):
                ring_copy(t, d).start()

    fraction = jnp.full((1, TOK), timestep[0].astype(f32), f32) / (STEPS - 1)
    noise_level = sigma_low * jnp.exp(fraction * math.log(sigma_high / sigma_low))
    spread = noise_level * noise_level + sigma_data * sigma_data
    c_skip = sigma_data * sigma_data / spread
    c_out = noise_level * sigma_data * lax.rsqrt(spread)
    c_in = lax.rsqrt(spread)

    def normalise(b, stream):
        inv = lax.rsqrt(jnp.sum(stream * stream, axis=0, keepdims=True) * (1.0 / D) + norm_eps)
        inverse[b] = inv
        nbuf[b, own[b]] = (stream * inv).astype(bf16)

    noisy_in.wait()
    noisy_t[...] = noisy_v[...].astype(f32).T
    normalise(0, c_in * noisy_t[...])
    pl.semaphore_wait(barrier, len(greeted))

    def gather_start(b):
        for k in range(CHUNKS):
            far_copy(b, k).start()
        near_copy(b).start()

    def prepare_weights(b):
        for third in range(3):
            col_in[b][third].wait()
            wt[b, third * TOK : (third + 1) * TOK, :] = wcol[b, third].T

    def project(b, block):
        packed = dot(wt[b], nbuf[b, block])
        q = split3(packed[:TOK] * (SCALE * LOG2E))
        k = split3(packed[TOK : 2 * TOK])
        v = split3(packed[2 * TOK :])
        zero = jnp.zeros((HS, TOK), bf16)
        lane = lax.broadcasted_iota(jnp.int32, (GROUPS, TOK), 1)
        row = lax.broadcasted_iota(jnp.int32, (GROUPS, TOK), 0)
        member = jnp.where(row == HALF * block + lane // HS, 1.0, 0.0).astype(bf16)
        for h in range(OWN):
            at = slice(h * HS, (h + 1) * HS)
            kh, km, kl = [x[at] for x in k]
            vh, vm, vl = [x[at] for x in v]
            q3[b, h, block] = jnp.concatenate([x[at] for x in q], axis=0)
            k3[b, h, block] = jnp.concatenate([kh, km, kl], axis=0)
            v3[b, h, block] = jnp.concatenate([vh, vm, vl], axis=0)
            k8t[b, h, block] = jnp.concatenate([kh, kh, kh, km, km, kl, member], axis=0).T
            v4t[b, h, block] = jnp.concatenate([vh, vm, vl, zero], axis=0).T

    def make_mask(b):
        ids = [[segs[HALF * at + s] * 4 + mark for s in range(HALF)] for at, mark in places[b][3]]
        lane = lax.broadcasted_iota(jnp.int32, (GROUPS, TOK), 1)
        row = lax.broadcasted_iota(jnp.int32, (GROUPS, TOK), 0)
        group_id = jnp.full((GROUPS, TOK), -1, jnp.int32)
        for g in range(4 * HALF):
            group_id = jnp.where(row == g, ids[g // HALF][g % HALF], group_id)
        for j in range(4):
            line = jnp.where(
                lane < 64,
                jnp.where(lane < 32, ids[j][0], ids[j][1]),
                jnp.where(lane < 96, ids[j][2], ids[j][3]),
            )
            apart = (line != group_id) & (row < 4 * HALF)
            mrow[b, j] = jnp.where(apart, MASKED, 0.0).astype(bf16)

    def relay(b):
        for k in range(CHUNKS):
            far_copy(b, k).wait_recv()
            relay_copy(b, k).start()

    def gather_last(b):
        relay_all(b).wait_recv()
        project(b, blocks[b][2])

    def scores_of(b, h, side):
        parts = []
        for i in range(2):
            q = q3[b, h, 2 * side + i]
            qh, qm, ql = q[:HS], q[HS : 2 * HS], q[2 * HS :]
            parts.append(
                jnp.concatenate([qh, qm, ql, qh, qm, qh, mrow[b, 2 * side + i]], axis=0)
            )
        return dot(k8t[b, h].reshape(4 * TOK, 8 * HS), jnp.concatenate(parts, axis=1))

    def softmax(scores):
        shifted = jnp.exp2(scores - jnp.max(scores, axis=0, keepdims=True))
        return shifted * (1.0 / jnp.sum(shifted, axis=0, keepdims=True))

    def wide(ref, b, h):
        return jnp.concatenate([ref[b, h, i] for i in range(4)], axis=1)

    def head_rows(h):
        return pl.ds(pl.multiple_of(h * HS, HS), HS)

    def prob_grad(b, h, side):
        parts = []
        for i in range(2):
            g = gbuf[b, 2 * side + i, head_rows(h), :]
            parts.append(jnp.concatenate([g, g, g, g], axis=0))
        return dot(v4t[b, h].reshape(4 * TOK, 4 * HS), jnp.concatenate(parts, axis=1))

    def score_grad(p, grad_prob):
        row_dot = jnp.sum(p * grad_prob, axis=0, keepdims=True)
        return (p * (grad_prob - row_dot)).astype(bf16)

    def head_back(b, h, side):
        keys = pl.ds(pl.multiple_of(side * 2 * TOK, TOK), 2 * TOK)
        pw = jnp.concatenate([pbuf[b, h, 0, keys, :], pbuf[b, h, 1, keys, :]], axis=1)
        dw = jnp.concatenate([dbuf[h, 0, keys, :], dbuf[h, 1, keys, :]], axis=1)
        g = jnp.concatenate([gbuf[b, i, head_rows(h), :] for i in range(4)], axis=1)
        grad_q = (fold3(dot(wide(k3, b, h), dbuf[h, side])) * SCALE).astype(bf16)
        grad_k = (fold3(dot_nt(wide(q3, b, h), dw)) * (1.0 / LOG2E)).astype(bf16)
        grad_v = dot_nt(g, pw).astype(bf16)
        for i in range(2):
            at = slice(i * TOK, (i + 1) * TOK)
            gpst[b, h, 2 * side + i] = jnp.concatenate(
                [grad_q[:, at], grad_k[:, at], grad_v[:, at]], axis=0
            )

    def other_back(b, h):
        head_back(b, h, 1 - own[b] // 2)
        gp_copy(b, 2, h).start()
        gp_copy(b, 1, h).start()

    def own_back(pair, carry, b):
        for u in range(2):
            h = 2 * pair + u
            head_back(b, h, own[b] // 2)
            gp_copy(b, 0, h).start()
            gpbuf[b, own[b], h] = gpst[b, h, own[b]]
        return carry

    def packed_back(b, stream, grad_next):
        own_side = own[b] // 2
        grad_normed = None
        for side, arrivals in ((own_side, (0,)), (1 - own_side, (1, 2))):
            for m in arrivals:
                gp_all(b, m).wait_recv()
            for third in range(3):
                pieces = []
                for i in range(2):
                    for h in range(OWN):
                        pieces.append(gpbuf[b, 2 * side + i, h, third * HS : (third + 1) * HS, :])
                at = pl.multiple_of(third * D + side * 2 * TOK, TOK)
                some = dot(wfull[b, :, pl.ds(at, 2 * TOK)], jnp.concatenate(pieces, axis=0))
                grad_normed = some if grad_normed is None else grad_normed + some
        inv = inverse[b]
        normed = stream * inv
        mean = jnp.sum(grad_normed * normed, axis=0, keepdims=True) * (1.0 / D)
        return grad_next + inv * (grad_normed - normed * mean)

    def send_grads(grad_next):
        grads = dot(wofull[0], grad_next.astype(bf16)).astype(bf16)
        gst[...] = grads.reshape(4, TOK, TOK)
        for m in (2, 1, 0):
            g_copy(m).start()
        gbuf[0, own[0]] = gst[own[0]]

    def second_grads(block):
        weight = mbuf[block].astype(f32) * jnp.broadcast_to(misfit_scale, (1, D))
        grad_next = (jnp.concatenate([c_out] * 4, axis=1) * weight).astype(bf16)
        rows = wofull[1, pl.ds(pl.multiple_of(own[1] * TOK, TOK), TOK), :]
        gbuf[1, block] = dot_nt(rows, grad_next).astype(bf16)

    def branch(b):
        return dot(wot[b], obuf[b].reshape(D, TOK))

    def forward(stage):
        if stage + 1 < len(stages):
            red_send(stage + 1, red_take(stage))

    gather_start(0)
    misfit_in.wait()
    misfit_copy(1).start()
    misfit_copy(0).start()
    misfit_f = mbuf[own[1]].astype(f32)
    squares = jnp.sum(misfit_f * misfit_f, axis=0, keepdims=True)
    squares = squares[:, :128] + squares[:, 128:256] + squares[:, 256:384] + squares[:, 384:]
    red_send(0, jnp.broadcast_to(squares, (8, 128)))
    for copy in out_in + col_in[1]:
        copy.start()
    prepare_weights(0)
    project(0, own[0])
    make_mask(0)
    misfit_t[...] = misfit_f.T
    near_copy(0).wait_recv()
    project(0, blocks[0][0])
    relay(0)
    forward(0)
    project(0, blocks[0][1])
    for b in range(2):
        out_in[b].wait()
    wot[0] = wofull[0].T
    gather_last(0)
    own_side = own[0] // 2
    order = [(side, h) for side in (1 - own_side, own_side) for h in range(OWN)]
    scores = [scores_of(0, order[0][1], order[0][0])]
    for at, (side, h) in enumerate(order):
        if at + 1 < len(order):
            scores.append(scores_of(0, order[at + 1][1], order[at + 1][0]))
        p = softmax(scores.pop(0))
        prob[h, side] = p
        p = p.astype(bf16)
        pbuf[0, h, side] = p
        o = fold3(dot(wide(v3, 0, h), p)).astype(bf16)
        for i in range(2):
            ost[0, 2 * side + i, h * HS : (h + 1) * HS, :] = o[:, i * TOK : (i + 1) * TOK]
        if at == 4:
            ring_own[...] = red_take(len(stages) - 1)
            ring_step(0)
        if at == 3:
            o_copy(0, 2).start()
            o_copy(0, 1).start()
    o_copy(0, 0).start()
    obuf[0, own[0]] = ost[0, own[0]]
    prepare_weights(1)
    misfit_copy(1).wait_recv()
    misfit_copy(2).start()
    ring_step(1)
    o_all(0).wait_recv()
    stream1[...] = c_in * noisy_t[...] + branch(0)
    normalise(1, stream1[...])

    gather_start(1)
    full_in[1].start()
    full_in[0].start()
    ring_step(2)
    project(1, own[1])
    make_mask(1)
    ring_step(3)
    near_copy(1).wait_recv()
    project(1, blocks[1][0])
    ring_step(4)
    ring_sum = ring_own[...]
    for t in range(steps):
        for d in ring_ways(t):
            ring_sum = ring_sum + ring[t, d]
    square_sum = jnp.sum(ring_sum[:1], axis=1, keepdims=True)
    entries = float(n_shot * n_rec * TOK * D)
    misfit_scale = lax.rsqrt(square_sum / entries + norm_eps)
    second_grads(own[1])
    misfit_copy(0).wait_recv()
    second_grads(blocks[1][0])
    second_grads(blocks[1][1])
    misfit_copy(2).wait_recv()
    second_grads(blocks[1][2])
    relay(1)
    project(1, blocks[1][1])
    wot[1] = wofull[1].T
    gather_last(1)

    def second(pair, carry):
        todo = [(2 * pair + u, side) for u in range(2) for side in range(2)]
        ahead = [(scores_of(1, *at), prob_grad(1, *at)) for at in todo[:2]]
        for step, (h, side) in enumerate(todo):
            scores, grad_prob = ahead.pop(0)
            p = softmax(scores)
            pbuf[1, h, side] = p.astype(bf16)
            dbuf[h, side] = score_grad(p, grad_prob)
            if step + 2 < len(todo):
                at = todo[step + 2]
                ahead.append((scores_of(1, *at), prob_grad(1, *at)))
            if side == 1:
                other_back(1, h)
        return carry

    lax.fori_loop(0, OWN // 2, second, 0)
    lax.fori_loop(0, OWN // 2, functools.partial(own_back, b=1), 0)

    for h in range(OWN):
        for side in range(2):
            o = fold3(dot(wide(v3, 1, h), pbuf[1, h, side])).astype(bf16)
            for i in range(2):
                ost[1, 2 * side + i, h * HS : (h + 1) * HS, :] = o[:, i * TOK : (i + 1) * TOK]
    for m in (2, 1, 0):
        o_copy(1, m).start()
    obuf[1, own[1]] = ost[1, own[1]]
    for b in (1, 0):
        full_in[b].wait()
    weight = misfit_t[...] * misfit_scale
    grad1 = packed_back(1, stream1[...], c_out * weight)
    send_grads(grad1)
    grad_mid[...] = grad1

    def first(pair, carry, side):
        todo = [2 * pair + u for u in range(2)]
        grad_probs = [prob_grad(0, h, side) for h in todo]
        for h, grad_prob in zip(todo, grad_probs):
            dbuf[h, side] = score_grad(prob[h, side], grad_prob)
        return carry

    def first_last(pair, carry):
        first(pair, carry, 1 - own_side)
        for u in range(2):
            other_back(0, 2 * pair + u)
        return carry

    g_copy(0).wait_recv()
    lax.fori_loop(0, OWN // 2, functools.partial(first, side=own_side), 0)
    g_copy(1).wait_recv()
    g_copy(2).wait_recv()
    lax.fori_loop(0, OWN // 2, first_last, 0)
    lax.fori_loop(0, OWN // 2, functools.partial(own_back, b=0), 0)

    o_all(1).wait_recv()
    final = stream1[...] + branch(1)
    out_v[0] = (c_skip * noisy_t[...] + c_out * final).T.astype(bf16)
    den_out = pltpu.make_async_copy(out_v.at[0], den, out_sem.at[0])
    den_out.start()
    for b in range(2):
        near_copy(b).wait_send()
        far_sent(b)
        relay_all(b).wait_send()
        o_all(b).wait_send()
    g_sent()
    misfit_sent()
    for stage in range(len(red_peers)):
        red_all(stage).wait_send()
    for t in range(steps):
        for d in ring_ways(t):
            ring_copy(t, d).wait_send()
    for m in range(3):
        gp_all(1, m).wait_send()
    grad0 = packed_back(0, c_in * noisy_t[...], grad_mid[...])
    weight = misfit_t[...] * misfit_scale
    out_v[1] = (c_skip * weight + c_in * grad0).T.astype(bf16)
    gui_out = pltpu.make_async_copy(out_v.at[1], gui, out_sem.at[1])
    gui_out.start()

    for m in range(3):
        gp_all(0, m).wait_send()
    den_out.wait()
    gui_out.wait()


def copy_pair(den, gui, den_out, gui_out, den_v, gui_v, sem):
    into = [
        pltpu.make_async_copy(den, den_v, sem.at[0]),
        pltpu.make_async_copy(gui, gui_v, sem.at[1]),
    ]
    away = [
        pltpu.make_async_copy(den_v, den_out, sem.at[2]),
        pltpu.make_async_copy(gui_v, gui_out, sem.at[3]),
    ]
    for copy in into:
        copy.start()
    for i in range(2):
        into[i].wait()
        away[i].start()
    for copy in away:
        copy.wait()


def local(n_shot, n_rec, noisy, misfit, timestep, segment_ids, w_qkv, w_out):
    stages = reduction_stages(n_shot, n_rec)
    shape = noisy.shape
    any_space = pl.BlockSpec(memory_space=pl.ANY)
    scalars = pl.BlockSpec(memory_space=pltpu.SMEM)
    dma = pltpu.SemaphoreType.DMA
    scratch = [
        pltpu.VMEM((TOK, D), bf16),
        pltpu.VMEM((D, TOK), f32),
        pltpu.VMEM((D, TOK), f32),
        pltpu.VMEM((D, TOK), f32),
        pltpu.VMEM((D, TOK), f32),
        pltpu.VMEM((2, 1, TOK), f32),
        pltpu.VMEM((2, D, 3 * D), bf16),
        pltpu.VMEM((2, D, D), bf16),
        pltpu.VMEM((2, 3, D, TOK), bf16),
        pltpu.VMEM((2, 3 * TOK, D), bf16),
        pltpu.VMEM((2, D, D), bf16),
        pltpu.VMEM((2, 4, D, TOK), bf16),
        pltpu.VMEM((4, TOK, D), bf16),
        pltpu.VMEM((2, OWN, 4, 3 * HS, TOK), bf16),
        pltpu.VMEM((2, OWN, 4, 3 * HS, TOK), bf16),
        pltpu.VMEM((2, OWN, 4, 3 * HS, TOK), bf16),
        pltpu.VMEM((2, OWN, 4, TOK, 8 * HS), bf16),
        pltpu.VMEM((2, OWN, 4, TOK, 4 * HS), bf16),
        pltpu.VMEM((2, 4, GROUPS, TOK), bf16),
        pltpu.VMEM((OWN, 2, 4 * TOK, 2 * TOK), f32),
        pltpu.VMEM((2, OWN, 2, 4 * TOK, 2 * TOK), bf16),
        pltpu.VMEM((OWN, 2, 4 * TOK, 2 * TOK), bf16),
        pltpu.VMEM((2, 4, TOK, TOK), bf16),
        pltpu.VMEM((2, 4, TOK, TOK), bf16),
        pltpu.VMEM((4, TOK, TOK), bf16),
        pltpu.VMEM((2, 4, TOK, TOK), bf16),
        pltpu.VMEM((2, OWN, 4, 3 * HS, TOK), bf16),
        pltpu.VMEM((2, 4, OWN, 3 * HS, TOK), bf16),
        pltpu.VMEM((len(stages), 8, 8, 128), f32),
        pltpu.VMEM((8, 128), f32),
        pltpu.VMEM((4, 2, 8, 128), f32),
        pltpu.VMEM((2, TOK, D), bf16),
        dma((2,)),
        dma((10,)),
        dma((2,)),
        dma((2,)),
        dma((2,)),
        dma((2,)),
        dma((2, CHUNKS)),
        dma((2,)),
        dma((2,)),
        dma((1,)),
        dma((3,)),
        dma((2,)),
        dma((2,)),
        dma((1,)),
        dma((3,)),
        dma((2, 3)),
        dma((2, 3)),
        dma((len(stages),)),
        dma((len(stages),)),
        dma((4, 2)),
        dma((4, 2)),
    ]
    den, gui = pl.pallas_call(
        functools.partial(kernel, n_shot, n_rec, stages),
        out_shape=[jax.ShapeDtypeStruct((TOK, D), bf16)] * 2,
        in_specs=[any_space, any_space, scalars, scalars, any_space, any_space],
        out_specs=[any_space, any_space],
        scratch_shapes=scratch,
        compiler_params=pltpu.CompilerParams(
            collective_id=0, has_side_effects=True, vmem_limit_bytes=VMEM_LIMIT
        ),
        cost_estimate=pl.CostEstimate(
            flops=2_000_000_000, bytes_accessed=6_000_000, transcendentals=2_000_000
        ),
        name="window_pair",
    )(noisy.reshape(TOK, D), misfit.reshape(TOK, D), timestep, segment_ids, w_qkv, w_out)
    den, gui = pl.pallas_call(
        copy_pair,
        out_shape=[jax.ShapeDtypeStruct((TOK, D), bf16)] * 2,
        in_specs=[any_space, any_space],
        out_specs=[any_space, any_space],
        scratch_shapes=[pltpu.VMEM((TOK, D), bf16), pltpu.VMEM((TOK, D), bf16), dma((4,))],
        compiler_params=pltpu.CompilerParams(vmem_limit_bytes=VMEM_LIMIT),
        name="copy_pair",
    )(den, gui)
    return den.reshape(shape), gui.reshape(shape)


def solution(mesh):
    tokens = P(None, "shot", "rec", None, None)
    return jax.shard_map(
        functools.partial(local, mesh.shape["shot"], mesh.shape["rec"]),
        mesh=mesh,
        in_specs=(tokens, tokens, P(), P(), P(), P()),
        out_specs=(tokens, tokens),
        check_vma=False,
    )
```

```python
import functools
import math

import jax
import jax.numpy as jnp
from jax import lax
from jax.experimental import pallas as pl
from jax.experimental.pallas import tpu as pltpu
from jax.sharding import PartitionSpec as P

HEADS = 16
HS = 32
STEPS = 1000
D = 512
TOK = 128
HALF = 4
OWN = 4
GROUPS = 64
CHUNKS = 4

sigma_low = 0.5
sigma_high = 8.0
sigma_data = 0.5
norm_eps = 1e-06
SCALE = HS ** (-0.5)
LOG2E = math.log2(math.e)
MASKED = -1e30
VMEM_LIMIT = 62 * 1024 * 1024

f32 = jnp.float32
bf16 = jnp.bfloat16
MESH = pl.DeviceIdType.MESH


def reduction_stages(n_shot, n_rec):
    stages = [
        [(1, 1, min(n_rec, 4)), (0, 1, 2)],
        [(0, 16, n_shot // 16), (1, 4, n_rec // 4)],
        [(0, 2, min(n_shot // 2, 8))],
    ]
    stages = [[digit for digit in stage if digit[2] > 1] for stage in stages]
    return [stage for stage in stages if stage]


def stage_peers(stage, shot, rec):
    place = [shot, rec]
    now, size = 0, 1
    for axis, stride, radix in stage:
        now = now + size * ((place[axis] // stride) % radix)
        size *= radix
    peers = []
    for k in range(1, size):
        later = (now + k) % size
        at = list(place)
        for axis, stride, radix in stage:
            digit = (place[axis] // stride) % radix
            at[axis] = at[axis] + stride * (later % radix - digit)
            later = later // radix
        peers.append((at[0], at[1]))
    return peers


def window_places(shot, rec, n_shot, n_rec):
    places = []
    near, far = shot % 2, rec % 2
    step_n, step_f = 1 - 2 * near, 1 - 2 * far
    places.append(
        (
            near,
            far,
            [(shot + step_n, rec), (shot, rec + step_f), (shot + step_n, rec + step_f)],
            [(shot - near + i % 2, 0) for i in range(4)],
        )
    )
    end = 1 - (rec % (n_rec - 1) + n_rec - 2) // (n_rec - 1)
    near = (shot + 1) % 2
    far = (1 - end) * ((rec + 1) % 2) + end * (((shot + 3) % 4) // 2)
    step_n, step_f = 1 - 2 * near, 1 - 2 * far
    move_s, move_r = 2 * end * step_f, (1 - end) * step_f
    near_shot = (shot + step_n + n_shot) % n_shot
    far_shot = (shot + move_s + n_shot) % n_shot
    diag_shot = (shot + step_n + move_s + n_shot) % n_shot
    first = shot - near - 2 * end * far + n_shot
    parts = []
    for i in range(4):
        at = (first + i % 2 + 2 * end * (i // 2)) % n_shot
        wrapped = 1 - (at + n_shot - 1) // n_shot
        parts.append((at, 2 * wrapped + end * (i // 2)))
    places.append(
        (near, far, [(near_shot, rec), (far_shot, rec + move_r), (diag_shot, rec + move_r)], parts)
    )
    return places


def split3(x):
    high = x.astype(bf16)
    rest = x - high.astype(f32)
    mid = rest.astype(bf16)
    low = (rest - mid.astype(f32)).astype(bf16)
    return high, mid, low


def dot(a, b):
    return lax.dot_general(a, b, (((1,), (0,)), ((), ())), preferred_element_type=f32)


def dot_nt(a, b):
    return lax.dot_general(a, b, (((1,), (1,)), ((), ())), preferred_element_type=f32)


def fold3(x):
    return x[:HS] + x[HS : 2 * HS] + x[2 * HS :]


def kernel(
    n_shot,
    n_rec,
    stages,
    noisy,
    misfit,
    timestep,
    segs,
    w_qkv,
    w_out,
    den,
    gui,
    noisy_v,
    noisy_t,
    misfit_t,
    stream1,
    grad_mid,
    inverse,
    wfull,
    wofull,
    wcol,
    wt,
    wot,
    nbuf,
    mbuf,
    q3,
    k3,
    v3,
    k8t,
    v4t,
    mrow,
    prob,
    pbuf,
    dbuf,
    ost,
    obuf,
    gst,
    gbuf,
    gpst,
    gpbuf,
    part,
    out_v,
    in_sem,
    w_sem,
    out_sem,
    near_s,
    near_r,
    far_s,
    far_r,
    rel_s,
    rel_r,
    mis_s,
    mis_r,
    o_s,
    o_r,
    g_s,
    g_r,
    gp_s,
    gp_r,
    red_s,
    red_r,
):
    shot, rec = lax.axis_index("shot"), lax.axis_index("rec")
    places = window_places(shot, rec, n_shot, n_rec)
    own, blocks, peers = [], [], []
    for near, far, partners, _ in places:
        here = 2 * far + near
        own.append(here)
        blocks.append([2 * far + 1 - near, 2 - 2 * far + near, 3 - 2 * far - near])
        peers.append(partners)
    red_peers = [stage_peers(stage, shot, rec) for stage in stages]

    barrier = pltpu.get_barrier_semaphore()
    greeted = peers[0] + peers[1] + [peer for some in red_peers for peer in some]
    for peer in greeted:
        pl.semaphore_signal(barrier, inc=1, device_id=peer, device_id_type=MESH)

    noisy_in = pltpu.make_async_copy(noisy, noisy_v, in_sem.at[0])
    misfit_in = pltpu.make_async_copy(misfit, mbuf.at[own[1]], in_sem.at[1])
    noisy_in.start()
    misfit_in.start()
    col_in = [
        [
            pltpu.make_async_copy(
                w_qkv.at[b, :, pl.ds(pl.multiple_of(third * D + own[b] * TOK, TOK), TOK)],
                wcol.at[b, third],
                w_sem.at[3 * b + third],
            )
            for third in range(3)
        ]
        for b in range(2)
    ]
    out_in = [pltpu.make_async_copy(w_out.at[b], wofull.at[b], w_sem.at[6 + b]) for b in range(2)]
    full_in = [pltpu.make_async_copy(w_qkv.at[b], wfull.at[b], w_sem.at[8 + b]) for b in range(2)]
    for copy in col_in[0]:
        copy.start()

    def remote(src, dst, send, recv, peer):
        return pltpu.make_async_remote_copy(
            src_ref=src, dst_ref=dst, send_sem=send, recv_sem=recv, device_id=peer, device_id_type=MESH
        )

    rows = D // CHUNKS

    def near_copy(b):
        block = nbuf.at[b, own[b]]
        return remote(block, block, near_s.at[b], near_r.at[b], peers[b][0])

    def far_copy(b, k):
        block = nbuf.at[b, own[b], pl.ds(k * rows, rows)]
        return remote(block, block, far_s.at[b], far_r.at[b, k], peers[b][1])

    def far_sent(b):
        block = nbuf.at[b, own[b]]
        remote(block, block, far_s.at[b], far_r.at[b, 0], peers[b][1]).wait_send()

    def relay_copy(b, k):
        block = nbuf.at[b, blocks[b][1], pl.ds(k * rows, rows)]
        return remote(block, block, rel_s.at[b], rel_r.at[b], peers[b][0])

    def relay_all(b):
        source, arrived = nbuf.at[b, blocks[b][1]], nbuf.at[b, blocks[b][2]]
        return remote(source, arrived, rel_s.at[b], rel_r.at[b], peers[b][0])

    def misfit_copy(m):
        block = mbuf.at[blocks[1][1] if m == 2 else own[1]]
        return remote(block, block, mis_s.at[0], mis_r.at[m], peers[1][m % 2])

    def misfit_sent():
        block = mbuf.at[pl.ds(0, 3)]
        remote(block, block, mis_s.at[0], mis_r.at[0], peers[1][0]).wait_send()

    def o_copy(b, m):
        return remote(
            ost.at[b, blocks[b][m]], obuf.at[b, own[b]], o_s.at[b], o_r.at[b], peers[b][m]
        )

    def o_all(b):
        source, arrived = ost.at[b, pl.ds(0, 3)], obuf.at[b, pl.ds(0, 3)]
        return remote(source, arrived, o_s.at[b], o_r.at[b], peers[b][0])

    def g_copy(m):
        return remote(
            gst.at[blocks[0][m]], gbuf.at[0, own[0]], g_s.at[0], g_r.at[m], peers[0][m]
        )

    def g_sent():
        source, arrived = gst.at[pl.ds(0, 3)], gbuf.at[0, pl.ds(0, 3)]
        remote(source, arrived, g_s.at[0], g_r.at[0], peers[0][0]).wait_send()

    def gp_copy(b, m, h):
        return remote(
            gpst.at[b, h, blocks[b][m]],
            gpbuf.at[b, own[b], h],
            gp_s.at[b, m],
            gp_r.at[b, m],
            peers[b][m],
        )

    def gp_all(b, m):
        source, arrived = gpst.at[b, :, blocks[b][m]], gpbuf.at[b, blocks[b][m]]
        return remote(source, arrived, gp_s.at[b, m], gp_r.at[b, m], peers[b][m])

    def red_copy(stage, k):
        return remote(
            part.at[stage, 0],
            part.at[stage, k + 1],
            red_s.at[stage],
            red_r.at[stage],
            red_peers[stage][k],
        )

    def red_all(stage):
        peers_of = red_peers[stage]
        block = part.at[stage, pl.ds(1, len(peers_of))]
        return remote(block, block, red_s.at[stage], red_r.at[stage], peers_of[0])

    def red_send(stage, value):
        part[stage, 0] = value
        for k in range(len(red_peers[stage])):
            red_copy(stage, k).start()

    def red_take(stage):
        red_all(stage).wait_recv()
        total = part[stage, 0]
        for k in range(len(red_peers[stage])):
            total = total + part[stage, k + 1]
        return total

    fraction = jnp.full((1, TOK), timestep[0].astype(f32), f32) / (STEPS - 1)
    noise_level = sigma_low * jnp.exp(fraction * math.log(sigma_high / sigma_low))
    spread = noise_level * noise_level + sigma_data * sigma_data
    c_skip = sigma_data * sigma_data / spread
    c_out = noise_level * sigma_data * lax.rsqrt(spread)
    c_in = lax.rsqrt(spread)

    def normalise(b, stream):
        inv = lax.rsqrt(jnp.sum(stream * stream, axis=0, keepdims=True) * (1.0 / D) + norm_eps)
        inverse[b] = inv
        nbuf[b, own[b]] = (stream * inv).astype(bf16)

    noisy_in.wait()
    noisy_t[...] = noisy_v[...].astype(f32).T
    normalise(0, c_in * noisy_t[...])
    pl.semaphore_wait(barrier, len(greeted))

    def gather_start(b):
        for k in range(CHUNKS):
            far_copy(b, k).start()
        near_copy(b).start()

    def prepare_weights(b):
        for third in range(3):
            col_in[b][third].wait()
            wt[b, third * TOK : (third + 1) * TOK, :] = wcol[b, third].T

    def project(b, block):
        packed = dot(wt[b], nbuf[b, block])
        q = split3(packed[:TOK] * (SCALE * LOG2E))
        k = split3(packed[TOK : 2 * TOK])
        v = split3(packed[2 * TOK :])
        zero = jnp.zeros((HS, TOK), bf16)
        lane = lax.broadcasted_iota(jnp.int32, (GROUPS, TOK), 1)
        row = lax.broadcasted_iota(jnp.int32, (GROUPS, TOK), 0)
        member = jnp.where(row == HALF * block + lane // HS, 1.0, 0.0).astype(bf16)
        for h in range(OWN):
            at = slice(h * HS, (h + 1) * HS)
            kh, km, kl = [x[at] for x in k]
            vh, vm, vl = [x[at] for x in v]
            q3[b, h, block] = jnp.concatenate([x[at] for x in q], axis=0)
            k3[b, h, block] = jnp.concatenate([kh, km, kl], axis=0)
            v3[b, h, block] = jnp.concatenate([vh, vm, vl], axis=0)
            k8t[b, h, block] = jnp.concatenate([kh, kh, kh, km, km, kl, member], axis=0).T
            v4t[b, h, block] = jnp.concatenate([vh, vm, vl, zero], axis=0).T

    def make_mask(b):
        ids = [[segs[HALF * at + s] * 4 + mark for s in range(HALF)] for at, mark in places[b][3]]
        lane = lax.broadcasted_iota(jnp.int32, (GROUPS, TOK), 1)
        row = lax.broadcasted_iota(jnp.int32, (GROUPS, TOK), 0)
        group_id = jnp.full((GROUPS, TOK), -1, jnp.int32)
        for g in range(4 * HALF):
            group_id = jnp.where(row == g, ids[g // HALF][g % HALF], group_id)
        for j in range(4):
            line = jnp.where(
                lane < 64,
                jnp.where(lane < 32, ids[j][0], ids[j][1]),
                jnp.where(lane < 96, ids[j][2], ids[j][3]),
            )
            apart = (line != group_id) & (row < 4 * HALF)
            mrow[b, j] = jnp.where(apart, MASKED, 0.0).astype(bf16)

    def relay(b):
        for k in range(CHUNKS):
            far_copy(b, k).wait_recv()
            relay_copy(b, k).start()

    def gather_last(b):
        relay_all(b).wait_recv()
        project(b, blocks[b][2])

    def scores_of(b, h, side):
        parts = []
        for i in range(2):
            q = q3[b, h, 2 * side + i]
            qh, qm, ql = q[:HS], q[HS : 2 * HS], q[2 * HS :]
            parts.append(
                jnp.concatenate([qh, qm, ql, qh, qm, qh, mrow[b, 2 * side + i]], axis=0)
            )
        return dot(k8t[b, h].reshape(4 * TOK, 8 * HS), jnp.concatenate(parts, axis=1))

    def softmax(scores):
        shifted = jnp.exp2(scores - jnp.max(scores, axis=0, keepdims=True))
        return shifted * (1.0 / jnp.sum(shifted, axis=0, keepdims=True))

    def wide(ref, b, h):
        return jnp.concatenate([ref[b, h, i] for i in range(4)], axis=1)

    def head_rows(h):
        return pl.ds(pl.multiple_of(h * HS, HS), HS)

    def prob_grad(b, h, side):
        parts = []
        for i in range(2):
            g = gbuf[b, 2 * side + i, head_rows(h), :]
            parts.append(jnp.concatenate([g, g, g, g], axis=0))
        return dot(v4t[b, h].reshape(4 * TOK, 4 * HS), jnp.concatenate(parts, axis=1))

    def score_grad(p, grad_prob):
        row_dot = jnp.sum(p * grad_prob, axis=0, keepdims=True)
        return (p * (grad_prob - row_dot)).astype(bf16)

    def head_back(b, h):
        pw = jnp.concatenate([pbuf[b, h, 0], pbuf[b, h, 1]], axis=1)
        dw = jnp.concatenate([dbuf[h, 0], dbuf[h, 1]], axis=1)
        g = jnp.concatenate([gbuf[b, i, head_rows(h), :] for i in range(4)], axis=1)
        grad_q = (fold3(dot(wide(k3, b, h), dw)) * SCALE).astype(bf16)
        grad_k = (fold3(dot_nt(wide(q3, b, h), dw)) * (1.0 / LOG2E)).astype(bf16)
        grad_v = dot_nt(g, pw).astype(bf16)
        for j in range(4):
            at = slice(j * TOK, (j + 1) * TOK)
            gpst[b, h, j] = jnp.concatenate([grad_q[:, at], grad_k[:, at], grad_v[:, at]], axis=0)
        for m in (2, 1, 0):
            gp_copy(b, m, h).start()
        gpbuf[b, own[b], h] = gpst[b, h, own[b]]

    def packed_back(b, stream, grad_next):
        own_side = own[b] // 2
        grad_normed = None
        for side, arrivals in ((own_side, (0,)), (1 - own_side, (1, 2))):
            for m in arrivals:
                gp_all(b, m).wait_recv()
            for third in range(3):
                pieces = []
                for i in range(2):
                    for h in range(OWN):
                        pieces.append(gpbuf[b, 2 * side + i, h, third * HS : (third + 1) * HS, :])
                at = pl.multiple_of(third * D + side * 2 * TOK, TOK)
                some = dot(wfull[b, :, pl.ds(at, 2 * TOK)], jnp.concatenate(pieces, axis=0))
                grad_normed = some if grad_normed is None else grad_normed + some
        inv = inverse[b]
        normed = stream * inv
        mean = jnp.sum(grad_normed * normed, axis=0, keepdims=True) * (1.0 / D)
        return grad_next + inv * (grad_normed - normed * mean)

    def send_grads(grad_next):
        grads = dot(wofull[0], grad_next.astype(bf16)).astype(bf16)
        gst[...] = grads.reshape(4, TOK, TOK)
        for m in (2, 1, 0):
            g_copy(m).start()
        gbuf[0, own[0]] = gst[own[0]]

    def second_grads(block):
        weight = mbuf[block].astype(f32) * jnp.broadcast_to(misfit_scale, (1, D))
        grad_next = (jnp.concatenate([c_out] * 4, axis=1) * weight).astype(bf16)
        rows = wofull[1, pl.ds(pl.multiple_of(own[1] * TOK, TOK), TOK), :]
        gbuf[1, block] = dot_nt(rows, grad_next).astype(bf16)

    def branch(b):
        return dot(wot[b], obuf[b].reshape(D, TOK))

    def forward(stage):
        if stage + 1 < len(stages):
            red_send(stage + 1, red_take(stage))

    gather_start(0)
    misfit_in.wait()
    misfit_copy(1).start()
    misfit_copy(0).start()
    misfit_f = mbuf[own[1]].astype(f32)
    squares = jnp.sum(misfit_f * misfit_f, axis=0, keepdims=True)
    squares = squares[:, :128] + squares[:, 128:256] + squares[:, 256:384] + squares[:, 384:]
    red_send(0, jnp.broadcast_to(squares, (8, 128)))
    for copy in out_in + col_in[1]:
        copy.start()
    prepare_weights(0)
    project(0, own[0])
    make_mask(0)
    misfit_t[...] = misfit_f.T
    near_copy(0).wait_recv()
    project(0, blocks[0][0])
    relay(0)
    project(0, blocks[0][1])
    for b in range(2):
        out_in[b].wait()
    wot[0] = wofull[0].T
    gather_last(0)
    forward(0)
    own_side = own[0] // 2
    order = [(side, h) for side in (1 - own_side, own_side) for h in range(OWN)]
    scores = [scores_of(0, order[0][1], order[0][0])]
    for at, (side, h) in enumerate(order):
        if at + 1 < len(order):
            scores.append(scores_of(0, order[at + 1][1], order[at + 1][0]))
        p = softmax(scores.pop(0))
        prob[h, side] = p
        p = p.astype(bf16)
        pbuf[0, h, side] = p
        o = fold3(dot(wide(v3, 0, h), p)).astype(bf16)
        for i in range(2):
            ost[0, 2 * side + i, h * HS : (h + 1) * HS, :] = o[:, i * TOK : (i + 1) * TOK]
        if at == 3:
            o_copy(0, 2).start()
            o_copy(0, 1).start()
    o_copy(0, 0).start()
    obuf[0, own[0]] = ost[0, own[0]]
    prepare_weights(1)
    misfit_copy(1).wait_recv()
    misfit_copy(2).start()
    o_all(0).wait_recv()
    stream1[...] = c_in * noisy_t[...] + branch(0)
    normalise(1, stream1[...])

    gather_start(1)
    full_in[1].start()
    full_in[0].start()
    forward(1)
    project(1, own[1])
    make_mask(1)
    near_copy(1).wait_recv()
    project(1, blocks[1][0])
    relay(1)
    project(1, blocks[1][1])
    square_sum = jnp.sum(red_take(len(stages) - 1)[:1], axis=1, keepdims=True)
    entries = float(n_shot * n_rec * TOK * D)
    misfit_scale = lax.rsqrt(square_sum / entries + norm_eps)
    second_grads(own[1])
    misfit_copy(0).wait_recv()
    second_grads(blocks[1][0])
    second_grads(blocks[1][1])
    misfit_copy(2).wait_recv()
    second_grads(blocks[1][2])
    wot[1] = wofull[1].T
    gather_last(1)

    def second(pair, carry):
        todo = [(2 * pair + u, side) for u in range(2) for side in range(2)]
        ahead = [(scores_of(1, *at), prob_grad(1, *at)) for at in todo[:2]]
        for step, (h, side) in enumerate(todo):
            scores, grad_prob = ahead.pop(0)
            p = softmax(scores)
            pbuf[1, h, side] = p.astype(bf16)
            dbuf[h, side] = score_grad(p, grad_prob)
            if step + 2 < len(todo):
                at = todo[step + 2]
                ahead.append((scores_of(1, *at), prob_grad(1, *at)))
            if side == 1:
                head_back(1, h)
        return carry

    lax.fori_loop(0, OWN // 2, second, 0)

    for h in range(OWN):
        for side in range(2):
            o = fold3(dot(wide(v3, 1, h), pbuf[1, h, side])).astype(bf16)
            for i in range(2):
                ost[1, 2 * side + i, h * HS : (h + 1) * HS, :] = o[:, i * TOK : (i + 1) * TOK]
    for m in (2, 1, 0):
        o_copy(1, m).start()
    obuf[1, own[1]] = ost[1, own[1]]
    for b in (1, 0):
        full_in[b].wait()
    weight = misfit_t[...] * misfit_scale
    grad1 = packed_back(1, stream1[...], c_out * weight)
    send_grads(grad1)
    grad_mid[...] = grad1

    def first(pair, carry, side):
        todo = [2 * pair + u for u in range(2)]
        grad_probs = [prob_grad(0, h, side) for h in todo]
        for h, grad_prob in zip(todo, grad_probs):
            dbuf[h, side] = score_grad(prob[h, side], grad_prob)
        return carry

    def first_last(pair, carry):
        first(pair, carry, 1 - own_side)
        for u in range(2):
            head_back(0, 2 * pair + u)
        return carry

    g_copy(0).wait_recv()
    lax.fori_loop(0, OWN // 2, functools.partial(first, side=own_side), 0)
    g_copy(1).wait_recv()
    g_copy(2).wait_recv()
    lax.fori_loop(0, OWN // 2, first_last, 0)

    o_all(1).wait_recv()
    final = stream1[...] + branch(1)
    out_v[0] = (c_skip * noisy_t[...] + c_out * final).T.astype(bf16)
    den_out = pltpu.make_async_copy(out_v.at[0], den, out_sem.at[0])
    den_out.start()
    for b in range(2):
        near_copy(b).wait_send()
        far_sent(b)
        relay_all(b).wait_send()
        o_all(b).wait_send()
    g_sent()
    misfit_sent()
    for stage in range(len(red_peers)):
        red_all(stage).wait_send()
    for m in range(3):
        gp_all(1, m).wait_send()
    grad0 = packed_back(0, c_in * noisy_t[...], grad_mid[...])
    weight = misfit_t[...] * misfit_scale
    out_v[1] = (c_skip * weight + c_in * grad0).T.astype(bf16)
    gui_out = pltpu.make_async_copy(out_v.at[1], gui, out_sem.at[1])
    gui_out.start()

    for m in range(3):
        gp_all(0, m).wait_send()
    den_out.wait()
    gui_out.wait()


def copy_pair(den, gui, den_out, gui_out, den_v, gui_v, sem):
    into = [
        pltpu.make_async_copy(den, den_v, sem.at[0]),
        pltpu.make_async_copy(gui, gui_v, sem.at[1]),
    ]
    away = [
        pltpu.make_async_copy(den_v, den_out, sem.at[2]),
        pltpu.make_async_copy(gui_v, gui_out, sem.at[3]),
    ]
    for copy in into:
        copy.start()
    for i in range(2):
        into[i].wait()
        away[i].start()
    for copy in away:
        copy.wait()


def local(n_shot, n_rec, noisy, misfit, timestep, segment_ids, w_qkv, w_out):
    stages = reduction_stages(n_shot, n_rec)
    shape = noisy.shape
    any_space = pl.BlockSpec(memory_space=pl.ANY)
    scalars = pl.BlockSpec(memory_space=pltpu.SMEM)
    dma = pltpu.SemaphoreType.DMA
    scratch = [
        pltpu.VMEM((TOK, D), bf16),
        pltpu.VMEM((D, TOK), f32),
        pltpu.VMEM((D, TOK), f32),
        pltpu.VMEM((D, TOK), f32),
        pltpu.VMEM((D, TOK), f32),
        pltpu.VMEM((2, 1, TOK), f32),
        pltpu.VMEM((2, D, 3 * D), bf16),
        pltpu.VMEM((2, D, D), bf16),
        pltpu.VMEM((2, 3, D, TOK), bf16),
        pltpu.VMEM((2, 3 * TOK, D), bf16),
        pltpu.VMEM((2, D, D), bf16),
        pltpu.VMEM((2, 4, D, TOK), bf16),
        pltpu.VMEM((4, TOK, D), bf16),
        pltpu.VMEM((2, OWN, 4, 3 * HS, TOK), bf16),
        pltpu.VMEM((2, OWN, 4, 3 * HS, TOK), bf16),
        pltpu.VMEM((2, OWN, 4, 3 * HS, TOK), bf16),
        pltpu.VMEM((2, OWN, 4, TOK, 8 * HS), bf16),
        pltpu.VMEM((2, OWN, 4, TOK, 4 * HS), bf16),
        pltpu.VMEM((2, 4, GROUPS, TOK), bf16),
        pltpu.VMEM((OWN, 2, 4 * TOK, 2 * TOK), f32),
        pltpu.VMEM((2, OWN, 2, 4 * TOK, 2 * TOK), bf16),
        pltpu.VMEM((OWN, 2, 4 * TOK, 2 * TOK), bf16),
        pltpu.VMEM((2, 4, TOK, TOK), bf16),
        pltpu.VMEM((2, 4, TOK, TOK), bf16),
        pltpu.VMEM((4, TOK, TOK), bf16),
        pltpu.VMEM((2, 4, TOK, TOK), bf16),
        pltpu.VMEM((2, OWN, 4, 3 * HS, TOK), bf16),
        pltpu.VMEM((2, 4, OWN, 3 * HS, TOK), bf16),
        pltpu.VMEM((len(stages), 8, 8, 128), f32),
        pltpu.VMEM((2, TOK, D), bf16),
        dma((2,)),
        dma((10,)),
        dma((2,)),
        dma((2,)),
        dma((2,)),
        dma((2,)),
        dma((2, CHUNKS)),
        dma((2,)),
        dma((2,)),
        dma((1,)),
        dma((3,)),
        dma((2,)),
        dma((2,)),
        dma((1,)),
        dma((3,)),
        dma((2, 3)),
        dma((2, 3)),
        dma((len(stages),)),
        dma((len(stages),)),
    ]
    den, gui = pl.pallas_call(
        functools.partial(kernel, n_shot, n_rec, stages),
        out_shape=[jax.ShapeDtypeStruct((TOK, D), bf16)] * 2,
        in_specs=[any_space, any_space, scalars, scalars, any_space, any_space],
        out_specs=[any_space, any_space],
        scratch_shapes=scratch,
        compiler_params=pltpu.CompilerParams(
            collective_id=0, has_side_effects=True, vmem_limit_bytes=VMEM_LIMIT
        ),
        cost_estimate=pl.CostEstimate(
            flops=2_000_000_000, bytes_accessed=6_000_000, transcendentals=2_000_000
        ),
        name="window_pair",
    )(noisy.reshape(TOK, D), misfit.reshape(TOK, D), timestep, segment_ids, w_qkv, w_out)
    den, gui = pl.pallas_call(
        copy_pair,
        out_shape=[jax.ShapeDtypeStruct((TOK, D), bf16)] * 2,
        in_specs=[any_space, any_space],
        out_specs=[any_space, any_space],
        scratch_shapes=[pltpu.VMEM((TOK, D), bf16), pltpu.VMEM((TOK, D), bf16), dma((4,))],
        compiler_params=pltpu.CompilerParams(vmem_limit_bytes=VMEM_LIMIT),
        name="copy_pair",
    )(den, gui)
    return den.reshape(shape), gui.reshape(shape)


def solution(mesh):
    tokens = P(None, "shot", "rec", None, None)
    return jax.shard_map(
        functools.partial(local, mesh.shape["shot"], mesh.shape["rec"]),
        mesh=mesh,
        in_specs=(tokens, tokens, P(), P(), P(), P()),
        out_specs=(tokens, tokens),
        check_vma=False,
    )
```

```python
import functools
import math

import jax
import jax.numpy as jnp
from jax import lax
from jax.experimental import pallas as pl
from jax.experimental.pallas import tpu as pltpu
from jax.sharding import PartitionSpec as P

HEADS = 16
HS = 32
STEPS = 1000
D = 512
TOK = 128
HALF = 4
OWN = 4
GROUPS = 64
CHUNKS = 4

sigma_low = 0.5
sigma_high = 8.0
sigma_data = 0.5
norm_eps = 1e-06
SCALE = HS ** (-0.5)
LOG2E = math.log2(math.e)
MASKED = -1e30
VMEM_LIMIT = 62 * 1024 * 1024

f32 = jnp.float32
bf16 = jnp.bfloat16
MESH = pl.DeviceIdType.MESH


def reduction_stages(n_shot, n_rec):
    stages = [
        [(1, 1, min(n_rec, 4)), (0, 1, 2)],
        [(0, 16, n_shot // 16), (1, 4, n_rec // 4)],
        [(0, 2, min(n_shot // 2, 8))],
    ]
    stages = [[digit for digit in stage if digit[2] > 1] for stage in stages]
    return [stage for stage in stages if stage]


def stage_peers(stage, shot, rec):
    place = [shot, rec]
    now, size = 0, 1
    for axis, stride, radix in stage:
        now = now + size * ((place[axis] // stride) % radix)
        size *= radix
    peers = []
    for k in range(1, size):
        later = (now + k) % size
        at = list(place)
        for axis, stride, radix in stage:
            digit = (place[axis] // stride) % radix
            at[axis] = at[axis] + stride * (later % radix - digit)
            later = later // radix
        peers.append((at[0], at[1]))
    return peers


def window_places(shot, rec, n_shot, n_rec):
    places = []
    near, far = shot % 2, rec % 2
    step_n, step_f = 1 - 2 * near, 1 - 2 * far
    places.append(
        (
            near,
            far,
            [(shot + step_n, rec), (shot, rec + step_f), (shot + step_n, rec + step_f)],
            [(shot - near + i % 2, 0) for i in range(4)],
        )
    )
    end = 1 - (rec % (n_rec - 1) + n_rec - 2) // (n_rec - 1)
    near = (shot + 1) % 2
    far = (1 - end) * ((rec + 1) % 2) + end * (((shot + 3) % 4) // 2)
    step_n, step_f = 1 - 2 * near, 1 - 2 * far
    move_s, move_r = 2 * end * step_f, (1 - end) * step_f
    near_shot = (shot + step_n + n_shot) % n_shot
    far_shot = (shot + move_s + n_shot) % n_shot
    diag_shot = (shot + step_n + move_s + n_shot) % n_shot
    first = shot - near - 2 * end * far + n_shot
    parts = []
    for i in range(4):
        at = (first + i % 2 + 2 * end * (i // 2)) % n_shot
        wrapped = 1 - (at + n_shot - 1) // n_shot
        parts.append((at, 2 * wrapped + end * (i // 2)))
    places.append(
        (near, far, [(near_shot, rec), (far_shot, rec + move_r), (diag_shot, rec + move_r)], parts)
    )
    return places


def split3(x):
    high = x.astype(bf16)
    rest = x - high.astype(f32)
    mid = rest.astype(bf16)
    low = (rest - mid.astype(f32)).astype(bf16)
    return high, mid, low


def dot(a, b):
    return lax.dot_general(a, b, (((1,), (0,)), ((), ())), preferred_element_type=f32)


def dot_nt(a, b):
    return lax.dot_general(a, b, (((1,), (1,)), ((), ())), preferred_element_type=f32)


def fold3(x):
    return x[:HS] + x[HS : 2 * HS] + x[2 * HS :]


def kernel(
    n_shot,
    n_rec,
    stages,
    noisy,
    misfit,
    timestep,
    segs,
    w_qkv,
    w_out,
    den,
    gui,
    noisy_v,
    noisy_t,
    misfit_t,
    stream1,
    grad_mid,
    inverse,
    wfull,
    wofull,
    wcol,
    wt,
    wot,
    nbuf,
    mbuf,
    q3,
    k3,
    v3,
    k8t,
    v4t,
    mrow,
    prob,
    pbuf,
    dbuf,
    ost,
    obuf,
    gst,
    gbuf,
    gpst,
    gpbuf,
    part,
    out_v,
    in_sem,
    w_sem,
    out_sem,
    near_s,
    near_r,
    far_s,
    far_r,
    rel_s,
    rel_r,
    mis_s,
    mis_r,
    o_s,
    o_r,
    g_s,
    g_r,
    gp_s,
    gp_r,
    red_s,
    red_r,
):
    shot, rec = lax.axis_index("shot"), lax.axis_index("rec")
    places = window_places(shot, rec, n_shot, n_rec)
    own, blocks, peers = [], [], []
    for near, far, partners, _ in places:
        here = 2 * far + near
        own.append(here)
        blocks.append([2 * far + 1 - near, 2 - 2 * far + near, 3 - 2 * far - near])
        peers.append(partners)
    red_peers = [stage_peers(stage, shot, rec) for stage in stages]

    barrier = pltpu.get_barrier_semaphore()
    greeted = peers[0] + peers[1] + [peer for some in red_peers for peer in some]
    for peer in greeted:
        pl.semaphore_signal(barrier, inc=1, device_id=peer, device_id_type=MESH)

    noisy_in = pltpu.make_async_copy(noisy, noisy_v, in_sem.at[0])
    misfit_in = pltpu.make_async_copy(misfit, mbuf.at[own[1]], in_sem.at[1])
    noisy_in.start()
    misfit_in.start()
    col_in = [
        [
            pltpu.make_async_copy(
                w_qkv.at[b, :, pl.ds(pl.multiple_of(third * D + own[b] * TOK, TOK), TOK)],
                wcol.at[b, third],
                w_sem.at[3 * b + third],
            )
            for third in range(3)
        ]
        for b in range(2)
    ]
    out_in = [pltpu.make_async_copy(w_out.at[b], wofull.at[b], w_sem.at[6 + b]) for b in range(2)]
    full_in = [pltpu.make_async_copy(w_qkv.at[b], wfull.at[b], w_sem.at[8 + b]) for b in range(2)]
    for copy in col_in[0]:
        copy.start()

    def remote(src, dst, send, recv, peer):
        return pltpu.make_async_remote_copy(
            src_ref=src, dst_ref=dst, send_sem=send, recv_sem=recv, device_id=peer, device_id_type=MESH
        )

    rows = D // CHUNKS

    def near_copy(b):
        block = nbuf.at[b, own[b]]
        return remote(block, block, near_s.at[b], near_r.at[b], peers[b][0])

    def far_copy(b, k):
        block = nbuf.at[b, own[b], pl.ds(k * rows, rows)]
        return remote(block, block, far_s.at[b], far_r.at[b, k], peers[b][1])

    def far_sent(b):
        block = nbuf.at[b, own[b]]
        remote(block, block, far_s.at[b], far_r.at[b, 0], peers[b][1]).wait_send()

    def relay_copy(b, k):
        block = nbuf.at[b, blocks[b][1], pl.ds(k * rows, rows)]
        return remote(block, block, rel_s.at[b], rel_r.at[b], peers[b][0])

    def relay_all(b):
        source, arrived = nbuf.at[b, blocks[b][1]], nbuf.at[b, blocks[b][2]]
        return remote(source, arrived, rel_s.at[b], rel_r.at[b], peers[b][0])

    def misfit_copy(m):
        block = mbuf.at[blocks[1][1] if m == 2 else own[1]]
        return remote(block, block, mis_s.at[0], mis_r.at[m], peers[1][m % 2])

    def misfit_sent():
        block = mbuf.at[pl.ds(0, 3)]
        remote(block, block, mis_s.at[0], mis_r.at[0], peers[1][0]).wait_send()

    def o_copy(b, m):
        return remote(
            ost.at[b, blocks[b][m]], obuf.at[b, own[b]], o_s.at[b], o_r.at[b], peers[b][m]
        )

    def o_all(b):
        source, arrived = ost.at[b, pl.ds(0, 3)], obuf.at[b, pl.ds(0, 3)]
        return remote(source, arrived, o_s.at[b], o_r.at[b], peers[b][0])

    def g_copy(m):
        return remote(
            gst.at[blocks[0][m]], gbuf.at[0, own[0]], g_s.at[0], g_r.at[m], peers[0][m]
        )

    def g_sent():
        source, arrived = gst.at[pl.ds(0, 3)], gbuf.at[0, pl.ds(0, 3)]
        remote(source, arrived, g_s.at[0], g_r.at[0], peers[0][0]).wait_send()

    def gp_copy(b, m, h):
        return remote(
            gpst.at[b, h, blocks[b][m]],
            gpbuf.at[b, own[b], h],
            gp_s.at[b, m],
            gp_r.at[b, m],
            peers[b][m],
        )

    def gp_all(b, m):
        source, arrived = gpst.at[b, :, blocks[b][m]], gpbuf.at[b, blocks[b][m]]
        return remote(source, arrived, gp_s.at[b, m], gp_r.at[b, m], peers[b][m])

    def red_copy(stage, k):
        return remote(
            part.at[stage, 0],
            part.at[stage, k + 1],
            red_s.at[stage],
            red_r.at[stage],
            red_peers[stage][k],
        )

    def red_all(stage):
        peers_of = red_peers[stage]
        block = part.at[stage, pl.ds(1, len(peers_of))]
        return remote(block, block, red_s.at[stage], red_r.at[stage], peers_of[0])

    def red_send(stage, value):
        part[stage, 0] = value
        for k in range(len(red_peers[stage])):
            red_copy(stage, k).start()

    def red_take(stage):
        red_all(stage).wait_recv()
        total = part[stage, 0]
        for k in range(len(red_peers[stage])):
            total = total + part[stage, k + 1]
        return total

    fraction = jnp.full((1, TOK), timestep[0].astype(f32), f32) / (STEPS - 1)
    noise_level = sigma_low * jnp.exp(fraction * math.log(sigma_high / sigma_low))
    spread = noise_level * noise_level + sigma_data * sigma_data
    c_skip = sigma_data * sigma_data / spread
    c_out = noise_level * sigma_data * lax.rsqrt(spread)
    c_in = lax.rsqrt(spread)

    def normalise(b, stream):
        inv = lax.rsqrt(jnp.sum(stream * stream, axis=0, keepdims=True) * (1.0 / D) + norm_eps)
        inverse[b] = inv
        nbuf[b, own[b]] = (stream * inv).astype(bf16)

    noisy_in.wait()
    noisy_t[...] = noisy_v[...].astype(f32).T
    normalise(0, c_in * noisy_t[...])
    pl.semaphore_wait(barrier, len(greeted))

    def gather_start(b):
        for k in range(CHUNKS):
            far_copy(b, k).start()
        near_copy(b).start()

    def prepare_weights(b):
        for third in range(3):
            col_in[b][third].wait()
            wt[b, third * TOK : (third + 1) * TOK, :] = wcol[b, third].T

    def project(b, block):
        packed = dot(wt[b], nbuf[b, block])
        q = split3(packed[:TOK] * (SCALE * LOG2E))
        k = split3(packed[TOK : 2 * TOK])
        v = split3(packed[2 * TOK :])
        zero = jnp.zeros((HS, TOK), bf16)
        lane = lax.broadcasted_iota(jnp.int32, (GROUPS, TOK), 1)
        row = lax.broadcasted_iota(jnp.int32, (GROUPS, TOK), 0)
        member = jnp.where(row == HALF * block + lane // HS, 1.0, 0.0).astype(bf16)
        for h in range(OWN):
            at = slice(h * HS, (h + 1) * HS)
            kh, km, kl = [x[at] for x in k]
            vh, vm, vl = [x[at] for x in v]
            q3[b, h, block] = jnp.concatenate([x[at] for x in q], axis=0)
            k3[b, h, block] = jnp.concatenate([kh, km, kl], axis=0)
            v3[b, h, block] = jnp.concatenate([vh, vm, vl], axis=0)
            k8t[b, h, block] = jnp.concatenate([kh, kh, kh, km, km, kl, member], axis=0).T
            v4t[b, h, block] = jnp.concatenate([vh, vm, vl, zero], axis=0).T

    def make_mask(b):
        ids = [[segs[HALF * at + s] * 4 + mark for s in range(HALF)] for at, mark in places[b][3]]
        lane = lax.broadcasted_iota(jnp.int32, (GROUPS, TOK), 1)
        row = lax.broadcasted_iota(jnp.int32, (GROUPS, TOK), 0)
        group_id = jnp.full((GROUPS, TOK), -1, jnp.int32)
        for g in range(4 * HALF):
            group_id = jnp.where(row == g, ids[g // HALF][g % HALF], group_id)
        for j in range(4):
            line = jnp.where(
                lane < 64,
                jnp.where(lane < 32, ids[j][0], ids[j][1]),
                jnp.where(lane < 96, ids[j][2], ids[j][3]),
            )
            apart = (line != group_id) & (row < 4 * HALF)
            mrow[b, j] = jnp.where(apart, MASKED, 0.0).astype(bf16)

    def relay(b):
        for k in range(CHUNKS):
            far_copy(b, k).wait_recv()
            relay_copy(b, k).start()

    def gather_last(b):
        relay_all(b).wait_recv()
        project(b, blocks[b][2])

    def scores_of(b, h, side):
        parts = []
        for i in range(2):
            q = q3[b, h, 2 * side + i]
            qh, qm, ql = q[:HS], q[HS : 2 * HS], q[2 * HS :]
            parts.append(
                jnp.concatenate([qh, qm, ql, qh, qm, qh, mrow[b, 2 * side + i]], axis=0)
            )
        return dot(k8t[b, h].reshape(4 * TOK, 8 * HS), jnp.concatenate(parts, axis=1))

    def softmax(scores):
        shifted = jnp.exp2(scores - jnp.max(scores, axis=0, keepdims=True))
        return shifted * (1.0 / jnp.sum(shifted, axis=0, keepdims=True))

    def wide(ref, b, h):
        return jnp.concatenate([ref[b, h, i] for i in range(4)], axis=1)

    def head_rows(h):
        return pl.ds(pl.multiple_of(h * HS, HS), HS)

    def prob_grad(b, h, side):
        parts = []
        for i in range(2):
            g = gbuf[b, 2 * side + i, head_rows(h), :]
            parts.append(jnp.concatenate([g, g, g, g], axis=0))
        return dot(v4t[b, h].reshape(4 * TOK, 4 * HS), jnp.concatenate(parts, axis=1))

    def score_grad(p, grad_prob):
        row_dot = jnp.sum(p * grad_prob, axis=0, keepdims=True)
        return (p * (grad_prob - row_dot)).astype(bf16)

    def head_back(b, h):
        pw = jnp.concatenate([pbuf[b, h, 0], pbuf[b, h, 1]], axis=1)
        dw = jnp.concatenate([dbuf[h, 0], dbuf[h, 1]], axis=1)
        g = jnp.concatenate([gbuf[b, i, head_rows(h), :] for i in range(4)], axis=1)
        grad_q = (fold3(dot(wide(k3, b, h), dw)) * SCALE).astype(bf16)
        grad_k = (fold3(dot_nt(wide(q3, b, h), dw)) * (1.0 / LOG2E)).astype(bf16)
        grad_v = dot_nt(g, pw).astype(bf16)
        for j in range(4):
            at = slice(j * TOK, (j + 1) * TOK)
            gpst[b, h, j] = jnp.concatenate([grad_q[:, at], grad_k[:, at], grad_v[:, at]], axis=0)
        for m in (2, 1, 0):
            gp_copy(b, m, h).start()
        gpbuf[b, own[b], h] = gpst[b, h, own[b]]

    def packed_back(b, stream, grad_next):
        own_side = own[b] // 2
        grad_normed = None
        for side, arrivals in ((own_side, (0,)), (1 - own_side, (1, 2))):
            for m in arrivals:
                gp_all(b, m).wait_recv()
            for third in range(3):
                pieces = []
                for i in range(2):
                    for h in range(OWN):
                        pieces.append(gpbuf[b, 2 * side + i, h, third * HS : (third + 1) * HS, :])
                at = pl.multiple_of(third * D + side * 2 * TOK, TOK)
                some = dot(wfull[b, :, pl.ds(at, 2 * TOK)], jnp.concatenate(pieces, axis=0))
                grad_normed = some if grad_normed is None else grad_normed + some
        inv = inverse[b]
        normed = stream * inv
        mean = jnp.sum(grad_normed * normed, axis=0, keepdims=True) * (1.0 / D)
        return grad_next + inv * (grad_normed - normed * mean)

    def send_grads(grad_next):
        grads = dot(wofull[0], grad_next.astype(bf16)).astype(bf16)
        gst[...] = grads.reshape(4, TOK, TOK)
        for m in (2, 1, 0):
            g_copy(m).start()
        gbuf[0, own[0]] = gst[own[0]]

    def second_grads(block):
        weight = mbuf[block].astype(f32) * jnp.broadcast_to(misfit_scale, (1, D))
        grad_next = (jnp.concatenate([c_out] * 4, axis=1) * weight).astype(bf16)
        rows = wofull[1, pl.ds(pl.multiple_of(own[1] * TOK, TOK), TOK), :]
        gbuf[1, block] = dot_nt(rows, grad_next).astype(bf16)

    def branch(b):
        return dot(wot[b], obuf[b].reshape(D, TOK))

    def forward(stage):
        if stage + 1 < len(stages):
            red_send(stage + 1, red_take(stage))

    gather_start(0)
    misfit_in.wait()
    misfit_copy(1).start()
    misfit_copy(0).start()
    misfit_f = mbuf[own[1]].astype(f32)
    squares = jnp.sum(misfit_f * misfit_f, axis=0, keepdims=True)
    squares = squares[:, :128] + squares[:, 128:256] + squares[:, 256:384] + squares[:, 384:]
    red_send(0, jnp.broadcast_to(squares, (8, 128)))
    for copy in out_in + col_in[1]:
        copy.start()
    prepare_weights(0)
    project(0, own[0])
    make_mask(0)
    misfit_t[...] = misfit_f.T
    near_copy(0).wait_recv()
    project(0, blocks[0][0])
    relay(0)
    project(0, blocks[0][1])
    for b in range(2):
        out_in[b].wait()
    wot[0] = wofull[0].T
    gather_last(0)
    forward(0)
    own_side = own[0] // 2
    order = [(side, h) for side in (1 - own_side, own_side) for h in range(OWN)]
    scores = [scores_of(0, order[0][1], order[0][0])]
    for at, (side, h) in enumerate(order):
        if at + 1 < len(order):
            scores.append(scores_of(0, order[at + 1][1], order[at + 1][0]))
        p = softmax(scores.pop(0))
        prob[h, side] = p
        p = p.astype(bf16)
        pbuf[0, h, side] = p
        o = fold3(dot(wide(v3, 0, h), p)).astype(bf16)
        for i in range(2):
            ost[0, 2 * side + i, h * HS : (h + 1) * HS, :] = o[:, i * TOK : (i + 1) * TOK]
        if at == 3:
            o_copy(0, 2).start()
            o_copy(0, 1).start()
    o_copy(0, 0).start()
    obuf[0, own[0]] = ost[0, own[0]]
    prepare_weights(1)
    o_all(0).wait_recv()
    stream1[...] = c_in * noisy_t[...] + branch(0)
    normalise(1, stream1[...])

    gather_start(1)
    full_in[1].start()
    full_in[0].start()
    forward(1)
    project(1, own[1])
    make_mask(1)
    misfit_copy(1).wait_recv()
    misfit_copy(2).start()
    near_copy(1).wait_recv()
    project(1, blocks[1][0])
    relay(1)
    project(1, blocks[1][1])
    square_sum = jnp.sum(red_take(len(stages) - 1)[:1], axis=1, keepdims=True)
    entries = float(n_shot * n_rec * TOK * D)
    misfit_scale = lax.rsqrt(square_sum / entries + norm_eps)
    second_grads(own[1])
    misfit_copy(0).wait_recv()
    second_grads(blocks[1][0])
    second_grads(blocks[1][1])
    misfit_copy(2).wait_recv()
    second_grads(blocks[1][2])
    gather_last(1)

    def second(pair, carry):
        todo = [(2 * pair + u, side) for u in range(2) for side in range(2)]
        ahead = [(scores_of(1, *at), prob_grad(1, *at)) for at in todo[:2]]
        for step, (h, side) in enumerate(todo):
            scores, grad_prob = ahead.pop(0)
            p = softmax(scores)
            pbuf[1, h, side] = p.astype(bf16)
            dbuf[h, side] = score_grad(p, grad_prob)
            if step + 2 < len(todo):
                at = todo[step + 2]
                ahead.append((scores_of(1, *at), prob_grad(1, *at)))
            if side == 1:
                head_back(1, h)
        return carry

    lax.fori_loop(0, OWN // 2, second, 0)

    wot[1] = wofull[1].T
    for h in range(OWN):
        for side in range(2):
            o = fold3(dot(wide(v3, 1, h), pbuf[1, h, side])).astype(bf16)
            for i in range(2):
                ost[1, 2 * side + i, h * HS : (h + 1) * HS, :] = o[:, i * TOK : (i + 1) * TOK]
    for m in (2, 1, 0):
        o_copy(1, m).start()
    obuf[1, own[1]] = ost[1, own[1]]
    for b in (1, 0):
        full_in[b].wait()
    weight = misfit_t[...] * misfit_scale
    grad1 = packed_back(1, stream1[...], c_out * weight)
    send_grads(grad1)
    grad_mid[...] = grad1

    def first(pair, carry, side):
        todo = [2 * pair + u for u in range(2)]
        grad_probs = [prob_grad(0, h, side) for h in todo]
        for h, grad_prob in zip(todo, grad_probs):
            dbuf[h, side] = score_grad(prob[h, side], grad_prob)
        return carry

    def first_last(pair, carry):
        first(pair, carry, 1 - own_side)
        for u in range(2):
            head_back(0, 2 * pair + u)
        return carry

    g_copy(0).wait_recv()
    lax.fori_loop(0, OWN // 2, functools.partial(first, side=own_side), 0)
    g_copy(1).wait_recv()
    g_copy(2).wait_recv()
    lax.fori_loop(0, OWN // 2, first_last, 0)

    o_all(1).wait_recv()
    final = stream1[...] + branch(1)
    out_v[0] = (c_skip * noisy_t[...] + c_out * final).T.astype(bf16)
    den_out = pltpu.make_async_copy(out_v.at[0], den, out_sem.at[0])
    den_out.start()
    for b in range(2):
        near_copy(b).wait_send()
        far_sent(b)
        relay_all(b).wait_send()
        o_all(b).wait_send()
    g_sent()
    misfit_sent()
    for stage in range(len(red_peers)):
        red_all(stage).wait_send()
    for m in range(3):
        gp_all(1, m).wait_send()
    grad0 = packed_back(0, c_in * noisy_t[...], grad_mid[...])
    weight = misfit_t[...] * misfit_scale
    out_v[1] = (c_skip * weight + c_in * grad0).T.astype(bf16)
    gui_out = pltpu.make_async_copy(out_v.at[1], gui, out_sem.at[1])
    gui_out.start()

    for m in range(3):
        gp_all(0, m).wait_send()
    den_out.wait()
    gui_out.wait()


def copy_pair(den, gui, den_out, gui_out, den_v, gui_v, sem):
    into = [
        pltpu.make_async_copy(den, den_v, sem.at[0]),
        pltpu.make_async_copy(gui, gui_v, sem.at[1]),
    ]
    away = [
        pltpu.make_async_copy(den_v, den_out, sem.at[2]),
        pltpu.make_async_copy(gui_v, gui_out, sem.at[3]),
    ]
    for copy in into:
        copy.start()
    for i in range(2):
        into[i].wait()
        away[i].start()
    for copy in away:
        copy.wait()


def local(n_shot, n_rec, noisy, misfit, timestep, segment_ids, w_qkv, w_out):
    stages = reduction_stages(n_shot, n_rec)
    shape = noisy.shape
    any_space = pl.BlockSpec(memory_space=pl.ANY)
    scalars = pl.BlockSpec(memory_space=pltpu.SMEM)
    dma = pltpu.SemaphoreType.DMA
    scratch = [
        pltpu.VMEM((TOK, D), bf16),
        pltpu.VMEM((D, TOK), f32),
        pltpu.VMEM((D, TOK), f32),
        pltpu.VMEM((D, TOK), f32),
        pltpu.VMEM((D, TOK), f32),
        pltpu.VMEM((2, 1, TOK), f32),
        pltpu.VMEM((2, D, 3 * D), bf16),
        pltpu.VMEM((2, D, D), bf16),
        pltpu.VMEM((2, 3, D, TOK), bf16),
        pltpu.VMEM((2, 3 * TOK, D), bf16),
        pltpu.VMEM((2, D, D), bf16),
        pltpu.VMEM((2, 4, D, TOK), bf16),
        pltpu.VMEM((4, TOK, D), bf16),
        pltpu.VMEM((2, OWN, 4, 3 * HS, TOK), bf16),
        pltpu.VMEM((2, OWN, 4, 3 * HS, TOK), bf16),
        pltpu.VMEM((2, OWN, 4, 3 * HS, TOK), bf16),
        pltpu.VMEM((2, OWN, 4, TOK, 8 * HS), bf16),
        pltpu.VMEM((2, OWN, 4, TOK, 4 * HS), bf16),
        pltpu.VMEM((2, 4, GROUPS, TOK), bf16),
        pltpu.VMEM((OWN, 2, 4 * TOK, 2 * TOK), f32),
        pltpu.VMEM((2, OWN, 2, 4 * TOK, 2 * TOK), bf16),
        pltpu.VMEM((OWN, 2, 4 * TOK, 2 * TOK), bf16),
        pltpu.VMEM((2, 4, TOK, TOK), bf16),
        pltpu.VMEM((2, 4, TOK, TOK), bf16),
        pltpu.VMEM((4, TOK, TOK), bf16),
        pltpu.VMEM((2, 4, TOK, TOK), bf16),
        pltpu.VMEM((2, OWN, 4, 3 * HS, TOK), bf16),
        pltpu.VMEM((2, 4, OWN, 3 * HS, TOK), bf16),
        pltpu.VMEM((len(stages), 8, 8, 128), f32),
        pltpu.VMEM((2, TOK, D), bf16),
        dma((2,)),
        dma((10,)),
        dma((2,)),
        dma((2,)),
        dma((2,)),
        dma((2,)),
        dma((2, CHUNKS)),
        dma((2,)),
        dma((2,)),
        dma((1,)),
        dma((3,)),
        dma((2,)),
        dma((2,)),
        dma((1,)),
        dma((3,)),
        dma((2, 3)),
        dma((2, 3)),
        dma((len(stages),)),
        dma((len(stages),)),
    ]
    den, gui = pl.pallas_call(
        functools.partial(kernel, n_shot, n_rec, stages),
        out_shape=[jax.ShapeDtypeStruct((TOK, D), bf16)] * 2,
        in_specs=[any_space, any_space, scalars, scalars, any_space, any_space],
        out_specs=[any_space, any_space],
        scratch_shapes=scratch,
        compiler_params=pltpu.CompilerParams(
            collective_id=0, has_side_effects=True, vmem_limit_bytes=VMEM_LIMIT
        ),
        cost_estimate=pl.CostEstimate(
            flops=2_000_000_000, bytes_accessed=6_000_000, transcendentals=2_000_000
        ),
        name="window_pair",
    )(noisy.reshape(TOK, D), misfit.reshape(TOK, D), timestep, segment_ids, w_qkv, w_out)
    den, gui = pl.pallas_call(
        copy_pair,
        out_shape=[jax.ShapeDtypeStruct((TOK, D), bf16)] * 2,
        in_specs=[any_space, any_space],
        out_specs=[any_space, any_space],
        scratch_shapes=[pltpu.VMEM((TOK, D), bf16), pltpu.VMEM((TOK, D), bf16), dma((4,))],
        compiler_params=pltpu.CompilerParams(vmem_limit_bytes=VMEM_LIMIT),
        name="copy_pair",
    )(den, gui)
    return den.reshape(shape), gui.reshape(shape)


def solution(mesh):
    tokens = P(None, "shot", "rec", None, None)
    return jax.shard_map(
        functools.partial(local, mesh.shape["shot"], mesh.shape["rec"]),
        mesh=mesh,
        in_specs=(tokens, tokens, P(), P(), P(), P()),
        out_specs=(tokens, tokens),
        check_vma=False,
    )
```

```python
import functools
import math

import jax
import jax.numpy as jnp
from jax import lax
from jax.experimental import pallas as pl
from jax.experimental.pallas import tpu as pltpu
from jax.sharding import PartitionSpec as P

HEADS = 16
HS = 32
STEPS = 1000
D = 512
TOK = 128
HALF = 4
OWN = 4
GROUPS = 64
CHUNKS = 4

sigma_low = 0.5
sigma_high = 8.0
sigma_data = 0.5
norm_eps = 1e-06
SCALE = HS ** (-0.5)
LOG2E = math.log2(math.e)
MASKED = -1e30
VMEM_LIMIT = 62 * 1024 * 1024

f32 = jnp.float32
bf16 = jnp.bfloat16
MESH = pl.DeviceIdType.MESH


def reduction_stages(n_shot, n_rec):
    stages = [
        [(1, 1, min(n_rec, 4)), (0, 1, 2)],
        [(0, 16, n_shot // 16), (1, 4, n_rec // 4)],
        [(0, 2, min(n_shot // 2, 8))],
    ]
    stages = [[digit for digit in stage if digit[2] > 1] for stage in stages]
    return [stage for stage in stages if stage]


def stage_peers(stage, shot, rec):
    place = [shot, rec]
    now, size = 0, 1
    for axis, stride, radix in stage:
        now = now + size * ((place[axis] // stride) % radix)
        size *= radix
    peers = []
    for k in range(1, size):
        later = (now + k) % size
        at = list(place)
        for axis, stride, radix in stage:
            digit = (place[axis] // stride) % radix
            at[axis] = at[axis] + stride * (later % radix - digit)
            later = later // radix
        peers.append((at[0], at[1]))
    return peers


def window_places(shot, rec, n_shot, n_rec):
    places = []
    near, far = shot % 2, rec % 2
    step_n, step_f = 1 - 2 * near, 1 - 2 * far
    places.append(
        (
            near,
            far,
            [(shot + step_n, rec), (shot, rec + step_f), (shot + step_n, rec + step_f)],
            [(shot - near + i % 2, 0) for i in range(4)],
        )
    )
    end = 1 - (rec % (n_rec - 1) + n_rec - 2) // (n_rec - 1)
    near = (shot + 1) % 2
    far = (1 - end) * ((rec + 1) % 2) + end * (((shot + 3) % 4) // 2)
    step_n, step_f = 1 - 2 * near, 1 - 2 * far
    move_s, move_r = 2 * end * step_f, (1 - end) * step_f
    near_shot = (shot + step_n + n_shot) % n_shot
    far_shot = (shot + move_s + n_shot) % n_shot
    diag_shot = (shot + step_n + move_s + n_shot) % n_shot
    first = shot - near - 2 * end * far + n_shot
    parts = []
    for i in range(4):
        at = (first + i % 2 + 2 * end * (i // 2)) % n_shot
        wrapped = 1 - (at + n_shot - 1) // n_shot
        parts.append((at, 2 * wrapped + end * (i // 2)))
    places.append(
        (near, far, [(near_shot, rec), (far_shot, rec + move_r), (diag_shot, rec + move_r)], parts)
    )
    return places


def split3(x):
    high = x.astype(bf16)
    rest = x - high.astype(f32)
    mid = rest.astype(bf16)
    low = (rest - mid.astype(f32)).astype(bf16)
    return high, mid, low


def dot(a, b):
    return lax.dot_general(a, b, (((1,), (0,)), ((), ())), preferred_element_type=f32)


def dot_nt(a, b):
    return lax.dot_general(a, b, (((1,), (1,)), ((), ())), preferred_element_type=f32)


def fold3(x):
    return x[:HS] + x[HS : 2 * HS] + x[2 * HS :]


def kernel(
    n_shot,
    n_rec,
    stages,
    noisy,
    misfit,
    timestep,
    segs,
    w_qkv,
    w_out,
    den,
    gui,
    noisy_v,
    noisy_t,
    misfit_t,
    stream1,
    grad_mid,
    inverse,
    wfull,
    wofull,
    wcol,
    wt,
    wot,
    nbuf,
    mbuf,
    q3,
    k3,
    v3,
    k8t,
    v4t,
    mrow,
    prob,
    pbuf,
    dbuf,
    ost,
    obuf,
    gst,
    gbuf,
    gpst,
    gpbuf,
    part,
    out_v,
    in_sem,
    w_sem,
    out_sem,
    near_s,
    near_r,
    far_s,
    far_r,
    rel_s,
    rel_r,
    mis_s,
    mis_r,
    o_s,
    o_r,
    g_s,
    g_r,
    gp_s,
    gp_r,
    red_s,
    red_r,
):
    shot, rec = lax.axis_index("shot"), lax.axis_index("rec")
    places = window_places(shot, rec, n_shot, n_rec)
    own, blocks, peers = [], [], []
    for near, far, partners, _ in places:
        here = 2 * far + near
        own.append(here)
        blocks.append([2 * far + 1 - near, 2 - 2 * far + near, 3 - 2 * far - near])
        peers.append(partners)
    red_peers = [stage_peers(stage, shot, rec) for stage in stages]

    barrier = pltpu.get_barrier_semaphore()
    greeted = peers[0] + peers[1] + [peer for some in red_peers for peer in some]
    for peer in greeted:
        pl.semaphore_signal(barrier, inc=1, device_id=peer, device_id_type=MESH)

    noisy_in = pltpu.make_async_copy(noisy, noisy_v, in_sem.at[0])
    misfit_in = pltpu.make_async_copy(misfit, mbuf.at[own[1]], in_sem.at[1])
    noisy_in.start()
    misfit_in.start()
    col_in = [
        [
            pltpu.make_async_copy(
                w_qkv.at[b, :, pl.ds(pl.multiple_of(third * D + own[b] * TOK, TOK), TOK)],
                wcol.at[b, third],
                w_sem.at[3 * b + third],
            )
            for third in range(3)
        ]
        for b in range(2)
    ]
    out_in = [pltpu.make_async_copy(w_out.at[b], wofull.at[b], w_sem.at[6 + b]) for b in range(2)]
    full_in = [pltpu.make_async_copy(w_qkv.at[b], wfull.at[b], w_sem.at[8 + b]) for b in range(2)]
    for copy in col_in[0]:
        copy.start()

    def remote(src, dst, send, recv, peer):
        return pltpu.make_async_remote_copy(
            src_ref=src, dst_ref=dst, send_sem=send, recv_sem=recv, device_id=peer, device_id_type=MESH
        )

    rows = D // CHUNKS

    def near_copy(b):
        block = nbuf.at[b, own[b]]
        return remote(block, block, near_s.at[b], near_r.at[b], peers[b][0])

    def far_copy(b, k):
        block = nbuf.at[b, own[b], pl.ds(k * rows, rows)]
        return remote(block, block, far_s.at[b], far_r.at[b, k], peers[b][1])

    def far_sent(b):
        block = nbuf.at[b, own[b]]
        remote(block, block, far_s.at[b], far_r.at[b, 0], peers[b][1]).wait_send()

    def relay_copy(b, k):
        block = nbuf.at[b, blocks[b][1], pl.ds(k * rows, rows)]
        return remote(block, block, rel_s.at[b], rel_r.at[b], peers[b][0])

    def relay_all(b):
        source, arrived = nbuf.at[b, blocks[b][1]], nbuf.at[b, blocks[b][2]]
        return remote(source, arrived, rel_s.at[b], rel_r.at[b], peers[b][0])

    def misfit_copy(m):
        block = mbuf.at[blocks[1][1] if m == 2 else own[1]]
        return remote(block, block, mis_s.at[0], mis_r.at[m], peers[1][m % 2])

    def misfit_sent():
        block = mbuf.at[pl.ds(0, 3)]
        remote(block, block, mis_s.at[0], mis_r.at[0], peers[1][0]).wait_send()

    def o_copy(b, m):
        return remote(
            ost.at[b, blocks[b][m]], obuf.at[b, own[b]], o_s.at[b], o_r.at[b], peers[b][m]
        )

    def o_all(b):
        source, arrived = ost.at[b, pl.ds(0, 3)], obuf.at[b, pl.ds(0, 3)]
        return remote(source, arrived, o_s.at[b], o_r.at[b], peers[b][0])

    def g_copy(m):
        return remote(
            gst.at[blocks[0][m]], gbuf.at[0, own[0]], g_s.at[0], g_r.at[m], peers[0][m]
        )

    def g_sent():
        source, arrived = gst.at[pl.ds(0, 3)], gbuf.at[0, pl.ds(0, 3)]
        remote(source, arrived, g_s.at[0], g_r.at[0], peers[0][0]).wait_send()

    def gp_copy(b, m, h):
        return remote(
            gpst.at[b, h, blocks[b][m]],
            gpbuf.at[b, own[b], h],
            gp_s.at[b, m],
            gp_r.at[b, m],
            peers[b][m],
        )

    def gp_all(b, m):
        source, arrived = gpst.at[b, :, blocks[b][m]], gpbuf.at[b, blocks[b][m]]
        return remote(source, arrived, gp_s.at[b, m], gp_r.at[b, m], peers[b][m])

    def red_copy(stage, k):
        return remote(
            part.at[stage, 0],
            part.at[stage, k + 1],
            red_s.at[stage],
            red_r.at[stage],
            red_peers[stage][k],
        )

    def red_all(stage):
        peers_of = red_peers[stage]
        block = part.at[stage, pl.ds(1, len(peers_of))]
        return remote(block, block, red_s.at[stage], red_r.at[stage], peers_of[0])

    def red_send(stage, value):
        part[stage, 0] = value
        for k in range(len(red_peers[stage])):
            red_copy(stage, k).start()

    def red_take(stage):
        red_all(stage).wait_recv()
        total = part[stage, 0]
        for k in range(len(red_peers[stage])):
            total = total + part[stage, k + 1]
        return total

    fraction = jnp.full((1, TOK), timestep[0].astype(f32), f32) / (STEPS - 1)
    noise_level = sigma_low * jnp.exp(fraction * math.log(sigma_high / sigma_low))
    spread = noise_level * noise_level + sigma_data * sigma_data
    c_skip = sigma_data * sigma_data / spread
    c_out = noise_level * sigma_data * lax.rsqrt(spread)
    c_in = lax.rsqrt(spread)

    def normalise(b, stream):
        inv = lax.rsqrt(jnp.sum(stream * stream, axis=0, keepdims=True) * (1.0 / D) + norm_eps)
        inverse[b] = inv
        nbuf[b, own[b]] = (stream * inv).astype(bf16)

    noisy_in.wait()
    noisy_t[...] = noisy_v[...].astype(f32).T
    normalise(0, c_in * noisy_t[...])
    pl.semaphore_wait(barrier, len(greeted))

    def gather_start(b):
        for k in range(CHUNKS):
            far_copy(b, k).start()
        near_copy(b).start()

    def prepare_weights(b):
        for third in range(3):
            col_in[b][third].wait()
            wt[b, third * TOK : (third + 1) * TOK, :] = wcol[b, third].T

    def project(b, block):
        packed = dot(wt[b], nbuf[b, block])
        q = split3(packed[:TOK] * (SCALE * LOG2E))
        k = split3(packed[TOK : 2 * TOK])
        v = split3(packed[2 * TOK :])
        zero = jnp.zeros((HS, TOK), bf16)
        lane = lax.broadcasted_iota(jnp.int32, (GROUPS, TOK), 1)
        row = lax.broadcasted_iota(jnp.int32, (GROUPS, TOK), 0)
        member = jnp.where(row == HALF * block + lane // HS, 1.0, 0.0).astype(bf16)
        for h in range(OWN):
            at = slice(h * HS, (h + 1) * HS)
            kh, km, kl = [x[at] for x in k]
            vh, vm, vl = [x[at] for x in v]
            q3[b, h, block] = jnp.concatenate([x[at] for x in q], axis=0)
            k3[b, h, block] = jnp.concatenate([kh, km, kl], axis=0)
            v3[b, h, block] = jnp.concatenate([vh, vm, vl], axis=0)
            k8t[b, h, block] = jnp.concatenate([kh, kh, kh, km, km, kl, member], axis=0).T
            v4t[b, h, block] = jnp.concatenate([vh, vm, vl, zero], axis=0).T

    def make_mask(b):
        ids = [[segs[HALF * at + s] * 4 + mark for s in range(HALF)] for at, mark in places[b][3]]
        lane = lax.broadcasted_iota(jnp.int32, (GROUPS, TOK), 1)
        row = lax.broadcasted_iota(jnp.int32, (GROUPS, TOK), 0)
        group_id = jnp.full((GROUPS, TOK), -1, jnp.int32)
        for g in range(4 * HALF):
            group_id = jnp.where(row == g, ids[g // HALF][g % HALF], group_id)
        for j in range(4):
            line = jnp.where(
                lane < 64,
                jnp.where(lane < 32, ids[j][0], ids[j][1]),
                jnp.where(lane < 96, ids[j][2], ids[j][3]),
            )
            apart = (line != group_id) & (row < 4 * HALF)
            mrow[b, j] = jnp.where(apart, MASKED, 0.0).astype(bf16)

    def relay(b):
        for k in range(CHUNKS):
            far_copy(b, k).wait_recv()
            relay_copy(b, k).start()

    def gather_last(b):
        relay_all(b).wait_recv()
        project(b, blocks[b][2])

    def scores_of(b, h, side):
        parts = []
        for i in range(2):
            q = q3[b, h, 2 * side + i]
            qh, qm, ql = q[:HS], q[HS : 2 * HS], q[2 * HS :]
            parts.append(
                jnp.concatenate([qh, qm, ql, qh, qm, qh, mrow[b, 2 * side + i]], axis=0)
            )
        return dot(k8t[b, h].reshape(4 * TOK, 8 * HS), jnp.concatenate(parts, axis=1))

    def softmax(scores):
        shifted = jnp.exp2(scores - jnp.max(scores, axis=0, keepdims=True))
        return shifted * (1.0 / jnp.sum(shifted, axis=0, keepdims=True))

    def wide(ref, b, h):
        return jnp.concatenate([ref[b, h, i] for i in range(4)], axis=1)

    def head_rows(h):
        return pl.ds(pl.multiple_of(h * HS, HS), HS)

    def prob_grad(b, h, side):
        parts = []
        for i in range(2):
            g = gbuf[b, 2 * side + i, head_rows(h), :]
            parts.append(jnp.concatenate([g, g, g, g], axis=0))
        return dot(v4t[b, h].reshape(4 * TOK, 4 * HS), jnp.concatenate(parts, axis=1))

    def score_grad(p, grad_prob):
        row_dot = jnp.sum(p * grad_prob, axis=0, keepdims=True)
        return (p * (grad_prob - row_dot)).astype(bf16)

    def head_back(b, h):
        pw = jnp.concatenate([pbuf[b, h, 0], pbuf[b, h, 1]], axis=1)
        dw = jnp.concatenate([dbuf[h, 0], dbuf[h, 1]], axis=1)
        g = jnp.concatenate([gbuf[b, i, head_rows(h), :] for i in range(4)], axis=1)
        grad_q = (fold3(dot(wide(k3, b, h), dw)) * SCALE).astype(bf16)
        grad_k = (fold3(dot_nt(wide(q3, b, h), dw)) * (1.0 / LOG2E)).astype(bf16)
        grad_v = dot_nt(g, pw).astype(bf16)
        for j in range(4):
            at = slice(j * TOK, (j + 1) * TOK)
            gpst[b, h, j] = jnp.concatenate([grad_q[:, at], grad_k[:, at], grad_v[:, at]], axis=0)
        for m in (2, 1, 0):
            gp_copy(b, m, h).start()
        gpbuf[b, own[b], h] = gpst[b, h, own[b]]

    def packed_back(b, stream, grad_next):
        own_side = own[b] // 2
        grad_normed = None
        for side, arrivals in ((own_side, (0,)), (1 - own_side, (1, 2))):
            for m in arrivals:
                gp_all(b, m).wait_recv()
            for third in range(3):
                pieces = []
                for i in range(2):
                    for h in range(OWN):
                        pieces.append(gpbuf[b, 2 * side + i, h, third * HS : (third + 1) * HS, :])
                at = pl.multiple_of(third * D + side * 2 * TOK, TOK)
                some = dot(wfull[b, :, pl.ds(at, 2 * TOK)], jnp.concatenate(pieces, axis=0))
                grad_normed = some if grad_normed is None else grad_normed + some
        inv = inverse[b]
        normed = stream * inv
        mean = jnp.sum(grad_normed * normed, axis=0, keepdims=True) * (1.0 / D)
        return grad_next + inv * (grad_normed - normed * mean)

    def send_grads(grad_next):
        grads = dot(wofull[0], grad_next.astype(bf16)).astype(bf16)
        gst[...] = grads.reshape(4, TOK, TOK)
        for m in (2, 1, 0):
            g_copy(m).start()
        gbuf[0, own[0]] = gst[own[0]]

    def second_grads(block):
        weight = mbuf[block].astype(f32) * jnp.broadcast_to(misfit_scale, (1, D))
        grad_next = (jnp.concatenate([c_out] * 4, axis=1) * weight).astype(bf16)
        rows = wofull[1, pl.ds(pl.multiple_of(own[1] * TOK, TOK), TOK), :]
        gbuf[1, block] = dot_nt(rows, grad_next).astype(bf16)

    def branch(b):
        return dot(wot[b], obuf[b].reshape(D, TOK))

    def forward(stage):
        if stage + 1 < len(stages):
            red_send(stage + 1, red_take(stage))

    gather_start(0)
    misfit_in.wait()
    misfit_copy(1).start()
    misfit_copy(0).start()
    misfit_f = mbuf[own[1]].astype(f32)
    squares = jnp.sum(misfit_f * misfit_f, axis=0, keepdims=True)
    squares = squares[:, :128] + squares[:, 128:256] + squares[:, 256:384] + squares[:, 384:]
    red_send(0, jnp.broadcast_to(squares, (8, 128)))
    for copy in out_in + col_in[1]:
        copy.start()
    prepare_weights(0)
    project(0, own[0])
    make_mask(0)
    misfit_t[...] = misfit_f.T
    near_copy(0).wait_recv()
    project(0, blocks[0][0])
    relay(0)
    project(0, blocks[0][1])
    for b in range(2):
        out_in[b].wait()
    wot[0] = wofull[0].T
    gather_last(0)
    forward(0)
    own_side = own[0] // 2
    order = [(side, h) for side in (1 - own_side, own_side) for h in range(OWN)]
    scores = [scores_of(0, order[0][1], order[0][0])]
    for at, (side, h) in enumerate(order):
        if at + 1 < len(order):
            scores.append(scores_of(0, order[at + 1][1], order[at + 1][0]))
        p = softmax(scores.pop(0))
        prob[h, side] = p
        p = p.astype(bf16)
        pbuf[0, h, side] = p
        o = fold3(dot(wide(v3, 0, h), p)).astype(bf16)
        for i in range(2):
            ost[0, 2 * side + i, h * HS : (h + 1) * HS, :] = o[:, i * TOK : (i + 1) * TOK]
        if at == 3:
            o_copy(0, 2).start()
            o_copy(0, 1).start()
    o_copy(0, 0).start()
    obuf[0, own[0]] = ost[0, own[0]]
    prepare_weights(1)
    misfit_copy(1).wait_recv()
    misfit_copy(2).start()
    o_all(0).wait_recv()
    stream1[...] = c_in * noisy_t[...] + branch(0)
    normalise(1, stream1[...])

    gather_start(1)
    full_in[1].start()
    full_in[0].start()
    forward(1)
    project(1, own[1])
    make_mask(1)
    near_copy(1).wait_recv()
    project(1, blocks[1][0])
    relay(1)
    project(1, blocks[1][1])
    square_sum = jnp.sum(red_take(len(stages) - 1)[:1], axis=1, keepdims=True)
    entries = float(n_shot * n_rec * TOK * D)
    misfit_scale = lax.rsqrt(square_sum / entries + norm_eps)
    second_grads(own[1])
    misfit_copy(0).wait_recv()
    second_grads(blocks[1][0])
    second_grads(blocks[1][1])
    misfit_copy(2).wait_recv()
    second_grads(blocks[1][2])
    wot[1] = wofull[1].T
    gather_last(1)

    def second(pair, carry):
        todo = [(2 * pair + u, side) for u in range(2) for side in range(2)]
        ahead = [(scores_of(1, *at), prob_grad(1, *at)) for at in todo[:2]]
        for step, (h, side) in enumerate(todo):
            scores, grad_prob = ahead.pop(0)
            p = softmax(scores)
            pbuf[1, h, side] = p.astype(bf16)
            dbuf[h, side] = score_grad(p, grad_prob)
            if step + 2 < len(todo):
                at = todo[step + 2]
                ahead.append((scores_of(1, *at), prob_grad(1, *at)))
            if side == 1:
                head_back(1, h)
        return carry

    lax.fori_loop(0, OWN // 2, second, 0)

    for h in range(OWN):
        for side in range(2):
            o = fold3(dot(wide(v3, 1, h), pbuf[1, h, side])).astype(bf16)
            for i in range(2):
                ost[1, 2 * side + i, h * HS : (h + 1) * HS, :] = o[:, i * TOK : (i + 1) * TOK]
    for m in (2, 1, 0):
        o_copy(1, m).start()
    obuf[1, own[1]] = ost[1, own[1]]
    for b in (1, 0):
        full_in[b].wait()
    for b in range(2):
        near_copy(b).wait_send()
        far_sent(b)
        relay_all(b).wait_send()
    o_all(0).wait_send()
    misfit_sent()
    for stage in range(len(red_peers)):
        red_all(stage).wait_send()
    weight = misfit_t[...] * misfit_scale
    grad1 = packed_back(1, stream1[...], c_out * weight)
    send_grads(grad1)
    grad_mid[...] = grad1

    def first(pair, carry, side):
        todo = [2 * pair + u for u in range(2)]
        grad_probs = [prob_grad(0, h, side) for h in todo]
        for h, grad_prob in zip(todo, grad_probs):
            dbuf[h, side] = score_grad(prob[h, side], grad_prob)
        return carry

    def first_last(pair, carry):
        first(pair, carry, 1 - own_side)
        for u in range(2):
            head_back(0, 2 * pair + u)
        return carry

    g_copy(0).wait_recv()
    lax.fori_loop(0, OWN // 2, functools.partial(first, side=own_side), 0)
    g_copy(1).wait_recv()
    g_copy(2).wait_recv()
    lax.fori_loop(0, OWN // 2, first_last, 0)

    o_all(1).wait_recv()
    final = stream1[...] + branch(1)
    out_v[0] = (c_skip * noisy_t[...] + c_out * final).T.astype(bf16)
    den_out = pltpu.make_async_copy(out_v.at[0], den, out_sem.at[0])
    den_out.start()
    o_all(1).wait_send()
    g_sent()
    for m in range(3):
        gp_all(1, m).wait_send()
    grad0 = packed_back(0, c_in * noisy_t[...], grad_mid[...])
    weight = misfit_t[...] * misfit_scale
    out_v[1] = (c_skip * weight + c_in * grad0).T.astype(bf16)
    gui_out = pltpu.make_async_copy(out_v.at[1], gui, out_sem.at[1])
    gui_out.start()

    for m in range(3):
        gp_all(0, m).wait_send()
    den_out.wait()
    gui_out.wait()


def copy_pair(den, gui, den_out, gui_out, den_v, gui_v, sem):
    into = [
        pltpu.make_async_copy(den, den_v, sem.at[0]),
        pltpu.make_async_copy(gui, gui_v, sem.at[1]),
    ]
    away = [
        pltpu.make_async_copy(den_v, den_out, sem.at[2]),
        pltpu.make_async_copy(gui_v, gui_out, sem.at[3]),
    ]
    for copy in into:
        copy.start()
    for i in range(2):
        into[i].wait()
        away[i].start()
    for copy in away:
        copy.wait()


def local(n_shot, n_rec, noisy, misfit, timestep, segment_ids, w_qkv, w_out):
    stages = reduction_stages(n_shot, n_rec)
    shape = noisy.shape
    any_space = pl.BlockSpec(memory_space=pl.ANY)
    scalars = pl.BlockSpec(memory_space=pltpu.SMEM)
    dma = pltpu.SemaphoreType.DMA
    scratch = [
        pltpu.VMEM((TOK, D), bf16),
        pltpu.VMEM((D, TOK), f32),
        pltpu.VMEM((D, TOK), f32),
        pltpu.VMEM((D, TOK), f32),
        pltpu.VMEM((D, TOK), f32),
        pltpu.VMEM((2, 1, TOK), f32),
        pltpu.VMEM((2, D, 3 * D), bf16),
        pltpu.VMEM((2, D, D), bf16),
        pltpu.VMEM((2, 3, D, TOK), bf16),
        pltpu.VMEM((2, 3 * TOK, D), bf16),
        pltpu.VMEM((2, D, D), bf16),
        pltpu.VMEM((2, 4, D, TOK), bf16),
        pltpu.VMEM((4, TOK, D), bf16),
        pltpu.VMEM((2, OWN, 4, 3 * HS, TOK), bf16),
        pltpu.VMEM((2, OWN, 4, 3 * HS, TOK), bf16),
        pltpu.VMEM((2, OWN, 4, 3 * HS, TOK), bf16),
        pltpu.VMEM((2, OWN, 4, TOK, 8 * HS), bf16),
        pltpu.VMEM((2, OWN, 4, TOK, 4 * HS), bf16),
        pltpu.VMEM((2, 4, GROUPS, TOK), bf16),
        pltpu.VMEM((OWN, 2, 4 * TOK, 2 * TOK), f32),
        pltpu.VMEM((2, OWN, 2, 4 * TOK, 2 * TOK), bf16),
        pltpu.VMEM((OWN, 2, 4 * TOK, 2 * TOK), bf16),
        pltpu.VMEM((2, 4, TOK, TOK), bf16),
        pltpu.VMEM((2, 4, TOK, TOK), bf16),
        pltpu.VMEM((4, TOK, TOK), bf16),
        pltpu.VMEM((2, 4, TOK, TOK), bf16),
        pltpu.VMEM((2, OWN, 4, 3 * HS, TOK), bf16),
        pltpu.VMEM((2, 4, OWN, 3 * HS, TOK), bf16),
        pltpu.VMEM((len(stages), 8, 8, 128), f32),
        pltpu.VMEM((2, TOK, D), bf16),
        dma((2,)),
        dma((10,)),
        dma((2,)),
        dma((2,)),
        dma((2,)),
        dma((2,)),
        dma((2, CHUNKS)),
        dma((2,)),
        dma((2,)),
        dma((1,)),
        dma((3,)),
        dma((2,)),
        dma((2,)),
        dma((1,)),
        dma((3,)),
        dma((2, 3)),
        dma((2, 3)),
        dma((len(stages),)),
        dma((len(stages),)),
    ]
    den, gui = pl.pallas_call(
        functools.partial(kernel, n_shot, n_rec, stages),
        out_shape=[jax.ShapeDtypeStruct((TOK, D), bf16)] * 2,
        in_specs=[any_space, any_space, scalars, scalars, any_space, any_space],
        out_specs=[any_space, any_space],
        scratch_shapes=scratch,
        compiler_params=pltpu.CompilerParams(
            collective_id=0, has_side_effects=True, vmem_limit_bytes=VMEM_LIMIT
        ),
        cost_estimate=pl.CostEstimate(
            flops=2_000_000_000, bytes_accessed=6_000_000, transcendentals=2_000_000
        ),
        name="window_pair",
    )(noisy.reshape(TOK, D), misfit.reshape(TOK, D), timestep, segment_ids, w_qkv, w_out)
    den, gui = pl.pallas_call(
        copy_pair,
        out_shape=[jax.ShapeDtypeStruct((TOK, D), bf16)] * 2,
        in_specs=[any_space, any_space],
        out_specs=[any_space, any_space],
        scratch_shapes=[pltpu.VMEM((TOK, D), bf16), pltpu.VMEM((TOK, D), bf16), dma((4,))],
        compiler_params=pltpu.CompilerParams(vmem_limit_bytes=VMEM_LIMIT),
        name="copy_pair",
    )(den, gui)
    return den.reshape(shape), gui.reshape(shape)


def solution(mesh):
    tokens = P(None, "shot", "rec", None, None)
    return jax.shard_map(
        functools.partial(local, mesh.shape["shot"], mesh.shape["rec"]),
        mesh=mesh,
        in_specs=(tokens, tokens, P(), P(), P(), P()),
        out_specs=(tokens, tokens),
        check_vma=False,
    )
```
